32 devices in a mesh: gx: 4 (over y, x), gy: 8 (over z, core).
Axes of the slice: x: 2, y: 2, z: 4, core: 2. Of those that a mesh axis runs over, the one named last changes fastest.
Arguments:
- right_side: float32 [28, 56, 168], P('gx', 'gy'), may hold values from -18 to 18
- stiff_coef: float32 [4, 8, 24], P('gx', 'gy'), may hold values from 0.3 to 3
- mass_coef: float32 [4, 8, 24], P('gx', 'gy'), may hold values from 2 to 200
- coarse_factor: float32 [256, 256], P(('gx', 'gy')), may hold values from -0.0390625 to 0.0390625
Outputs:
- solution: float32 [28, 56, 168], P('gx', 'gy')
- residual: float32 [28, 56, 168], P('gx', 'gy')
The draws below stay inside these ranges and needn't reach their ends.
All inputs are finite; a program needn't handle non-finite values.
Results may differ from the reference program's by a relative error of at most 0.0003.
Values sent between devices are 32-bit elements; how exact they have to be, the bound alone decides.
A program may use at most 64 MiB of HBM per device.

```python
import math
import jax
import jax.numpy as jnp
import numpy as np
from jax import lax

EZ = 24
C_DEV = 8
ITERS = 2
ELX = 4
ELY = 8
NX = 28
NY = 56
NZ = 168
NC = 256
N_GX = 4
N_GY = 8


def draw_right_side(key, part):
    first_pos = jnp.arange(NX, dtype=jnp.float32)[:, None, None] / NX
    second_pos = jnp.arange(NY, dtype=jnp.float32)[None, :, None] / NY
    rising = 1.0 + first_pos + second_pos
    jitter = jax.random.normal(key, (NX, NY, NZ), jnp.float32)
    return jnp.clip(jitter * rising, -18.0, 18.0)


def block_levels(stream_key, dims, split, low, high):
    def one(dim, shards_of):
        draws = jax.random.uniform(jax.random.fold_in(jax.random.fold_in(stream_key, 6), dim), (shards_of,), jnp.float32, low / len(split), high / len(split))
        return jnp.repeat(jnp.exp(draws), dims[dim] // shards_of).reshape((-1,) + (1,) * (len(dims) - dim - 1))

    level = one(*split[0])
    for cut in split[1:]:
        level = level * one(*cut)
    return level


def scatter_about(stream_key, shape, width, most, cuts=(), kind=jnp.bfloat16):
    values = jax.random.normal(stream_key, shape, jnp.float32) * width
    if len(cuts) > 0:
        values = block_levels(stream_key, shape, cuts, -0.22, 0.18) * values
    return jnp.clip(values, min=-most, max=most).astype(kind)


def setup_inputs(seed: int = 0) -> dict:
    streams_of = jax.random.split(jax.random.key(seed), 5)
    right_side = draw_right_side(jax.random.fold_in(streams_of[4], 71), 0)
    stiff_coef = jnp.clip(jnp.exp(math.log(3.0) - 2.3025851 * jax.random.uniform(streams_of[1], (ELX, ELY, EZ), jnp.float32) ** block_levels(streams_of[1], (ELX, ELY, EZ), ((0, 4), (1, 8)), -0.2, 0.2)), 0.3, 3.0)
    mass_coef = jnp.clip(jnp.exp(math.log(200.0) - 4.6051702 * jax.random.uniform(streams_of[2], (ELX, ELY, EZ), jnp.float32) ** block_levels(streams_of[2], (ELX, ELY, EZ), ((0, 4), (1, 8)), -0.2, 0.2)), 2.0, 200.0)
    coarse_factor = scatter_about(streams_of[3], (NC, NC), (NC * 96) ** -0.5, 0.0390625, ((0, 32),), jnp.float32)
    return dict(right_side=right_side, stiff_coef=stiff_coef, mass_coef=mass_coef, coarse_factor=coarse_factor)


exact_mode = lax.Precision.HIGHEST

def legendre_pair(position, degree):
    p_prev = 1.0
    p_now = position
    for order in range(2, degree + 1):
        p_next = ((2 * order - 1) * position * p_now - (order - 1) * p_prev) / order
        p_prev = p_now
        p_now = p_next
    return (p_now, p_prev)

def jacobi_eigen(matrix):
    size_n = matrix.shape[0]
    current = np.array(matrix)
    vectors = np.eye(size_n)
    for sweep in range(20):
        for row_p in range(size_n - 1):
            for row_q in range(row_p + 1, size_n):
                off_value = current[row_p, row_q]
                if abs(off_value) > 1e-300:
                    theta = (current[row_q, row_q] - current[row_p, row_p]) / (2.0 * off_value)
                    sign_t = 1.0 if theta >= 0.0 else -1.0
                    tangent = sign_t / (abs(theta) + math.sqrt(theta * theta + 1.0))
                    cosine = 1.0 / math.sqrt(tangent * tangent + 1.0)
                    sine = tangent * cosine
                    rotation = np.eye(size_n)
                    rotation[row_p, row_p] = cosine
                    rotation[row_q, row_q] = cosine
                    rotation[row_p, row_q] = sine
                    rotation[row_q, row_p] = -sine
                    current = rotation.T @ current @ rotation
                    vectors = vectors @ rotation
    return (np.array([current[idx, idx] for idx in range(size_n)]), vectors)

def gll_tables():
    degree = 7
    guesses = [-0.8717401485096066, -0.5917001814331423, -0.2092992179024789, 0.2092992179024789, 0.5917001814331423, 0.8717401485096066]
    interior = []
    for guess in guesses:
        position = guess
        for newton in range(30):
            p_now, p_prev = legendre_pair(position, degree)
            first = degree * (position * p_now - p_prev) / (position * position - 1.0)
            second = (2.0 * position * first - degree * (degree + 1) * p_now) / (1.0 - position * position)
            position = position - first / second
        interior.append(position)
    points = np.array([-1.0] + interior + [1.0])
    values = np.array([legendre_pair(float(pt), degree)[0] for pt in points])
    weights = 2.0 / (degree * (degree + 1) * values ** 2)
    deriv_mat = np.zeros((8, 8))
    for left_idx in range(8):
        for right_idx in range(8):
            if left_idx != right_idx:
                deriv_mat[left_idx, right_idx] = values[left_idx] / (values[right_idx] * (points[left_idx] - points[right_idx]))
    deriv_mat[0, 0] = -degree * (degree + 1) / 4.0
    deriv_mat[7, 7] = degree * (degree + 1) / 4.0
    stiffness = deriv_mat.T @ (weights[:, None] * deriv_mat)
    ext_stiff = np.zeros((10, 10))
    ext_stiff[1:9, 1:9] += stiffness
    ext_stiff[0:2, 0:2] += stiffness[6:8, 6:8]
    ext_stiff[8:10, 8:10] += stiffness[0:2, 0:2]
    ext_mass = np.zeros(10)
    ext_mass[1:9] += weights
    ext_mass[0:2] += weights[6:8]
    ext_mass[8:10] += weights[0:2]
    inv_root = 1.0 / np.sqrt(ext_mass)
    eigen_vals, eigen_vecs = jacobi_eigen(inv_root[:, None] * ext_stiff * inv_root[None, :])
    eigen_basis = inv_root[:, None] * eigen_vecs
    return (jnp.asarray(stiffness, jnp.float32), jnp.asarray(weights, jnp.float32), jnp.asarray(eigen_basis, jnp.float32), jnp.asarray(eigen_vals, jnp.float32))

def take_rows(widened, low, high, fold_axis):
    return lax.slice_in_dim(widened, low, high, axis=fold_axis)

def face_fold(widened, fold_axis):
    pieces = [take_rows(widened, 0, 1, fold_axis), take_rows(widened, 2, 3, fold_axis) + take_rows(widened, 1, 2, fold_axis), take_rows(widened, 3, 9, fold_axis), take_rows(widened, 9, 10, fold_axis) + take_rows(widened, 10, 11, fold_axis), take_rows(widened, 11, 12, fold_axis)]
    return jnp.concatenate(pieces, axis=fold_axis)

def spread_fold(widened, fold_axis):
    pieces = [take_rows(widened, 3, 5, fold_axis) + take_rows(widened, 0, 2, fold_axis), take_rows(widened, 5, 9, fold_axis), take_rows(widened, 9, 11, fold_axis) + take_rows(widened, 12, 14, fold_axis)]
    return jnp.concatenate(pieces, axis=fold_axis)

def z_windows(field_in, span):
    leading = field_in.shape[:2]
    elements = field_in.shape[2] // 7
    blocks = jnp.moveaxis(field_in.reshape(leading + (elements, 7)), 2, 3)
    if span == 8:
        return jnp.concatenate([blocks, jnp.roll(blocks[:, :, 0:1], -1, axis=3)], axis=2)
    behind = jnp.roll(blocks[:, :, 6:7], 1, axis=3)
    forward = jnp.roll(blocks[:, :, 0:2], -1, axis=3)
    return jnp.concatenate([behind, blocks, forward], axis=2)

def z_fold(blocks):
    if blocks.shape[2] == 8:
        owned = jnp.concatenate([blocks[:, :, 0:1] + jnp.roll(blocks[:, :, 7:8], 1, axis=3), blocks[:, :, 1:7]], axis=2)
    else:
        first_two = blocks[:, :, 1:3] + jnp.roll(blocks[:, :, 8:10], 1, axis=3)
        last_one = blocks[:, :, 7:8] + jnp.roll(blocks[:, :, 0:1], -1, axis=3)
        owned = jnp.concatenate([first_two, blocks[:, :, 3:7], last_one], axis=2)
    leading = owned.shape[:2]
    return jnp.moveaxis(owned, 2, 3).reshape(leading + (-1,))

def element_apply(blocks, stiff_line, mass_line, stiffness, weights):
    along_x = jnp.einsum('ai,ijte->ajte', stiffness, blocks, precision=exact_mode)
    along_y = jnp.einsum('aj,ijte->iate', stiffness, blocks, precision=exact_mode)
    along_z = jnp.einsum('at,ijte->ijae', stiffness, blocks, precision=exact_mode)
    weight_x = weights[:, None, None, None]
    weight_y = weights[None, :, None, None]
    weight_z = weights[None, None, :, None]
    laplace = along_x * weight_y * weight_z + along_y * weight_x * weight_z + along_z * weight_x * weight_y
    return stiff_line * laplace + mass_line * (weight_x * weight_y * weight_z) * blocks

def local_solve(blocks, stiff_line, mass_line, eigen_basis, eigen_vals):
    spectral = jnp.einsum('ia,ijte->ajte', eigen_basis, blocks, precision=exact_mode)
    spectral = jnp.einsum('jb,ajte->abte', eigen_basis, spectral, precision=exact_mode)
    spectral = jnp.einsum('tc,abte->abce', eigen_basis, spectral, precision=exact_mode)
    eigen_sum = eigen_vals[:, None, None] + eigen_vals[None, :, None] + eigen_vals[None, None, :]
    spectral = spectral / (stiff_line * eigen_sum[..., None] + mass_line)
    restored = jnp.einsum('ai,ijte->ajte', eigen_basis, spectral, precision=exact_mode)
    restored = jnp.einsum('bj,ajte->abte', eigen_basis, restored, precision=exact_mode)
    return jnp.einsum('ct,abte->abce', eigen_basis, restored, precision=exact_mode)

def ref_halo(blocks):
    from_left = jnp.roll(blocks, 1, axis=0)[:, :, -2:]
    from_right = jnp.roll(blocks, -1, axis=0)[:, :, :2]
    widened = jnp.concatenate([from_left, blocks, from_right], axis=2)
    from_below = jnp.roll(widened, 1, axis=1)[:, :, :, -2:]
    from_above = jnp.roll(widened, -1, axis=1)[:, :, :, :2]
    return jnp.concatenate([from_below, widened, from_above], axis=3)

def reference(right_side, stiff_coef, mass_coef, coarse_factor):
    stiffness, weights, eigen_basis, eigen_vals = gll_tables()
    z_points = right_side.shape[2]
    blocks = right_side.reshape(N_GX, 7, N_GY, 7, z_points).transpose(0, 2, 1, 3, 4)

    def per_column(worker, fields):

        def one_row(packed):
            return jax.vmap(worker)(packed[0], packed[1], packed[2])
        return lax.map(one_row, (fields, stiff_coef, mass_coef))

    def element_sum(field_in, stiff_line, mass_line):
        return z_fold(element_apply(z_windows(field_in, 8), stiff_line, mass_line, stiffness, weights))

    def schwarz_sum(field_in, stiff_line, mass_line):
        return z_fold(local_solve(z_windows(field_in, 10), stiff_line, mass_line, eigen_basis, eigen_vals))

    def operate(direction):
        return face_fold(face_fold(ref_halo(per_column(element_sum, direction)), 2), 3)

    def precondition(current):
        smooth = spread_fold(spread_fold(ref_halo(per_column(schwarz_sum, current)), 2), 3)
        coarse_in = lax.optimization_barrier(jnp.sum(current[:, :, 2:8, 2:8], axis=(2, 3))).reshape(N_GX * N_GY * C_DEV, -1).sum(axis=1)
        coarse_y = jnp.dot(coarse_in, coarse_factor, precision=exact_mode)
        coarse_out = jnp.dot(coarse_factor, coarse_y, precision=exact_mode).reshape(N_GX, N_GY, C_DEV, 1)
        coarse_line = jnp.broadcast_to(coarse_out, (N_GX, N_GY, C_DEV, z_points // C_DEV)).reshape(N_GX, N_GY, 1, 1, z_points)
        coarse_plate = jnp.pad(jnp.broadcast_to(coarse_line, (N_GX, N_GY, 6, 6, z_points)), ((0, 0), (0, 0), (1, 1), (1, 1), (0, 0)))
        return smooth + coarse_plate
    padded = jnp.pad(blocks, ((0, 0), (0, 0), (0, 1), (0, 1), (0, 0)))
    current = face_fold(face_fold(ref_halo(padded), 2), 3)
    solution = jnp.zeros(blocks.shape, jnp.float32)
    smooth = precondition(current)
    direction = smooth
    rho_now = jnp.sum(current[:, :, 1:8, 1:8] * smooth[:, :, :7, :7])
    for iteration in range(ITERS):
        applied = operate(direction)
        step_len = rho_now / jnp.sum(direction[:, :, :7, :7] * applied[:, :, 1:8, 1:8])
        solution = solution + step_len * direction[:, :, :7, :7]
        current = current - step_len * applied
        if iteration + 1 < ITERS:
            smooth = precondition(current)
            rho_next = jnp.sum(current[:, :, 1:8, 1:8] * smooth[:, :, :7, :7])
            direction = smooth + rho_next / rho_now * direction
            rho_now = rho_next
    solution_out = solution.transpose(0, 2, 1, 3, 4).reshape(NX, NY, NZ)
    residual_out = current[:, :, 1:8, 1:8].transpose(0, 2, 1, 3, 4).reshape(NX, NY, NZ)
    return (solution_out, residual_out)
```

```python
import functools
import math

import jax
import jax.numpy as jnp
import numpy as np
from jax import lax
from jax.experimental import pallas as pl
from jax.experimental.pallas import tpu as pltpu
from jax.sharding import PartitionSpec as P

MESH = pl.DeviceIdType.MESH
exact_mode = lax.Precision.HIGHEST
ROUNDS = 5

OWN = 64
SLOTS = (
    (-1, 0, 64, 16),
    (1, 0, 80, 16),
    (0, -1, 96, 16),
    (0, 1, 112, 16),
    (-1, -1, 128, 8),
    (-1, 1, 136, 8),
    (1, -1, 144, 8),
    (1, 1, 152, 8),
)
STACK = 160
SPEC = 112


def legendre_pair(position, degree):
    p_prev = 1.0
    p_now = position
    for order in range(2, degree + 1):
        p_next = ((2 * order - 1) * position * p_now - (order - 1) * p_prev) / order
        p_prev = p_now
        p_now = p_next
    return (p_now, p_prev)


def jacobi_eigen(matrix):
    size_n = matrix.shape[0]
    current = np.array(matrix)
    vectors = np.eye(size_n)
    for sweep in range(20):
        for row_p in range(size_n - 1):
            for row_q in range(row_p + 1, size_n):
                off_value = current[row_p, row_q]
                if abs(off_value) > 1e-300:
                    theta = (current[row_q, row_q] - current[row_p, row_p]) / (2.0 * off_value)
                    sign_t = 1.0 if theta >= 0.0 else -1.0
                    tangent = sign_t / (abs(theta) + math.sqrt(theta * theta + 1.0))
                    cosine = 1.0 / math.sqrt(tangent * tangent + 1.0)
                    sine = tangent * cosine
                    rotation = np.eye(size_n)
                    rotation[row_p, row_p] = cosine
                    rotation[row_q, row_q] = cosine
                    rotation[row_p, row_q] = sine
                    rotation[row_q, row_p] = -sine
                    current = rotation.T @ current @ rotation
                    vectors = vectors @ rotation
    return (np.array([current[idx, idx] for idx in range(size_n)]), vectors)


def gll_tables():
    degree = 7
    guesses = [
        -0.8717401485096066,
        -0.5917001814331423,
        -0.2092992179024789,
        0.2092992179024789,
        0.5917001814331423,
        0.8717401485096066,
    ]
    interior = []
    for guess in guesses:
        position = guess
        for newton in range(30):
            p_now, p_prev = legendre_pair(position, degree)
            first = degree * (position * p_now - p_prev) / (position * position - 1.0)
            second = (2.0 * position * first - degree * (degree + 1) * p_now) / (
                1.0 - position * position
            )
            position = position - first / second
        interior.append(position)
    points = np.array([-1.0] + interior + [1.0])
    values = np.array([legendre_pair(float(pt), degree)[0] for pt in points])
    weights = 2.0 / (degree * (degree + 1) * values**2)
    deriv_mat = np.zeros((8, 8))
    for left_idx in range(8):
        for right_idx in range(8):
            if left_idx != right_idx:
                deriv_mat[left_idx, right_idx] = values[left_idx] / (
                    values[right_idx] * (points[left_idx] - points[right_idx])
                )
    deriv_mat[0, 0] = -degree * (degree + 1) / 4.0
    deriv_mat[7, 7] = degree * (degree + 1) / 4.0
    stiffness = deriv_mat.T @ (weights[:, None] * deriv_mat)
    ext_stiff = np.zeros((10, 10))
    ext_stiff[1:9, 1:9] += stiffness
    ext_stiff[0:2, 0:2] += stiffness[6:8, 6:8]
    ext_stiff[8:10, 8:10] += stiffness[0:2, 0:2]
    ext_mass = np.zeros(10)
    ext_mass[1:9] += weights
    ext_mass[0:2] += weights[6:8]
    ext_mass[8:10] += weights[0:2]
    inv_root = 1.0 / np.sqrt(ext_mass)
    eigen_vals, eigen_vecs = jacobi_eigen(inv_root[:, None] * ext_stiff * inv_root[None, :])
    eigen_basis = inv_root[:, None] * eigen_vecs
    return stiffness, weights, eigen_basis, eigen_vals


def round_up(count, unit):
    return -(-count // unit) * unit


def stack_map(taken, placed, size_from, size_to):
    pick = np.zeros((STACK, size_from * size_from))
    place = np.zeros((size_to * size_to, STACK))
    for off_x, off_y, start, _ in ((0, 0, 0, OWN),) + SLOTS:
        row = start
        for from_x, to_x in zip(taken[off_x], placed[off_x]):
            for from_y, to_y in zip(taken[off_y], placed[off_y]):
                pick[row, from_x * size_from + from_y] = 1.0
                place[to_x * size_to + to_y, row] = 1.0
                row += 1
    return pick, place


def halves(matrix):
    exact = np.asarray(matrix, np.float32)
    high = exact.astype(jnp.bfloat16)
    low = (exact - high.astype(np.float32)).astype(jnp.bfloat16)
    return high, low


def left_split(matrix):
    high, low = halves(matrix)
    return np.concatenate([high, low, high], axis=1)


def left_exact(matrix):
    return np.concatenate([np.asarray(matrix).astype(jnp.bfloat16)] * 3, axis=1)


def constants(elements, coarse_count):
    stiffness, weights, basis, lam = gll_tables()
    stiffness = np.asarray(stiffness, np.float32).astype(np.float64)
    weights = np.asarray(weights, np.float32).astype(np.float64)
    basis = np.asarray(basis, np.float32).astype(np.float64)
    lam = np.asarray(lam, np.float32).astype(np.float64)
    points = 7 * elements
    z_pad = round_up(points, 128)
    s_pad = round_up(10 * elements, 128)
    every = list(range(8))
    pick_a, place_a = stack_map(
        {-1: [6, 7], 0: every, 1: [0, 1]}, {-1: [0, 1], 0: list(range(1, 9)), 1: [8, 9]}, 8, 10
    )
    pick_s, place_s = stack_map(
        {-1: [8, 9], 0: list(range(1, 9)), 1: [0, 1]}, {-1: [0, 1], 0: every, 1: [6, 7]}, 10, 8
    )
    basis_two = np.kron(basis, basis)
    spectral_in = np.zeros((SPEC, STACK))
    spectral_in[:100] = basis_two.T @ place_a
    spectral_out = np.zeros((STACK, SPEC))
    spectral_out[:, :100] = pick_s @ basis_two
    plane = np.kron(stiffness, np.diag(weights)) + np.kron(np.diag(weights), stiffness)
    plane_weight = np.kron(weights, weights)
    window = np.zeros((z_pad, s_pad))
    own_cols = np.zeros((z_pad, z_pad))
    before_cols = np.zeros((z_pad, z_pad))
    spread = np.zeros((elements, s_pad + 2 * z_pad))
    lines = np.zeros((8, max(z_pad, s_pad)))
    lines[2, 10 * elements :] = 1.0
    for elem in range(elements):
        prior = (elem - 1) % elements
        for col in range(10):
            spread[elem, col * elements + elem] = 1.0
            for row in range(10):
                window[(7 * elem - 1 + row) % points, col * elements + elem] += basis[row, col]
        for step in range(7):
            spread[elem, s_pad + 7 * elem + step] = 1.0
            spread[prior, s_pad + z_pad + 7 * elem + step] = 1.0
            lines[0, 7 * elem + step] = weights[step]
            for row in range(8):
                own_cols[(7 * elem + row) % points, 7 * elem + step] += stiffness[row, step]
        lines[1, 7 * elem] = weights[7]
        for row in range(8):
            before_cols[(7 * prior + row) % points, 7 * elem] += stiffness[row, 7]
    lam_all = np.zeros((SPEC, s_pad))
    lam_two = (lam[:, None] + lam[None, :]).reshape(-1)
    lam_all[:100, : 10 * elements] = lam_two[:, None] + np.repeat(lam, elements)[None, :]
    segments = np.zeros((coarse_count, z_pad))
    for row in range(coarse_count):
        length = points // coarse_count
        segments[row, row * length : (row + 1) * length] = 1.0
    window_high, window_low = halves(window)
    back_high, back_low = halves(window.T)
    inner = place_a.reshape(10, 10, STACK)[1:9, 1:9].reshape(OWN, STACK)
    single = lambda value: np.asarray(value, np.float32)
    return (
        left_exact(pick_a),
        left_split(spectral_in),
        left_split(spectral_out),
        left_exact(pick_a @ place_s),
        left_split(pick_a @ plane),
        left_exact(inner),
        window_high,
        window_low,
        back_high,
        back_low,
        single(own_cols),
        single(before_cols),
        single(lam_all),
        single(spread),
        single(lines),
        single(segments),
        single((pick_a @ plane_weight)[:, None]),
    )


def split_two(value):
    high = value.astype(jnp.bfloat16)
    return high, (value - high.astype(jnp.float32)).astype(jnp.bfloat16)


def mul(left, right):
    return jnp.dot(left, right, preferred_element_type=jnp.float32)


def left_mul(matrix_ref, value):
    high, low = split_two(value)
    return mul(matrix_ref[...], jnp.concatenate([high, high, low], axis=0))


def left_place(matrix_ref, value):
    high = value.astype(jnp.bfloat16)
    rest = value - high.astype(jnp.float32)
    middle, low = split_two(rest)
    return mul(matrix_ref[...], jnp.concatenate([high, middle, low], axis=0))


def right_mul(value, high_ref, low_ref):
    high, low = split_two(value)
    return mul(high, high_ref[...]) + (mul(high, low_ref[...]) + mul(low, high_ref[...]))


def each_other(count, act):
    if count <= 8:
        for step in range(1, count):
            act(step)
    else:

        def body(step, carry):
            act(step)
            return carry

        lax.fori_loop(1, count, body, 0)


def kernel(
    n_gx, n_gy, rhs, stiff, mass, factor,
    pick_a, spec_in, spec_out, pick_place, plane, inner, win_h, win_l, back_h, back_l,
    own_cols, before_cols, lam_all, spread, lines, segments, plane_weight,
    out_x, out_r,
    stack, sending, coarse_x, coarse_y, sums_x, sums_y, z_high, z_low, scale, first, field_w,
    halo_send, halo_recv, cx_send, cx_recv, cy_send, cy_recv, sx_send, sx_recv, sy_send, sy_recv,
):
    me_x, me_y = lax.axis_index("gx"), lax.axis_index("gy")
    points = rhs.shape[2]
    z_pad = win_h.shape[0]
    s_pad = win_h.shape[1]

    def beside(off_x, off_y):
        return (lax.rem(me_x + off_x + n_gx, n_gx), lax.rem(me_y + off_y + n_gy, n_gy))

    barrier = pltpu.get_barrier_semaphore()

    def greet(where):
        pl.semaphore_signal(barrier, inc=1, device_id=where, device_id_type=MESH)

    each_other(n_gx, lambda step: greet(beside(step, 0)))
    each_other(n_gy, lambda step: greet(beside(0, step)))
    for off_x, off_y, _, _ in SLOTS[4:]:
        greet(beside(off_x, off_y))

    def halo_copy(turn, slot):
        off_x, off_y, start, rows = SLOTS[slot]
        return pltpu.make_async_remote_copy(
            src_ref=sending.at[turn, pl.ds(start, rows)],
            dst_ref=stack.at[turn, pl.ds(start, rows)],
            send_sem=halo_send.at[turn, slot],
            recv_sem=halo_recv.at[turn, slot],
            device_id=beside(-off_x, -off_y),
            device_id_type=MESH,
        )

    def halo_start(turn, rows):
        sending[turn] = rows
        for slot in range(8):
            halo_copy(turn, slot).start()
        stack[turn, pl.ds(0, OWN)] = rows[:OWN]

    def halo_wait(turn):
        for slot in range(8):
            halo_copy(turn, slot).wait_recv()
        return stack[turn]

    def line_copy(buf, send, recv, axis, step, sender):
        return pltpu.make_async_remote_copy(
            src_ref=buf.at[sender],
            dst_ref=buf.at[sender],
            send_sem=send.at[step],
            recv_sem=recv.at[step],
            device_id=beside(step, 0) if axis == 0 else beside(0, step),
            device_id_type=MESH,
        )

    def line_start(buf, send, recv, axis, value):
        me, count = ((me_x, n_gx), (me_y, n_gy))[axis]
        buf[me] = value
        each_other(count, lambda step: line_copy(buf, send, recv, axis, step, me).start())

    def line_total(buf, send, recv, axis):
        me, count = ((me_x, n_gx), (me_y, n_gy))[axis]

        def take(step):
            sender = lax.rem(me - step + count, count)
            line_copy(buf, send, recv, axis, step, sender).wait_recv()

        each_other(count, take)
        return jnp.sum(buf[...], axis=0)

    def line_drain(buf, send, recv, axis):
        me, count = ((me_x, n_gx), (me_y, n_gy))[axis]
        each_other(count, lambda step: line_copy(buf, send, recv, axis, step, me).wait_send())

    cx = [(coarse_x.at[turn], cx_send.at[turn], cx_recv.at[turn], 0) for turn in range(2)]
    cy = [(coarse_y.at[turn], cy_send.at[turn], cy_recv.at[turn], 1) for turn in range(2)]
    sx = (sums_x, sx_send, sx_recv, 0)
    sy = (sums_y, sy_send, sy_recv, 1)

    point = lax.broadcasted_iota(jnp.int32, (OWN, z_pad), 0)
    at_x, at_y = point // 8, point % 8
    coarse_mask = (at_x >= 1) & (at_x <= 6) & (at_y >= 1) & (at_y <= 6)

    def coarse_start(turn, rows):
        line = jnp.sum(jnp.where(coarse_mask, rows, 0.0), axis=0, keepdims=True)
        sums = jnp.sum(segments[...] * line, axis=1, keepdims=True)
        line_start(*cx[turn], jnp.sum(factor[...] * sums, axis=0, keepdims=True))

    def coarse_middle(turn):
        line_start(*cy[turn], line_total(*cx[turn]))

    def coarse_finish(turn):
        total = line_total(*cy[turn])
        values = jnp.sum(factor[...] * total, axis=1, keepdims=True)
        line = jnp.sum(segments[...] * values, axis=0, keepdims=True)
        return jnp.where(coarse_mask, line, 0.0)

    first[...] = jnp.zeros_like(first)
    for row in range(7):
        first[pl.ds(8 * row, 7), pl.ds(0, points)] = rhs[row]
    right = first[...]
    rows = left_place(pick_a, right)
    pl.semaphore_wait(barrier, n_gx - 1 + n_gy - 1 + 4)
    halo_start(0, rows)
    coarse_start(0, right)

    def spread_out(coef):
        flat = jnp.dot(
            jnp.broadcast_to(coef[0], (8, coef.shape[2])), spread[...],
            precision=exact_mode, preferred_element_type=jnp.float32,
        )[0:1]
        return flat[:, :s_pad], flat[:, s_pad : s_pad + z_pad], flat[:, s_pad + z_pad :]

    stiff_s, stiff_own, stiff_before = spread_out(stiff)
    mass_s, mass_own, mass_before = spread_out(mass)
    weight_own, weight_before = lines[0:1, :z_pad], lines[1:2, :z_pad]
    line_stiff = stiff_own * weight_own + stiff_before * weight_before
    line_mass = mass_own * weight_own + mass_before * weight_before
    scale[...] = 1.0 / (stiff_s * lam_all[...] + (mass_s + lines[2:3, :s_pad]))
    diagonal = lax.broadcasted_iota(jnp.int32, (z_pad, z_pad), 0) == lax.broadcasted_iota(
        jnp.int32, (z_pad, z_pad), 1
    )
    along = own_cols[...] * stiff_own + before_cols[...] * stiff_before
    z_high[...], z_low[...] = split_two(along + jnp.where(diagonal, line_mass, 0.0))

    def schwarz(rows):
        spectral = right_mul(left_mul(spec_in, rows), win_h, win_l) * scale[...]
        return left_mul(spec_out, right_mul(spectral, back_h, back_l))

    def element(rows):
        wide = left_place(pick_place, rows)
        field = wide[:OWN]
        result = left_mul(plane, field * line_stiff) + plane_weight[...] * right_mul(
            wide, z_high, z_low
        )
        return field, result

    def precondition(turn, rows):
        coarse_middle(turn)
        result = schwarz(halo_wait(2 * turn))
        halo_start(2 * turn + 1, result)
        plate = coarse_finish(turn)
        stack[2 * turn + 1, pl.ds(0, OWN)] = result[:OWN] + plate

    def dot_line(left, other):
        return jnp.sum(left * other, axis=0, keepdims=True)

    owned = (at_x < 7) & (at_y < 7)

    precondition(0, rows)
    z_field, w_rows = element(halo_wait(1))
    halo_start(2, w_rows)
    w_local = w_rows[:OWN]
    coarse_start(1, w_local)
    precondition(1, w_rows)
    field_w[...] = left_place(inner, stack[2])
    v_field, av_rows = element(halo_wait(3))
    halo_start(4, av_rows)
    av_local = av_rows[:OWN]
    partial = jnp.concatenate(
        [
            dot_line(right, jnp.where(owned, z_field, 0.0)),
            dot_line(z_field, w_local),
            dot_line(right, jnp.where(owned, v_field, 0.0)),
            dot_line(v_field, w_local),
            dot_line(v_field, av_local),
            dot_line(z_field, av_local),
            jnp.zeros((2, z_pad), jnp.float32),
        ],
        axis=0,
    )
    line_start(*sx, partial)
    line_start(*sy, line_total(*sx))
    av_field = left_place(inner, halo_wait(4))
    w_field = field_w[...]
    totals = jnp.sum(line_total(*sy), axis=1, keepdims=True)
    rz, zw, rv, vw, vav, zav = [totals[row : row + 1] for row in range(6)]
    step_0 = rz / zw
    rho_1 = rz - step_0 * (rv + zw) + step_0 * step_0 * vw
    momentum = rho_1 / rz
    curve = (
        zw - step_0 * (vw + zav) + step_0 * step_0 * vav
        + momentum * ((zw - step_0 * vw) + (zw - step_0 * zav))
        + momentum * momentum * zw
    )
    step_1 = rho_1 / curve
    next_dir = (z_field - step_0 * v_field) + momentum * z_field
    next_image = (w_field - step_0 * av_field) + momentum * w_field
    final_x = step_0 * z_field + step_1 * next_dir
    final_r = (right - step_0 * w_field) - step_1 * next_image
    for row in range(7):
        out_x[row] = final_x[8 * row : 8 * row + 7, :points]
        out_r[row] = final_r[8 * row : 8 * row + 7, :points]

    for turn in range(ROUNDS):
        for slot in range(8):
            halo_copy(turn, slot).wait_send()
    for group in (*cx, *cy, sx, sy):
        line_drain(*group)


def local(n_gx, n_gy, right_side, stiff_coef, mass_coef, coarse_factor):
    elements = stiff_coef.shape[2]
    coarse_count, coarse_all = coarse_factor.shape
    tables = constants(elements, coarse_count)
    z_pad = round_up(7 * elements, 128)
    s_pad = round_up(10 * elements, 128)
    dma = pltpu.SemaphoreType.DMA
    single = jnp.float32
    whole = pl.BlockSpec(memory_space=pltpu.VMEM)
    shape = jax.ShapeDtypeStruct(right_side.shape, single)
    return pl.pallas_call(
        functools.partial(kernel, n_gx, n_gy),
        out_shape=(shape, shape),
        in_specs=[whole] * (4 + len(tables)),
        out_specs=(whole, whole),
        scratch_shapes=[
            pltpu.VMEM((ROUNDS, STACK, z_pad), single),
            pltpu.VMEM((ROUNDS, STACK, z_pad), single),
            pltpu.VMEM((2, n_gx, 1, coarse_all), single),
            pltpu.VMEM((2, n_gy, 1, coarse_all), single),
            pltpu.VMEM((n_gx, 8, z_pad), single),
            pltpu.VMEM((n_gy, 8, z_pad), single),
            pltpu.VMEM((z_pad, z_pad), jnp.bfloat16),
            pltpu.VMEM((z_pad, z_pad), jnp.bfloat16),
            pltpu.VMEM((SPEC, s_pad), single),
            pltpu.VMEM((OWN, z_pad), single),
            pltpu.VMEM((OWN, z_pad), single),
            dma((ROUNDS, 8)),
            dma((ROUNDS, 8)),
            dma((2, n_gx)),
            dma((2, n_gx)),
            dma((2, n_gy)),
            dma((2, n_gy)),
            dma((n_gx,)),
            dma((n_gx,)),
            dma((n_gy,)),
            dma((n_gy,)),
        ],
        compiler_params=pltpu.CompilerParams(
            collective_id=0, has_side_effects=True, vmem_limit_bytes=40 * 1024 * 1024
        ),
    )(right_side, stiff_coef, mass_coef, coarse_factor, *[jnp.asarray(table) for table in tables])


def solution(mesh):
    placed = (P("gx", "gy", None), P("gx", "gy", None), P("gx", "gy", None), P(("gx", "gy"), None))
    return jax.shard_map(
        functools.partial(local, mesh.shape["gx"], mesh.shape["gy"]),
        mesh=mesh,
        in_specs=placed,
        out_specs=(P("gx", "gy", None), P("gx", "gy", None)),
        check_vma=False,
    )
```

```python
import functools
import math

import jax
import jax.numpy as jnp
import numpy as np
from jax import lax
from jax.experimental import pallas as pl
from jax.experimental.pallas import tpu as pltpu
from jax.sharding import PartitionSpec as P

MESH = pl.DeviceIdType.MESH
exact_mode = lax.Precision.HIGHEST
ROUNDS = 5

OWN = 64
SLOTS = (
    (-1, 0, 64, 16),
    (1, 0, 80, 16),
    (0, -1, 96, 16),
    (0, 1, 112, 16),
    (-1, -1, 128, 8),
    (-1, 1, 136, 8),
    (1, -1, 144, 8),
    (1, 1, 152, 8),
)
STACK = 160
SPEC = 112
LAST = ((72, 0), (104, 2), (128, 4))
OPERANDS = (
    "rhs", "pick_a", "segments", "factor", "stiff", "mass", "spread", "lines", "lam_all", "own_cols", "before_cols",
    "spec_in", "win_h", "win_l", "back_h", "back_l", "spec_out", "pick_place", "plane", "plane_weight", "inner",
)
DIRECT = 64


def legendre_pair(position, degree):
    p_prev = 1.0
    p_now = position
    for order in range(2, degree + 1):
        p_next = ((2 * order - 1) * position * p_now - (order - 1) * p_prev) / order
        p_prev = p_now
        p_now = p_next
    return (p_now, p_prev)


def jacobi_eigen(matrix):
    size_n = matrix.shape[0]
    current = np.array(matrix)
    vectors = np.eye(size_n)
    for sweep in range(20):
        for row_p in range(size_n - 1):
            for row_q in range(row_p + 1, size_n):
                off_value = current[row_p, row_q]
                if abs(off_value) > 1e-300:
                    theta = (current[row_q, row_q] - current[row_p, row_p]) / (2.0 * off_value)
                    sign_t = 1.0 if theta >= 0.0 else -1.0
                    tangent = sign_t / (abs(theta) + math.sqrt(theta * theta + 1.0))
                    cosine = 1.0 / math.sqrt(tangent * tangent + 1.0)
                    sine = tangent * cosine
                    rotation = np.eye(size_n)
                    rotation[row_p, row_p] = cosine
                    rotation[row_q, row_q] = cosine
                    rotation[row_p, row_q] = sine
                    rotation[row_q, row_p] = -sine
                    current = rotation.T @ current @ rotation
                    vectors = vectors @ rotation
    return (np.array([current[idx, idx] for idx in range(size_n)]), vectors)


def gll_tables():
    degree = 7
    guesses = [
        -0.8717401485096066,
        -0.5917001814331423,
        -0.2092992179024789,
        0.2092992179024789,
        0.5917001814331423,
        0.8717401485096066,
    ]
    interior = []
    for guess in guesses:
        position = guess
        for newton in range(30):
            p_now, p_prev = legendre_pair(position, degree)
            first = degree * (position * p_now - p_prev) / (position * position - 1.0)
            second = (2.0 * position * first - degree * (degree + 1) * p_now) / (
                1.0 - position * position
            )
            position = position - first / second
        interior.append(position)
    points = np.array([-1.0] + interior + [1.0])
    values = np.array([legendre_pair(float(pt), degree)[0] for pt in points])
    weights = 2.0 / (degree * (degree + 1) * values**2)
    deriv_mat = np.zeros((8, 8))
    for left_idx in range(8):
        for right_idx in range(8):
            if left_idx != right_idx:
                deriv_mat[left_idx, right_idx] = values[left_idx] / (
                    values[right_idx] * (points[left_idx] - points[right_idx])
                )
    deriv_mat[0, 0] = -degree * (degree + 1) / 4.0
    deriv_mat[7, 7] = degree * (degree + 1) / 4.0
    stiffness = deriv_mat.T @ (weights[:, None] * deriv_mat)
    ext_stiff = np.zeros((10, 10))
    ext_stiff[1:9, 1:9] += stiffness
    ext_stiff[0:2, 0:2] += stiffness[6:8, 6:8]
    ext_stiff[8:10, 8:10] += stiffness[0:2, 0:2]
    ext_mass = np.zeros(10)
    ext_mass[1:9] += weights
    ext_mass[0:2] += weights[6:8]
    ext_mass[8:10] += weights[0:2]
    inv_root = 1.0 / np.sqrt(ext_mass)
    eigen_vals, eigen_vecs = jacobi_eigen(inv_root[:, None] * ext_stiff * inv_root[None, :])
    eigen_basis = inv_root[:, None] * eigen_vecs
    return stiffness, weights, eigen_basis, eigen_vals


def round_up(count, unit):
    return -(-count // unit) * unit


def stack_map(taken, placed, size_from, size_to):
    pick = np.zeros((STACK, size_from * size_from))
    place = np.zeros((size_to * size_to, STACK))
    for off_x, off_y, start, _ in ((0, 0, 0, OWN),) + SLOTS:
        row = start
        pairs_x = list(zip(taken[off_x], placed[off_x]))
        pairs_y = list(zip(taken[off_y], placed[off_y]))
        pairs = [(one, two) for one in pairs_x for two in pairs_y]
        if off_x == 0 and off_y != 0:
            pairs = [(one, two) for two in pairs_y for one in pairs_x]
        for (from_x, to_x), (from_y, to_y) in pairs:
            pick[row, from_x * size_from + from_y] = 1.0
            place[to_x * size_to + to_y, row] = 1.0
            row += 1
    return pick, place


def halves(matrix):
    exact = np.asarray(matrix, np.float32)
    high = exact.astype(jnp.bfloat16)
    low = (exact - high.astype(np.float32)).astype(jnp.bfloat16)
    return high, low


def left_split(matrix):
    high, low = halves(matrix)
    return np.concatenate([high, low, high], axis=1)


def left_exact(matrix):
    return np.concatenate([np.asarray(matrix).astype(jnp.bfloat16)] * 3, axis=1)


def constants(elements, coarse_count):
    stiffness, weights, basis, lam = gll_tables()
    stiffness = np.asarray(stiffness, np.float32).astype(np.float64)
    weights = np.asarray(weights, np.float32).astype(np.float64)
    basis = np.asarray(basis, np.float32).astype(np.float64)
    lam = np.asarray(lam, np.float32).astype(np.float64)
    points = 7 * elements
    z_pad = round_up(points, 128)
    s_pad = round_up(10 * elements, 128)
    every = list(range(8))
    pick_a, place_a = stack_map(
        {-1: [6, 7], 0: every, 1: [0, 1]}, {-1: [0, 1], 0: list(range(1, 9)), 1: [8, 9]}, 8, 10
    )
    pick_s, place_s = stack_map(
        {-1: [8, 9], 0: list(range(1, 9)), 1: [0, 1]}, {-1: [0, 1], 0: every, 1: [6, 7]}, 10, 8
    )
    basis_two = np.kron(basis, basis)
    spectral_in = np.zeros((SPEC, STACK))
    spectral_in[:100] = basis_two.T @ place_a
    spectral_out = np.zeros((STACK, SPEC))
    spectral_out[:, :100] = pick_s @ basis_two
    plane = np.kron(stiffness, np.diag(weights)) + np.kron(np.diag(weights), stiffness)
    plane_weight = np.kron(weights, weights)
    window = np.zeros((z_pad, s_pad))
    own_cols = np.zeros((z_pad, z_pad))
    before_cols = np.zeros((z_pad, z_pad))
    spread = np.zeros((elements, s_pad + 2 * z_pad))
    lines = np.zeros((8, max(z_pad, s_pad)))
    lines[2, 10 * elements :] = 1.0
    for elem in range(elements):
        prior = (elem - 1) % elements
        for col in range(10):
            spread[elem, col * elements + elem] = 1.0
            for row in range(10):
                window[(7 * elem - 1 + row) % points, col * elements + elem] += basis[row, col]
        for step in range(7):
            spread[elem, s_pad + 7 * elem + step] = 1.0
            spread[prior, s_pad + z_pad + 7 * elem + step] = 1.0
            lines[0, 7 * elem + step] = weights[step]
            for row in range(8):
                own_cols[(7 * elem + row) % points, 7 * elem + step] += stiffness[row, step]
        lines[1, 7 * elem] = weights[7]
        for row in range(8):
            before_cols[(7 * prior + row) % points, 7 * elem] += stiffness[row, 7]
    lam_all = np.zeros((SPEC, s_pad))
    lam_two = (lam[:, None] + lam[None, :]).reshape(-1)
    lam_all[:100, : 10 * elements] = lam_two[:, None] + np.repeat(lam, elements)[None, :]
    segments = np.zeros((coarse_count, z_pad))
    for row in range(coarse_count):
        length = points // coarse_count
        segments[row, row * length : (row + 1) * length] = 1.0
    window_high, window_low = halves(window)
    back_high, back_low = halves(window.T)
    inner = place_a.reshape(10, 10, STACK)[1:9, 1:9].reshape(OWN, STACK)
    inner = np.concatenate([inner[:, start : start + 8] for start, _ in LAST] + [np.zeros((OWN, 8))], axis=1)
    single = lambda value: np.asarray(value, np.float32)
    return {
        "pick_a": left_exact(pick_a),
        "spec_in": left_split(spectral_in),
        "spec_out": left_split(spectral_out),
        "pick_place": left_exact(pick_a @ place_s),
        "plane": left_split(pick_a @ plane),
        "inner": left_exact(inner),
        "win_h": window_high,
        "win_l": window_low,
        "back_h": back_high,
        "back_l": back_low,
        "own_cols": single(own_cols),
        "before_cols": single(before_cols),
        "lam_all": single(lam_all),
        "spread": single(spread),
        "lines": single(lines),
        "segments": single(segments),
        "plane_weight": single((pick_a @ plane_weight)[:, None]),
    }


def split_two(value):
    high = value.astype(jnp.bfloat16)
    return high, (value - high.astype(jnp.float32)).astype(jnp.bfloat16)


def mul(left, right):
    return jnp.dot(left, right, preferred_element_type=jnp.float32)


def left_mul(matrix_ref, value):
    high, low = split_two(value)
    return mul(matrix_ref[...], jnp.concatenate([high, high, low], axis=0))


def left_place(matrix_ref, value):
    high = value.astype(jnp.bfloat16)
    rest = value - high.astype(jnp.float32)
    middle, low = split_two(rest)
    return mul(matrix_ref[...], jnp.concatenate([high, middle, low], axis=0))


def right_mul(value, high_ref, low_ref):
    high, low = split_two(value)
    return mul(high, high_ref[...]) + (mul(high, low_ref[...]) + mul(low, high_ref[...]))


def each_other(count, act):
    if count <= 8:
        for step in range(1, count):
            act(step)
    else:

        def body(step, carry):
            act(step)
            return carry

        lax.fori_loop(1, count, body, 0)


def stages_of(n_gx, n_gy):
    return ("xy",) if n_gx * n_gy <= DIRECT else ("x", "y")


def stage_size(stage, n_gx, n_gy):
    return {"x": n_gx, "y": n_gy, "xy": n_gx * n_gy}[stage]


def kernel(n_gx, n_gy, n_in, *refs):
    sources = refs[:n_in]
    out_x, out_r = refs[n_in : n_in + 2]
    loaded = refs[n_in + 2 : 2 * n_in + 2]
    load_sem, stack, sending, z_high, z_low, scale, first, field_w, halo_send, halo_recv = refs[
        2 * n_in + 2 : 2 * n_in + 12
    ]
    lanes = refs[2 * n_in + 12 :]
    (
        rhs, pick_a, segments, factor, stiff, mass, spread, lines, lam_all, own_cols, before_cols,
        spec_in, win_h, win_l, back_h, back_l, spec_out, pick_place, plane, plane_weight, inner,
    ) = loaded
    loads = [
        pltpu.make_async_copy(source, target, load_sem.at[index])
        for index, (source, target) in enumerate(zip(sources, loaded))
    ]
    for load in loads:
        load.start()

    me_x, me_y = lax.axis_index("gx"), lax.axis_index("gy")
    points = rhs.shape[2]
    z_pad = win_h.shape[0]
    s_pad = win_h.shape[1]
    stages = stages_of(n_gx, n_gy)

    def beside(off_x, off_y):
        return (lax.rem(me_x + off_x + n_gx, n_gx), lax.rem(me_y + off_y + n_gy, n_gy))

    def each_offset(stage, act):
        if stage == "xy":
            for off_x in range(n_gx):
                for off_y in range(n_gy):
                    if off_x or off_y:
                        act(off_x, off_y)
        elif stage == "x":
            each_other(n_gx, lambda step: act(step, 0))
        else:
            each_other(n_gy, lambda step: act(0, step))

    barrier = pltpu.get_barrier_semaphore()

    def greet(off_x, off_y):
        pl.semaphore_signal(barrier, inc=1, device_id=beside(off_x, off_y), device_id_type=MESH)

    greeted = 0
    for stage in stages:
        each_offset(stage, greet)
        greeted += stage_size(stage, n_gx, n_gy) - 1
    if stages != ("xy",):
        for off_x, off_y, _, _ in SLOTS[4:]:
            greet(off_x, off_y)
        greeted += 4

    def halo_copy(turn, slot, start, rows):
        off_x, off_y, _, _ = SLOTS[slot]
        return pltpu.make_async_remote_copy(
            src_ref=sending.at[turn, pl.ds(start, rows)],
            dst_ref=stack.at[turn, pl.ds(start, rows)],
            send_sem=halo_send.at[turn, slot],
            recv_sem=halo_recv.at[turn, slot],
            device_id=beside(-off_x, -off_y),
            device_id_type=MESH,
        )

    def halo_copies(turn):
        if turn == ROUNDS - 1:
            return [halo_copy(turn, slot, start, 8) for start, slot in LAST]
        return [halo_copy(turn, slot, SLOTS[slot][2], SLOTS[slot][3]) for slot in range(8)]

    def halo_start(turn, rows):
        sending[turn] = rows
        for copy in halo_copies(turn):
            copy.start()
        stack[turn, pl.ds(0, OWN)] = rows[:OWN]

    def halo_wait(turn):
        for copy in halo_copies(turn):
            copy.wait_recv()

    def slot_of(stage, off_x, off_y):
        at_x, at_y = beside(off_x, off_y)
        return {"x": at_x, "y": at_y, "xy": at_x * n_gy + at_y}[stage]

    class Lane:
        def __init__(self, buffers):
            self.legs = [(stage,) + tuple(buffers[3 * at : 3 * at + 3]) for at, stage in enumerate(stages)]

        def copy(self, leg, off_x, off_y, slot):
            _, buf, send, recv = leg
            return pltpu.make_async_remote_copy(
                src_ref=buf.at[slot],
                dst_ref=buf.at[slot],
                send_sem=send.at[off_x * n_gy + off_y if leg[0] == "xy" else off_x + off_y],
                recv_sem=recv.at[off_x * n_gy + off_y if leg[0] == "xy" else off_x + off_y],
                device_id=beside(off_x, off_y),
                device_id_type=MESH,
            )

        def put(self, leg, value):
            mine = slot_of(leg[0], 0, 0)
            leg[1][mine] = value
            each_offset(leg[0], lambda x, y: self.copy(leg, x, y, mine).start())

        def take(self, leg):
            each_offset(leg[0], lambda x, y: self.copy(leg, x, y, slot_of(leg[0], -x, -y)).wait_recv())
            return jnp.sum(leg[1][...], axis=0)

        def start(self, value):
            self.put(self.legs[0], value)

        def middle(self):
            for before, after in zip(self.legs, self.legs[1:]):
                self.put(after, self.take(before))

        def finish(self):
            return self.take(self.legs[-1])

        def drain(self):
            for leg in self.legs:
                mine = slot_of(leg[0], 0, 0)
                each_offset(leg[0], lambda x, y: self.copy(leg, x, y, mine).wait_send())

    per_lane = 3 * len(stages)
    coarse = [Lane(lanes[:per_lane]), Lane(lanes[per_lane : 2 * per_lane])]
    sums = Lane(lanes[2 * per_lane :])

    point = lax.broadcasted_iota(jnp.int32, (OWN, z_pad), 0)
    at_x, at_y = point // 8, point % 8
    coarse_mask = (at_x >= 1) & (at_x <= 6) & (at_y >= 1) & (at_y <= 6)

    def coarse_start(turn, rows):
        line = jnp.sum(jnp.where(coarse_mask, rows, 0.0), axis=0, keepdims=True)
        held = jnp.sum(segments[...] * line, axis=1, keepdims=True)
        coarse[turn].start(jnp.sum(factor[...] * held, axis=0, keepdims=True))

    def coarse_finish(turn):
        total = coarse[turn].finish()
        values = jnp.sum(factor[...] * total, axis=1, keepdims=True)
        line = jnp.sum(segments[...] * values, axis=0, keepdims=True)
        return jnp.where(coarse_mask, line, 0.0)

    first[...] = jnp.zeros_like(first)
    for load in loads[:4]:
        load.wait()
    for row in range(7):
        first[pl.ds(8 * row, 7), pl.ds(0, points)] = rhs[row]
    right = first[...]
    rows = left_place(pick_a, right)
    pl.semaphore_wait(barrier, greeted)
    halo_start(0, rows)
    coarse_start(0, right)

    for load in loads[4:11]:
        load.wait()

    def spread_out(coef):
        flat = jnp.dot(
            jnp.broadcast_to(coef[0], (8, coef.shape[2])), spread[...],
            precision=exact_mode, preferred_element_type=jnp.float32,
        )[0:1]
        return flat[:, :s_pad], flat[:, s_pad : s_pad + z_pad], flat[:, s_pad + z_pad :]

    stiff_s, stiff_own, stiff_before = spread_out(stiff)
    mass_s, mass_own, mass_before = spread_out(mass)
    weight_own, weight_before = lines[0:1, :z_pad], lines[1:2, :z_pad]
    line_stiff = stiff_own * weight_own + stiff_before * weight_before
    line_mass = mass_own * weight_own + mass_before * weight_before
    scale[...] = 1.0 / (stiff_s * lam_all[...] + (mass_s + lines[2:3, :s_pad]))
    diagonal = lax.broadcasted_iota(jnp.int32, (z_pad, z_pad), 0) == lax.broadcasted_iota(
        jnp.int32, (z_pad, z_pad), 1
    )
    along = own_cols[...] * stiff_own + before_cols[...] * stiff_before
    z_high[...], z_low[...] = split_two(along + jnp.where(diagonal, line_mass, 0.0))

    for load in loads[11:]:
        load.wait()

    def schwarz(rows):
        spectral = right_mul(left_mul(spec_in, rows), win_h, win_l) * scale[...]
        return left_mul(spec_out, right_mul(spectral, back_h, back_l))

    def element(rows):
        wide = left_place(pick_place, rows)
        field = wide[:OWN]
        result = left_mul(plane, field * line_stiff) + plane_weight[...] * right_mul(
            wide, z_high, z_low
        )
        return field, result

    def precondition(turn):
        coarse[turn].middle()
        halo_wait(2 * turn)
        result = schwarz(stack[2 * turn])
        halo_start(2 * turn + 1, result)
        plate = coarse_finish(turn)
        stack[2 * turn + 1, pl.ds(0, OWN)] = result[:OWN] + plate

    def dot_line(left, other):
        return jnp.sum(left * other, axis=0, keepdims=True)

    def gathered(turn, own):
        parts = [stack[turn, pl.ds(start, 8)] for start, _ in LAST]
        return own + left_place(inner, jnp.concatenate(parts + [jnp.zeros_like(parts[0])], axis=0))

    owned = (at_x < 7) & (at_y < 7)

    precondition(0)
    halo_wait(1)
    z_field, w_rows = element(stack[1])
    halo_start(2, w_rows)
    w_local = w_rows[:OWN]
    coarse_start(1, w_local)
    precondition(1)
    field_w[...] = gathered(2, w_local)
    halo_wait(3)
    v_field, av_rows = element(stack[3])
    halo_start(4, av_rows)
    av_local = av_rows[:OWN]
    partial = jnp.concatenate(
        [
            dot_line(right, jnp.where(owned, z_field, 0.0)),
            dot_line(z_field, w_local),
            dot_line(right, jnp.where(owned, v_field, 0.0)),
            dot_line(v_field, w_local),
            dot_line(v_field, av_local),
            dot_line(z_field, av_local),
            jnp.zeros((2, z_pad), jnp.float32),
        ],
        axis=0,
    )
    at_row = lax.broadcasted_iota(jnp.int32, (8, 128), 0)
    at_lane = lax.broadcasted_iota(jnp.int32, (8, 128), 1)
    packed = jnp.where(at_row == at_lane, jnp.sum(partial, axis=1, keepdims=True), 0.0)
    sums.start(jnp.sum(packed, axis=0, keepdims=True))
    sums.middle()
    halo_wait(4)
    av_field = gathered(4, av_local)
    w_field = field_w[...]
    totals = sums.finish()
    rz, zw, rv, vw, vav, zav = [totals[:, lane : lane + 1] for lane in range(6)]
    step_0 = rz / zw
    rho_1 = rz - step_0 * (rv + zw) + step_0 * step_0 * vw
    momentum = rho_1 / rz
    curve = (
        zw - step_0 * (vw + zav) + step_0 * step_0 * vav
        + momentum * ((zw - step_0 * vw) + (zw - step_0 * zav))
        + momentum * momentum * zw
    )
    step_1 = rho_1 / curve
    next_dir = (z_field - step_0 * v_field) + momentum * z_field
    next_image = (w_field - step_0 * av_field) + momentum * w_field
    final_x = step_0 * z_field + step_1 * next_dir
    final_r = (right - step_0 * w_field) - step_1 * next_image
    for row in range(7):
        out_x[row] = final_x[8 * row : 8 * row + 7, :points]
        out_r[row] = final_r[8 * row : 8 * row + 7, :points]

    for turn in range(ROUNDS):
        for copy in halo_copies(turn):
            copy.wait_send()
    for lane in (*coarse, sums):
        lane.drain()


def local(n_gx, n_gy, right_side, stiff_coef, mass_coef, coarse_factor):
    elements = stiff_coef.shape[2]
    coarse_count, coarse_all = coarse_factor.shape
    tables = {name: jnp.asarray(table) for name, table in constants(elements, coarse_count).items()}
    tables.update(rhs=right_side, stiff=stiff_coef, mass=mass_coef, factor=coarse_factor)
    operands = [tables[name] for name in OPERANDS]
    z_pad = round_up(7 * elements, 128)
    s_pad = round_up(10 * elements, 128)
    dma = pltpu.SemaphoreType.DMA
    single = jnp.float32
    whole = pl.BlockSpec(memory_space=pltpu.VMEM)
    shape = jax.ShapeDtypeStruct(right_side.shape, single)
    lanes = []
    for width in (coarse_all, coarse_all, 128):
        for stage in stages_of(n_gx, n_gy):
            size = stage_size(stage, n_gx, n_gy)
            lanes += [pltpu.VMEM((size, 1, width), single), dma((size,)), dma((size,))]
    return pl.pallas_call(
        functools.partial(kernel, n_gx, n_gy, len(operands)),
        out_shape=(shape, shape),
        in_specs=[pl.BlockSpec(memory_space=pltpu.HBM)] * len(operands),
        out_specs=(whole, whole),
        scratch_shapes=[pltpu.VMEM(operand.shape, operand.dtype) for operand in operands]
        + [
            dma((len(operands),)),
            pltpu.VMEM((ROUNDS, STACK, z_pad), single),
            pltpu.VMEM((ROUNDS, STACK, z_pad), single),
            pltpu.VMEM((z_pad, z_pad), jnp.bfloat16),
            pltpu.VMEM((z_pad, z_pad), jnp.bfloat16),
            pltpu.VMEM((SPEC, s_pad), single),
            pltpu.VMEM((OWN, z_pad), single),
            pltpu.VMEM((OWN, z_pad), single),
            dma((ROUNDS, 8)),
            dma((ROUNDS, 8)),
        ]
        + lanes,
        compiler_params=pltpu.CompilerParams(
            collective_id=0, has_side_effects=True, vmem_limit_bytes=40 * 1024 * 1024
        ),
    )(*operands)


def solution(mesh):
    placed = (P("gx", "gy", None), P("gx", "gy", None), P("gx", "gy", None), P(("gx", "gy"), None))
    return jax.shard_map(
        functools.partial(local, mesh.shape["gx"], mesh.shape["gy"]),
        mesh=mesh,
        in_specs=placed,
        out_specs=(P("gx", "gy", None), P("gx", "gy", None)),
        check_vma=False,
    )
```

```python
import functools
import math

import jax
import jax.numpy as jnp
import numpy as np
from jax import lax
from jax.experimental import pallas as pl
from jax.experimental.pallas import tpu as pltpu
from jax.sharding import PartitionSpec as P

MESH = pl.DeviceIdType.MESH
exact_mode = lax.Precision.HIGHEST
ROUNDS = 5

OWN = 64
SLOTS = (
    (-1, 0, 64, 16),
    (1, 0, 80, 16),
    (0, -1, 96, 16),
    (0, 1, 112, 16),
    (-1, -1, 128, 8),
    (-1, 1, 136, 8),
    (1, -1, 144, 8),
    (1, 1, 152, 8),
)
STACK = 160
SPEC = 112
LAST = ((72, 0), (104, 2), (128, 4))
OPERANDS = (
    "rhs", "pick_a", "segments", "factor", "stiff", "mass", "spread", "lines", "lam_all", "own_cols", "before_cols",
    "spec_in", "window", "back", "spec_out", "pick_place", "plane", "plane_weight", "inner",
)
DIRECT = 64


def legendre_pair(position, degree):
    p_prev = 1.0
    p_now = position
    for order in range(2, degree + 1):
        p_next = ((2 * order - 1) * position * p_now - (order - 1) * p_prev) / order
        p_prev = p_now
        p_now = p_next
    return (p_now, p_prev)


def jacobi_eigen(matrix):
    size_n = matrix.shape[0]
    current = np.array(matrix)
    vectors = np.eye(size_n)
    for sweep in range(20):
        for row_p in range(size_n - 1):
            for row_q in range(row_p + 1, size_n):
                off_value = current[row_p, row_q]
                if abs(off_value) > 1e-300:
                    theta = (current[row_q, row_q] - current[row_p, row_p]) / (2.0 * off_value)
                    sign_t = 1.0 if theta >= 0.0 else -1.0
                    tangent = sign_t / (abs(theta) + math.sqrt(theta * theta + 1.0))
                    cosine = 1.0 / math.sqrt(tangent * tangent + 1.0)
                    sine = tangent * cosine
                    rotation = np.eye(size_n)
                    rotation[row_p, row_p] = cosine
                    rotation[row_q, row_q] = cosine
                    rotation[row_p, row_q] = sine
                    rotation[row_q, row_p] = -sine
                    current = rotation.T @ current @ rotation
                    vectors = vectors @ rotation
    return (np.array([current[idx, idx] for idx in range(size_n)]), vectors)


def gll_tables():
    degree = 7
    guesses = [
        -0.8717401485096066,
        -0.5917001814331423,
        -0.2092992179024789,
        0.2092992179024789,
        0.5917001814331423,
        0.8717401485096066,
    ]
    interior = []
    for guess in guesses:
        position = guess
        for newton in range(30):
            p_now, p_prev = legendre_pair(position, degree)
            first = degree * (position * p_now - p_prev) / (position * position - 1.0)
            second = (2.0 * position * first - degree * (degree + 1) * p_now) / (
                1.0 - position * position
            )
            position = position - first / second
        interior.append(position)
    points = np.array([-1.0] + interior + [1.0])
    values = np.array([legendre_pair(float(pt), degree)[0] for pt in points])
    weights = 2.0 / (degree * (degree + 1) * values**2)
    deriv_mat = np.zeros((8, 8))
    for left_idx in range(8):
        for right_idx in range(8):
            if left_idx != right_idx:
                deriv_mat[left_idx, right_idx] = values[left_idx] / (
                    values[right_idx] * (points[left_idx] - points[right_idx])
                )
    deriv_mat[0, 0] = -degree * (degree + 1) / 4.0
    deriv_mat[7, 7] = degree * (degree + 1) / 4.0
    stiffness = deriv_mat.T @ (weights[:, None] * deriv_mat)
    ext_stiff = np.zeros((10, 10))
    ext_stiff[1:9, 1:9] += stiffness
    ext_stiff[0:2, 0:2] += stiffness[6:8, 6:8]
    ext_stiff[8:10, 8:10] += stiffness[0:2, 0:2]
    ext_mass = np.zeros(10)
    ext_mass[1:9] += weights
    ext_mass[0:2] += weights[6:8]
    ext_mass[8:10] += weights[0:2]
    inv_root = 1.0 / np.sqrt(ext_mass)
    eigen_vals, eigen_vecs = jacobi_eigen(inv_root[:, None] * ext_stiff * inv_root[None, :])
    eigen_basis = inv_root[:, None] * eigen_vecs
    return stiffness, weights, eigen_basis, eigen_vals


def round_up(count, unit):
    return -(-count // unit) * unit


def stack_map(taken, placed, size_from, size_to):
    pick = np.zeros((STACK, size_from * size_from))
    place = np.zeros((size_to * size_to, STACK))
    for off_x, off_y, start, _ in ((0, 0, 0, OWN),) + SLOTS:
        row = start
        pairs_x = list(zip(taken[off_x], placed[off_x]))
        pairs_y = list(zip(taken[off_y], placed[off_y]))
        pairs = [(one, two) for one in pairs_x for two in pairs_y]
        if off_x == 0 and off_y != 0:
            pairs = [(one, two) for two in pairs_y for one in pairs_x]
        for (from_x, to_x), (from_y, to_y) in pairs:
            pick[row, from_x * size_from + from_y] = 1.0
            place[to_x * size_to + to_y, row] = 1.0
            row += 1
    return pick, place


def thrice(matrix):
    return np.concatenate([np.asarray(matrix, np.float32)] * 3, axis=1)


def constants(elements, coarse_count):
    stiffness, weights, basis, lam = gll_tables()
    stiffness = np.asarray(stiffness, np.float32).astype(np.float64)
    weights = np.asarray(weights, np.float32).astype(np.float64)
    basis = np.asarray(basis, np.float32).astype(np.float64)
    lam = np.asarray(lam, np.float32).astype(np.float64)
    points = 7 * elements
    z_pad = round_up(points, 128)
    s_pad = round_up(10 * elements, 128)
    every = list(range(8))
    pick_a, place_a = stack_map(
        {-1: [6, 7], 0: every, 1: [0, 1]}, {-1: [0, 1], 0: list(range(1, 9)), 1: [8, 9]}, 8, 10
    )
    pick_s, place_s = stack_map(
        {-1: [8, 9], 0: list(range(1, 9)), 1: [0, 1]}, {-1: [0, 1], 0: every, 1: [6, 7]}, 10, 8
    )
    basis_two = np.kron(basis, basis)
    spectral_in = np.zeros((SPEC, STACK))
    spectral_in[:100] = basis_two.T @ place_a
    spectral_out = np.zeros((STACK, SPEC))
    spectral_out[:, :100] = pick_s @ basis_two
    plane = np.kron(stiffness, np.diag(weights)) + np.kron(np.diag(weights), stiffness)
    plane_weight = np.kron(weights, weights)
    window = np.zeros((z_pad, s_pad))
    own_cols = np.zeros((z_pad, z_pad))
    before_cols = np.zeros((z_pad, z_pad))
    spread = np.zeros((elements, s_pad + 2 * z_pad))
    lines = np.zeros((8, max(z_pad, s_pad)))
    lines[2, 10 * elements :] = 1.0
    for elem in range(elements):
        prior = (elem - 1) % elements
        for col in range(10):
            spread[elem, col * elements + elem] = 1.0
            for row in range(10):
                window[(7 * elem - 1 + row) % points, col * elements + elem] += basis[row, col]
        for step in range(7):
            spread[elem, s_pad + 7 * elem + step] = 1.0
            spread[prior, s_pad + z_pad + 7 * elem + step] = 1.0
            lines[0, 7 * elem + step] = weights[step]
            for row in range(8):
                own_cols[(7 * elem + row) % points, 7 * elem + step] += stiffness[row, step]
        lines[1, 7 * elem] = weights[7]
        for row in range(8):
            before_cols[(7 * prior + row) % points, 7 * elem] += stiffness[row, 7]
    lam_all = np.zeros((SPEC, s_pad))
    lam_two = (lam[:, None] + lam[None, :]).reshape(-1)
    lam_all[:100, : 10 * elements] = lam_two[:, None] + np.repeat(lam, elements)[None, :]
    segments = np.zeros((coarse_count, z_pad))
    for row in range(coarse_count):
        length = points // coarse_count
        segments[row, row * length : (row + 1) * length] = 1.0
    inner = place_a.reshape(10, 10, STACK)[1:9, 1:9].reshape(OWN, STACK)
    inner = np.concatenate([inner[:, start : start + 8] for start, _ in LAST] + [np.zeros((OWN, 8))], axis=1)
    single = lambda value: np.asarray(value, np.float32)
    return {
        "pick_a": thrice(pick_a),
        "spec_in": thrice(spectral_in),
        "spec_out": thrice(spectral_out),
        "pick_place": thrice(pick_a @ place_s),
        "plane": thrice(pick_a @ plane),
        "inner": thrice(inner),
        "window": single(window),
        "back": single(window.T),
        "own_cols": single(own_cols),
        "before_cols": single(before_cols),
        "lam_all": single(lam_all),
        "spread": single(spread),
        "lines": single(lines),
        "segments": single(segments),
        "plane_weight": single((pick_a @ plane_weight)[:, None]),
    }


def split_two(value):
    high = value.astype(jnp.bfloat16)
    return high, (value - high.astype(jnp.float32)).astype(jnp.bfloat16)


def mul(left, right):
    return jnp.dot(left, right, preferred_element_type=jnp.float32)


def left_mul(matrix, value):
    high, low = split_two(value)
    return mul(matrix[...], jnp.concatenate([high, high, low], axis=0))


def left_place(matrix, value):
    high = value.astype(jnp.bfloat16)
    rest = value - high.astype(jnp.float32)
    middle, low = split_two(rest)
    return mul(matrix[...], jnp.concatenate([high, middle, low], axis=0))


def right_mul(value, high_ref, low_ref):
    high, low = split_two(value)
    return mul(high, high_ref[...]) + (mul(high, low_ref[...]) + mul(low, high_ref[...]))


def each_other(count, act):
    if count <= 8:
        for step in range(1, count):
            act(step)
    else:

        def body(step, carry):
            act(step)
            return carry

        lax.fori_loop(1, count, body, 0)


def stages_of(n_gx, n_gy):
    return ("xy",) if n_gx * n_gy <= DIRECT else ("x", "y")


def stage_size(stage, n_gx, n_gy):
    return {"x": n_gx, "y": n_gy, "xy": n_gx * n_gy}[stage]


def kernel(n_gx, n_gy, n_in, *refs):
    sources = refs[:n_in]
    out_x, out_r = refs[n_in : n_in + 2]
    loaded = refs[n_in + 2 : 2 * n_in + 2]
    load_sem, stack, sending, z_high, z_low, scale, first, field_w, halo_send, halo_recv = refs[
        2 * n_in + 2 : 2 * n_in + 12
    ]
    spec_in, spec_out, pick_place, plane, inner, win_h, win_l, back_h, back_l = refs[
        2 * n_in + 12 : 2 * n_in + 21
    ]
    lanes = refs[2 * n_in + 21 :]
    (
        rhs, pick_a_f, segments, factor, stiff, mass, spread, lines, lam_all, own_cols, before_cols,
        spec_in_f, window, back, spec_out_f, pick_place_f, plane_f, plane_weight, inner_f,
    ) = loaded
    loads = [
        pltpu.make_async_copy(source, target, load_sem.at[index])
        for index, (source, target) in enumerate(zip(sources, loaded))
    ]
    for load in loads:
        load.start()

    me_x, me_y = lax.axis_index("gx"), lax.axis_index("gy")
    points = rhs.shape[2]
    z_pad, s_pad = window.shape
    stages = stages_of(n_gx, n_gy)

    def beside(off_x, off_y):
        return (lax.rem(me_x + off_x + n_gx, n_gx), lax.rem(me_y + off_y + n_gy, n_gy))

    def each_offset(stage, act):
        if stage == "xy":
            for off_x in range(n_gx):
                for off_y in range(n_gy):
                    if off_x or off_y:
                        act(off_x, off_y)
        elif stage == "x":
            each_other(n_gx, lambda step: act(step, 0))
        else:
            each_other(n_gy, lambda step: act(0, step))

    barrier = pltpu.get_barrier_semaphore()

    def greet(off_x, off_y):
        pl.semaphore_signal(barrier, inc=1, device_id=beside(off_x, off_y), device_id_type=MESH)

    greeted = 0
    for stage in stages:
        each_offset(stage, greet)
        greeted += stage_size(stage, n_gx, n_gy) - 1
    if stages != ("xy",):
        for off_x, off_y, _, _ in SLOTS[4:]:
            greet(off_x, off_y)
        greeted += 4

    def halo_copy(turn, slot, start, rows):
        off_x, off_y, _, _ = SLOTS[slot]
        return pltpu.make_async_remote_copy(
            src_ref=sending.at[turn, pl.ds(start, rows)],
            dst_ref=stack.at[turn, pl.ds(start, rows)],
            send_sem=halo_send.at[turn, slot],
            recv_sem=halo_recv.at[turn, slot],
            device_id=beside(-off_x, -off_y),
            device_id_type=MESH,
        )

    def halo_copies(turn):
        if turn == ROUNDS - 1:
            return [halo_copy(turn, slot, start, 8) for start, slot in LAST]
        return [halo_copy(turn, slot, SLOTS[slot][2], SLOTS[slot][3]) for slot in range(8)]

    def halo_start(turn, rows):
        sending[turn] = rows
        for copy in halo_copies(turn):
            copy.start()
        stack[turn, pl.ds(0, OWN)] = rows[:OWN]

    def halo_wait(turn):
        for copy in halo_copies(turn):
            copy.wait_recv()

    def slot_of(stage, off_x, off_y):
        at_x, at_y = beside(off_x, off_y)
        return {"x": at_x, "y": at_y, "xy": at_x * n_gy + at_y}[stage]

    class Lane:
        def __init__(self, buffers):
            self.legs = [(stage,) + tuple(buffers[3 * at : 3 * at + 3]) for at, stage in enumerate(stages)]

        def copy(self, leg, off_x, off_y, slot):
            _, buf, send, recv = leg
            return pltpu.make_async_remote_copy(
                src_ref=buf.at[slot],
                dst_ref=buf.at[slot],
                send_sem=send.at[off_x * n_gy + off_y if leg[0] == "xy" else off_x + off_y],
                recv_sem=recv.at[off_x * n_gy + off_y if leg[0] == "xy" else off_x + off_y],
                device_id=beside(off_x, off_y),
                device_id_type=MESH,
            )

        def put(self, leg, value):
            mine = slot_of(leg[0], 0, 0)
            leg[1][mine] = value
            each_offset(leg[0], lambda x, y: self.copy(leg, x, y, mine).start())

        def take(self, leg):
            each_offset(leg[0], lambda x, y: self.copy(leg, x, y, slot_of(leg[0], -x, -y)).wait_recv())
            return jnp.sum(leg[1][...], axis=0)

        def start(self, value):
            self.put(self.legs[0], value)

        def middle(self):
            for before, after in zip(self.legs, self.legs[1:]):
                self.put(after, self.take(before))

        def finish(self):
            return self.take(self.legs[-1])

        def drain(self):
            for leg in self.legs:
                mine = slot_of(leg[0], 0, 0)
                each_offset(leg[0], lambda x, y: self.copy(leg, x, y, mine).wait_send())

    per_lane = 3 * len(stages)
    coarse = [Lane(lanes[:per_lane]), Lane(lanes[per_lane : 2 * per_lane])]
    sums = Lane(lanes[2 * per_lane :])

    point = lax.broadcasted_iota(jnp.int32, (OWN, z_pad), 0)
    at_x, at_y = point // 8, point % 8
    coarse_mask = (at_x >= 1) & (at_x <= 6) & (at_y >= 1) & (at_y <= 6)

    def coarse_start(turn, rows):
        line = jnp.sum(jnp.where(coarse_mask, rows, 0.0), axis=0, keepdims=True)
        held = jnp.sum(segments[...] * line, axis=1, keepdims=True)
        coarse[turn].start(jnp.sum(factor[...] * held, axis=0, keepdims=True))

    def coarse_finish(turn):
        total = coarse[turn].finish()
        values = jnp.sum(factor[...] * total, axis=1, keepdims=True)
        line = jnp.sum(segments[...] * values, axis=0, keepdims=True)
        return jnp.where(coarse_mask, line, 0.0)

    first[...] = jnp.zeros_like(first)
    for load in loads[:4]:
        load.wait()
    for row in range(7):
        first[pl.ds(8 * row, 7), pl.ds(0, points)] = rhs[row]
    right = first[...]
    rows = left_place(pick_a_f[...].astype(jnp.bfloat16), right)
    pl.semaphore_wait(barrier, greeted)
    halo_start(0, rows)
    coarse_start(0, right)

    for load in loads[4:11]:
        load.wait()

    def spread_out(coef):
        flat = jnp.dot(
            jnp.broadcast_to(coef[0], (8, coef.shape[2])), spread[...],
            precision=exact_mode, preferred_element_type=jnp.float32,
        )[0:1]
        return flat[:, :s_pad], flat[:, s_pad : s_pad + z_pad], flat[:, s_pad + z_pad :]

    stiff_s, stiff_own, stiff_before = spread_out(stiff)
    mass_s, mass_own, mass_before = spread_out(mass)
    weight_own, weight_before = lines[0:1, :z_pad], lines[1:2, :z_pad]
    line_stiff = stiff_own * weight_own + stiff_before * weight_before
    line_mass = mass_own * weight_own + mass_before * weight_before
    scale[...] = 1.0 / (stiff_s * lam_all[...] + (mass_s + lines[2:3, :s_pad]))
    diagonal = lax.broadcasted_iota(jnp.int32, (z_pad, z_pad), 0) == lax.broadcasted_iota(
        jnp.int32, (z_pad, z_pad), 1
    )
    along = own_cols[...] * stiff_own + before_cols[...] * stiff_before
    z_high[...], z_low[...] = split_two(along + jnp.where(diagonal, line_mass, 0.0))

    for load in loads[11:]:
        load.wait()

    def three_parts(source, target):
        high, low = split_two(source[...])
        column = lax.broadcasted_iota(jnp.int32, source.shape, 1)
        third = source.shape[1] // 3
        middle = (column >= third) & (column < 2 * third)
        target[...] = jnp.where(
            middle, low.astype(jnp.float32), high.astype(jnp.float32)
        ).astype(jnp.bfloat16)

    for source, target in ((spec_in_f, spec_in), (spec_out_f, spec_out), (plane_f, plane)):
        three_parts(source, target)
    for source, target in ((pick_place_f, pick_place), (inner_f, inner)):
        target[...] = source[...].astype(jnp.bfloat16)
    win_h[...], win_l[...] = split_two(window[...])
    back_h[...], back_l[...] = split_two(back[...])

    def schwarz(rows):
        spectral = right_mul(left_mul(spec_in, rows), win_h, win_l) * scale[...]
        return left_mul(spec_out, right_mul(spectral, back_h, back_l))

    def element(rows):
        wide = left_place(pick_place, rows)
        field = wide[:OWN]
        result = left_mul(plane, field * line_stiff) + plane_weight[...] * right_mul(
            wide, z_high, z_low
        )
        return field, result

    def precondition(turn):
        coarse[turn].middle()
        halo_wait(2 * turn)
        result = schwarz(stack[2 * turn])
        halo_start(2 * turn + 1, result)
        plate = coarse_finish(turn)
        stack[2 * turn + 1, pl.ds(0, OWN)] = result[:OWN] + plate

    def dot_line(left, other):
        return jnp.sum(left * other, axis=0, keepdims=True)

    def gathered(turn, own):
        parts = [stack[turn, pl.ds(start, 8)] for start, _ in LAST]
        return own + left_place(inner, jnp.concatenate(parts + [jnp.zeros_like(parts[0])], axis=0))

    owned = (at_x < 7) & (at_y < 7)

    precondition(0)
    halo_wait(1)
    z_field, w_rows = element(stack[1])
    halo_start(2, w_rows)
    w_local = w_rows[:OWN]
    coarse_start(1, w_local)
    precondition(1)
    field_w[...] = gathered(2, w_local)
    halo_wait(3)
    v_field, av_rows = element(stack[3])
    halo_start(4, av_rows)
    av_local = av_rows[:OWN]
    partial = jnp.concatenate(
        [
            dot_line(right, jnp.where(owned, z_field, 0.0)),
            dot_line(z_field, w_local),
            dot_line(right, jnp.where(owned, v_field, 0.0)),
            dot_line(v_field, w_local),
            dot_line(v_field, av_local),
            dot_line(z_field, av_local),
            jnp.zeros((2, z_pad), jnp.float32),
        ],
        axis=0,
    )
    at_row = lax.broadcasted_iota(jnp.int32, (8, 128), 0)
    at_lane = lax.broadcasted_iota(jnp.int32, (8, 128), 1)
    packed = jnp.where(at_row == at_lane, jnp.sum(partial, axis=1, keepdims=True), 0.0)
    sums.start(jnp.sum(packed, axis=0, keepdims=True))
    sums.middle()
    halo_wait(4)
    av_field = gathered(4, av_local)
    w_field = field_w[...]
    totals = sums.finish()
    rz, zw, rv, vw, vav, zav = [totals[:, lane : lane + 1] for lane in range(6)]
    step_0 = rz / zw
    rho_1 = rz - step_0 * (rv + zw) + step_0 * step_0 * vw
    momentum = rho_1 / rz
    curve = (
        zw - step_0 * (vw + zav) + step_0 * step_0 * vav
        + momentum * ((zw - step_0 * vw) + (zw - step_0 * zav))
        + momentum * momentum * zw
    )
    step_1 = rho_1 / curve
    next_dir = (z_field - step_0 * v_field) + momentum * z_field
    next_image = (w_field - step_0 * av_field) + momentum * w_field
    final_x = step_0 * z_field + step_1 * next_dir
    final_r = (right - step_0 * w_field) - step_1 * next_image
    for row in range(7):
        out_x[row] = final_x[8 * row : 8 * row + 7, :points]
        out_r[row] = final_r[8 * row : 8 * row + 7, :points]

    for turn in range(ROUNDS):
        for copy in halo_copies(turn):
            copy.wait_send()
    for lane in (*coarse, sums):
        lane.drain()


def local(n_gx, n_gy, right_side, stiff_coef, mass_coef, coarse_factor):
    elements = stiff_coef.shape[2]
    coarse_count, coarse_all = coarse_factor.shape
    tables = {name: jnp.asarray(table) for name, table in constants(elements, coarse_count).items()}
    tables.update(rhs=right_side, stiff=stiff_coef, mass=mass_coef, factor=coarse_factor)
    operands = [tables[name] for name in OPERANDS]
    z_pad = round_up(7 * elements, 128)
    s_pad = round_up(10 * elements, 128)
    dma = pltpu.SemaphoreType.DMA
    single = jnp.float32
    whole = pl.BlockSpec(memory_space=pltpu.VMEM)
    shape = jax.ShapeDtypeStruct(right_side.shape, single)
    lanes = []
    for width in (coarse_all, coarse_all, 128):
        for stage in stages_of(n_gx, n_gy):
            size = stage_size(stage, n_gx, n_gy)
            lanes += [pltpu.VMEM((size, 1, width), single), dma((size,)), dma((size,))]
    return pl.pallas_call(
        functools.partial(kernel, n_gx, n_gy, len(operands)),
        out_shape=(shape, shape),
        in_specs=[pl.BlockSpec(memory_space=pltpu.HBM)] * len(operands),
        out_specs=(whole, whole),
        scratch_shapes=[pltpu.VMEM(operand.shape, operand.dtype) for operand in operands]
        + [
            dma((len(operands),)),
            pltpu.VMEM((ROUNDS, STACK, z_pad), single),
            pltpu.VMEM((ROUNDS, STACK, z_pad), single),
            pltpu.VMEM((z_pad, z_pad), jnp.bfloat16),
            pltpu.VMEM((z_pad, z_pad), jnp.bfloat16),
            pltpu.VMEM((SPEC, s_pad), single),
            pltpu.VMEM((OWN, z_pad), single),
            pltpu.VMEM((OWN, z_pad), single),
            dma((ROUNDS, 8)),
            dma((ROUNDS, 8)),
        ]
        + [
            pltpu.VMEM(tables[name].shape, jnp.bfloat16)
            for name in (
                "spec_in", "spec_out", "pick_place", "plane", "inner", "window", "window", "back", "back",
            )
        ]
        + lanes,
        compiler_params=pltpu.CompilerParams(
            collective_id=0, has_side_effects=True, vmem_limit_bytes=60 * 1024 * 1024
        ),
    )(*operands)


def solution(mesh):
    placed = (P("gx", "gy", None), P("gx", "gy", None), P("gx", "gy", None), P(("gx", "gy"), None))
    return jax.shard_map(
        functools.partial(local, mesh.shape["gx"], mesh.shape["gy"]),
        mesh=mesh,
        in_specs=placed,
        out_specs=(P("gx", "gy", None), P("gx", "gy", None)),
        check_vma=False,
    )
```

```python
import functools
import math

import jax
import jax.numpy as jnp
import numpy as np
from jax import lax
from jax.experimental import pallas as pl
from jax.experimental.pallas import tpu as pltpu
from jax.sharding import PartitionSpec as P

MESH = pl.DeviceIdType.MESH
exact_mode = lax.Precision.HIGHEST
ROUNDS = 5

OWN = 64
SLOTS = (
    (-1, 0, 64, 16),
    (1, 0, 80, 16),
    (0, -1, 96, 16),
    (0, 1, 112, 16),
    (-1, -1, 128, 8),
    (-1, 1, 136, 8),
    (1, -1, 144, 8),
    (1, 1, 152, 8),
)
STACK = 160
SPEC = 112
PACKED = ((0, 24), (24, 24), (48, 24), (72, 24), (96, 8), (104, 8), (112, 8), (120, 8))
MESSAGE = 128
LAST = ((72, 0), (104, 2), (128, 4))
LAST_PACKED = {0: (8, 16), 2: (56, 16), 4: (96, 8)}
OPERANDS = (
    "rhs", "pick_a", "segments", "factor", "stiff", "mass", "spread", "lines", "lam_all", "own_cols", "before_cols",
    "spec_in", "window", "back", "spec_out", "pick_place", "plane", "plane_weight", "inner",
)
DIRECT = 64


def legendre_pair(position, degree):
    p_prev = 1.0
    p_now = position
    for order in range(2, degree + 1):
        p_next = ((2 * order - 1) * position * p_now - (order - 1) * p_prev) / order
        p_prev = p_now
        p_now = p_next
    return (p_now, p_prev)


def jacobi_eigen(matrix):
    size_n = matrix.shape[0]
    current = np.array(matrix)
    vectors = np.eye(size_n)
    for sweep in range(20):
        for row_p in range(size_n - 1):
            for row_q in range(row_p + 1, size_n):
                off_value = current[row_p, row_q]
                if abs(off_value) > 1e-300:
                    theta = (current[row_q, row_q] - current[row_p, row_p]) / (2.0 * off_value)
                    sign_t = 1.0 if theta >= 0.0 else -1.0
                    tangent = sign_t / (abs(theta) + math.sqrt(theta * theta + 1.0))
                    cosine = 1.0 / math.sqrt(tangent * tangent + 1.0)
                    sine = tangent * cosine
                    rotation = np.eye(size_n)
                    rotation[row_p, row_p] = cosine
                    rotation[row_q, row_q] = cosine
                    rotation[row_p, row_q] = sine
                    rotation[row_q, row_p] = -sine
                    current = rotation.T @ current @ rotation
                    vectors = vectors @ rotation
    return (np.array([current[idx, idx] for idx in range(size_n)]), vectors)


def gll_tables():
    degree = 7
    guesses = [
        -0.8717401485096066,
        -0.5917001814331423,
        -0.2092992179024789,
        0.2092992179024789,
        0.5917001814331423,
        0.8717401485096066,
    ]
    interior = []
    for guess in guesses:
        position = guess
        for newton in range(30):
            p_now, p_prev = legendre_pair(position, degree)
            first = degree * (position * p_now - p_prev) / (position * position - 1.0)
            second = (2.0 * position * first - degree * (degree + 1) * p_now) / (
                1.0 - position * position
            )
            position = position - first / second
        interior.append(position)
    points = np.array([-1.0] + interior + [1.0])
    values = np.array([legendre_pair(float(pt), degree)[0] for pt in points])
    weights = 2.0 / (degree * (degree + 1) * values**2)
    deriv_mat = np.zeros((8, 8))
    for left_idx in range(8):
        for right_idx in range(8):
            if left_idx != right_idx:
                deriv_mat[left_idx, right_idx] = values[left_idx] / (
                    values[right_idx] * (points[left_idx] - points[right_idx])
                )
    deriv_mat[0, 0] = -degree * (degree + 1) / 4.0
    deriv_mat[7, 7] = degree * (degree + 1) / 4.0
    stiffness = deriv_mat.T @ (weights[:, None] * deriv_mat)
    ext_stiff = np.zeros((10, 10))
    ext_stiff[1:9, 1:9] += stiffness
    ext_stiff[0:2, 0:2] += stiffness[6:8, 6:8]
    ext_stiff[8:10, 8:10] += stiffness[0:2, 0:2]
    ext_mass = np.zeros(10)
    ext_mass[1:9] += weights
    ext_mass[0:2] += weights[6:8]
    ext_mass[8:10] += weights[0:2]
    inv_root = 1.0 / np.sqrt(ext_mass)
    eigen_vals, eigen_vecs = jacobi_eigen(inv_root[:, None] * ext_stiff * inv_root[None, :])
    eigen_basis = inv_root[:, None] * eigen_vecs
    return stiffness, weights, eigen_basis, eigen_vals


def round_up(count, unit):
    return -(-count // unit) * unit


def stack_map(taken, placed, size_from, size_to):
    pick = np.zeros((STACK, size_from * size_from))
    place = np.zeros((size_to * size_to, STACK))
    for off_x, off_y, start, _ in ((0, 0, 0, OWN),) + SLOTS:
        row = start
        pairs_x = list(zip(taken[off_x], placed[off_x]))
        pairs_y = list(zip(taken[off_y], placed[off_y]))
        pairs = [(one, two) for one in pairs_x for two in pairs_y]
        if off_x == 0 and off_y != 0:
            pairs = [(one, two) for two in pairs_y for one in pairs_x]
        if off_x != 0 and off_y != 0:
            pairs = pairs + pairs
        for (from_x, to_x), (from_y, to_y) in pairs:
            pick[row, from_x * size_from + from_y] = 1.0
            place[to_x * size_to + to_y, row] = 1.0
            row += 1
    return pick, place


def thrice(matrix):
    return np.concatenate([np.asarray(matrix, np.float32)] * 3, axis=1)


def constants(elements, coarse_count):
    stiffness, weights, basis, lam = gll_tables()
    stiffness = np.asarray(stiffness, np.float32).astype(np.float64)
    weights = np.asarray(weights, np.float32).astype(np.float64)
    basis = np.asarray(basis, np.float32).astype(np.float64)
    lam = np.asarray(lam, np.float32).astype(np.float64)
    points = 7 * elements
    z_pad = round_up(points, 128)
    s_pad = round_up(10 * elements, 128)
    every = list(range(8))
    pick_a, place_a = stack_map(
        {-1: [6, 7], 0: every, 1: [0, 1]}, {-1: [0, 1], 0: list(range(1, 9)), 1: [8, 9]}, 8, 10
    )
    pick_s, place_s = stack_map(
        {-1: [8, 9], 0: list(range(1, 9)), 1: [0, 1]}, {-1: [0, 1], 0: every, 1: [6, 7]}, 10, 8
    )
    basis_two = np.kron(basis, basis)
    spectral_in = np.zeros((SPEC, STACK))
    spectral_in[:100] = basis_two.T @ place_a
    spectral_out = np.zeros((STACK, SPEC))
    spectral_out[:, :100] = pick_s @ basis_two
    plane = np.kron(stiffness, np.diag(weights)) + np.kron(np.diag(weights), stiffness)
    plane_weight = np.kron(weights, weights)
    window = np.zeros((z_pad, s_pad))
    own_cols = np.zeros((z_pad, z_pad))
    before_cols = np.zeros((z_pad, z_pad))
    spread = np.zeros((elements, s_pad + 2 * z_pad))
    lines = np.zeros((8, max(z_pad, s_pad)))
    lines[2, 10 * elements :] = 1.0
    for elem in range(elements):
        prior = (elem - 1) % elements
        for col in range(10):
            spread[elem, col * elements + elem] = 1.0
            for row in range(10):
                window[(7 * elem - 1 + row) % points, col * elements + elem] += basis[row, col]
        for step in range(7):
            spread[elem, s_pad + 7 * elem + step] = 1.0
            spread[prior, s_pad + z_pad + 7 * elem + step] = 1.0
            lines[0, 7 * elem + step] = weights[step]
            for row in range(8):
                own_cols[(7 * elem + row) % points, 7 * elem + step] += stiffness[row, step]
        lines[1, 7 * elem] = weights[7]
        for row in range(8):
            before_cols[(7 * prior + row) % points, 7 * elem] += stiffness[row, 7]
    lam_all = np.zeros((SPEC, s_pad))
    lam_two = (lam[:, None] + lam[None, :]).reshape(-1)
    lam_all[:100, : 10 * elements] = lam_two[:, None] + np.repeat(lam, elements)[None, :]
    segments = np.zeros((coarse_count, z_pad))
    for row in range(coarse_count):
        length = points // coarse_count
        segments[row, row * length : (row + 1) * length] = 1.0
    inner = place_a.reshape(10, 10, STACK)[1:9, 1:9].reshape(OWN, STACK)
    inner = np.concatenate([inner[:, start : start + 8] for start, _ in LAST] + [np.zeros((OWN, 8))], axis=1)
    single = lambda value: np.asarray(value, np.float32)
    return {
        "pick_a": thrice(pick_a),
        "spec_in": thrice(spectral_in),
        "spec_out": thrice(spectral_out),
        "pick_place": thrice(pick_a @ place_s),
        "plane": thrice(pick_a @ plane),
        "inner": thrice(inner),
        "window": single(window),
        "back": single(window.T),
        "own_cols": single(own_cols),
        "before_cols": single(before_cols),
        "lam_all": single(lam_all),
        "spread": single(spread),
        "lines": single(lines),
        "segments": single(segments),
        "plane_weight": single((pick_a @ plane_weight)[:, None]),
    }


def split_two(value):
    high = value.astype(jnp.bfloat16)
    return high, (value - high.astype(jnp.float32)).astype(jnp.bfloat16)


def mul(left, right):
    return jnp.dot(left, right, preferred_element_type=jnp.float32)


def left_mul(matrix, value):
    high, low = split_two(value)
    return mul(matrix[...], jnp.concatenate([high, high, low], axis=0))


def left_place(matrix, value):
    high = value.astype(jnp.bfloat16)
    rest = value - high.astype(jnp.float32)
    middle, low = split_two(rest)
    return mul(matrix[...], jnp.concatenate([high, middle, low], axis=0))


def right_mul(value, high_ref, low_ref):
    high, low = split_two(value)
    return mul(high, high_ref[...]) + (mul(high, low_ref[...]) + mul(low, high_ref[...]))


def each_other(count, act):
    if count <= 8:
        for step in range(1, count):
            act(step)
    else:

        def body(step, carry):
            act(step)
            return carry

        lax.fori_loop(1, count, body, 0)


def stages_of(n_gx, n_gy):
    return ("xy",) if n_gx * n_gy <= DIRECT else ("x", "y")


def stage_size(stage, n_gx, n_gy):
    return {"x": n_gx, "y": n_gy, "xy": n_gx * n_gy}[stage]


def kernel(n_gx, n_gy, n_in, *refs):
    sources = refs[:n_in]
    out_x, out_r = refs[n_in : n_in + 2]
    loaded = refs[n_in + 2 : 2 * n_in + 2]
    load_sem, arrived, sending, own_rows, z_high, z_low, scale, first, field_w, halo_send, halo_recv = refs[
        2 * n_in + 2 : 2 * n_in + 13
    ]
    spec_in, spec_out, pick_place, plane, inner, win_h, win_l, back_h, back_l = refs[
        2 * n_in + 13 : 2 * n_in + 22
    ]
    lanes = refs[2 * n_in + 22 :]
    (
        rhs, pick_a_f, segments, factor, stiff, mass, spread, lines, lam_all, own_cols, before_cols,
        spec_in_f, window, back, spec_out_f, pick_place_f, plane_f, plane_weight, inner_f,
    ) = loaded
    loads = [
        pltpu.make_async_copy(source, target, load_sem.at[index])
        for index, (source, target) in enumerate(zip(sources, loaded))
    ]
    for load in loads:
        load.start()

    me_x, me_y = lax.axis_index("gx"), lax.axis_index("gy")
    points = rhs.shape[2]
    z_pad, s_pad = window.shape
    stages = stages_of(n_gx, n_gy)

    def beside(off_x, off_y):
        return (lax.rem(me_x + off_x + n_gx, n_gx), lax.rem(me_y + off_y + n_gy, n_gy))

    def each_offset(stage, act):
        if stage == "xy":
            for off_x in range(n_gx):
                for off_y in range(n_gy):
                    if off_x or off_y:
                        act(off_x, off_y)
        elif stage == "x":
            each_other(n_gx, lambda step: act(step, 0))
        else:
            each_other(n_gy, lambda step: act(0, step))

    barrier = pltpu.get_barrier_semaphore()

    def greet(off_x, off_y):
        pl.semaphore_signal(barrier, inc=1, device_id=beside(off_x, off_y), device_id_type=MESH)

    greeted = 0
    for stage in stages:
        each_offset(stage, greet)
        greeted += stage_size(stage, n_gx, n_gy) - 1
    if stages != ("xy",):
        for off_x, off_y, _, _ in SLOTS[4:]:
            greet(off_x, off_y)
        greeted += 4

    def halo_copy(turn, slot, start, rows):
        off_x, off_y, _, _ = SLOTS[slot]
        return pltpu.make_async_remote_copy(
            src_ref=sending.at[turn, pl.ds(start, rows)],
            dst_ref=arrived.at[turn, pl.ds(start, rows)],
            send_sem=halo_send.at[turn, slot],
            recv_sem=halo_recv.at[turn, slot],
            device_id=beside(-off_x, -off_y),
            device_id_type=MESH,
        )

    def halo_copies(turn):
        if turn == ROUNDS - 1:
            return [halo_copy(turn, slot, *LAST_PACKED[slot]) for _, slot in LAST]
        return [halo_copy(turn, slot, *PACKED[slot]) for slot in range(8)]

    tile_row = lax.broadcasted_iota(jnp.int32, (8, 128), 0)
    tile_lane = lax.broadcasted_iota(jnp.int32, (8, 128), 1)

    def halo_start(turn, rows):
        for slot, (_, _, start, count) in enumerate(SLOTS):
            at = PACKED[slot][0]
            if count == 8:
                part = rows[start : start + 8]
                sending[turn, pl.ds(at, 8)] = jnp.where(tile_row < 4, part[:, :128], part[:, 128:])
            else:
                sending[turn, pl.ds(at, 16)] = rows[start : start + 16, :128]
                sending[turn, pl.ds(at + 16, 8)] = rows[start : start + 8, 128:] + pltpu.roll(
                    rows[start + 8 : start + 16, 128:], 64, 1
                )
        for copy in halo_copies(turn):
            copy.start()
        own_rows[turn] = rows[:OWN]

    def left_half(tile):
        return jnp.where(tile_lane < 64, tile, 0.0)

    def corner_rows(turn, slot):
        tile = arrived[turn, pl.ds(PACKED[slot][0], 8)]
        upper = jnp.where(tile_row < 4, tile, 0.0)
        return jnp.concatenate([upper, jnp.where(tile_row < 4, 0.0, tile)], axis=1)

    def first_rows(turn, slot):
        at = PACKED[slot][0]
        tail = arrived[turn, pl.ds(at + 16, 8)]
        return jnp.concatenate([arrived[turn, pl.ds(at, 8)], left_half(tail)], axis=1)

    def second_rows(turn, slot):
        at = PACKED[slot][0]
        tail = pltpu.roll(arrived[turn, pl.ds(at + 16, 8)], 64, 1)
        return jnp.concatenate([arrived[turn, pl.ds(at + 8, 8)], left_half(tail)], axis=1)

    def halo_wait(turn):
        for copy in halo_copies(turn):
            copy.wait_recv()

    def stack(turn):
        parts = [own_rows[turn]]
        for slot in range(4):
            parts += [first_rows(turn, slot), second_rows(turn, slot)]
        parts += [corner_rows(turn, slot) for slot in range(4, 8)]
        return jnp.concatenate(parts, axis=0)

    def halo_drain(turn):
        for copy in halo_copies(turn):
            copy.wait_send()

    def slot_of(stage, off_x, off_y):
        at_x, at_y = beside(off_x, off_y)
        return {"x": at_x, "y": at_y, "xy": at_x * n_gy + at_y}[stage]

    class Lane:
        def __init__(self, stages, buffers):
            self.legs = [(stage,) + tuple(buffers[3 * at : 3 * at + 3]) for at, stage in enumerate(stages)]

        def copy(self, leg, off_x, off_y, slot):
            _, buf, send, recv = leg
            return pltpu.make_async_remote_copy(
                src_ref=buf.at[slot],
                dst_ref=buf.at[slot],
                send_sem=send.at[off_x * n_gy + off_y if leg[0] == "xy" else off_x + off_y],
                recv_sem=recv.at[off_x * n_gy + off_y if leg[0] == "xy" else off_x + off_y],
                device_id=beside(off_x, off_y),
                device_id_type=MESH,
            )

        def put(self, leg, value):
            mine = slot_of(leg[0], 0, 0)
            leg[1][mine] = value
            each_offset(leg[0], lambda x, y: self.copy(leg, x, y, mine).start())

        def take(self, leg):
            each_offset(leg[0], lambda x, y: self.copy(leg, x, y, slot_of(leg[0], -x, -y)).wait_recv())
            return jnp.sum(leg[1][...], axis=0)

        def start(self, value):
            self.put(self.legs[0], value)

        def middle(self):
            for before, after in zip(self.legs, self.legs[1:]):
                self.put(after, self.take(before))

        def finish(self):
            return self.take(self.legs[-1])

        def drain(self):
            for leg in self.legs:
                mine = slot_of(leg[0], 0, 0)
                each_offset(leg[0], lambda x, y: self.copy(leg, x, y, mine).wait_send())

    coarse = [Lane(("x", "y"), lanes[:6]), Lane(("x", "y"), lanes[6:12])]
    sums = Lane(stages, lanes[12:])

    point = lax.broadcasted_iota(jnp.int32, (OWN, z_pad), 0)
    at_x, at_y = point // 8, point % 8
    coarse_mask = (at_x >= 1) & (at_x <= 6) & (at_y >= 1) & (at_y <= 6)

    def coarse_start(turn, rows):
        line = jnp.sum(jnp.where(coarse_mask, rows, 0.0), axis=0, keepdims=True)
        held = jnp.sum(segments[...] * line, axis=1, keepdims=True)
        coarse[turn].start(jnp.sum(factor[...] * held, axis=0, keepdims=True))

    def coarse_finish(turn):
        total = coarse[turn].finish()
        values = jnp.sum(factor[...] * total, axis=1, keepdims=True)
        line = jnp.sum(segments[...] * values, axis=0, keepdims=True)
        return jnp.where(coarse_mask, line, 0.0)

    first[...] = jnp.zeros_like(first)
    for load in loads[:4]:
        load.wait()
    for row in range(7):
        first[pl.ds(8 * row, 7), pl.ds(0, points)] = rhs[row]
    right = first[...]
    rows = left_place(pick_a_f[...].astype(jnp.bfloat16), right)
    pl.semaphore_wait(barrier, greeted)
    halo_start(0, rows)
    coarse_start(0, right)

    for load in loads[4:11]:
        load.wait()

    def spread_out(coef):
        flat = jnp.dot(
            jnp.broadcast_to(coef[0], (8, coef.shape[2])), spread[...],
            precision=exact_mode, preferred_element_type=jnp.float32,
        )[0:1]
        return flat[:, :s_pad], flat[:, s_pad : s_pad + z_pad], flat[:, s_pad + z_pad :]

    stiff_s, stiff_own, stiff_before = spread_out(stiff)
    mass_s, mass_own, mass_before = spread_out(mass)
    weight_own, weight_before = lines[0:1, :z_pad], lines[1:2, :z_pad]
    line_stiff = stiff_own * weight_own + stiff_before * weight_before
    line_mass = mass_own * weight_own + mass_before * weight_before
    scale[...] = 1.0 / (stiff_s * lam_all[...] + (mass_s + lines[2:3, :s_pad]))
    diagonal = lax.broadcasted_iota(jnp.int32, (z_pad, z_pad), 0) == lax.broadcasted_iota(
        jnp.int32, (z_pad, z_pad), 1
    )
    along = own_cols[...] * stiff_own + before_cols[...] * stiff_before
    z_high[...], z_low[...] = split_two(along + jnp.where(diagonal, line_mass, 0.0))

    for load in loads[11:]:
        load.wait()

    def three_parts(source, target):
        high, low = split_two(source[...])
        column = lax.broadcasted_iota(jnp.int32, source.shape, 1)
        third = source.shape[1] // 3
        middle = (column >= third) & (column < 2 * third)
        target[...] = jnp.where(
            middle, low.astype(jnp.float32), high.astype(jnp.float32)
        ).astype(jnp.bfloat16)

    for source, target in ((spec_in_f, spec_in), (spec_out_f, spec_out), (plane_f, plane)):
        three_parts(source, target)
    for source, target in ((pick_place_f, pick_place), (inner_f, inner)):
        target[...] = source[...].astype(jnp.bfloat16)
    win_h[...], win_l[...] = split_two(window[...])
    back_h[...], back_l[...] = split_two(back[...])

    def schwarz(rows):
        spectral = right_mul(left_mul(spec_in, rows), win_h, win_l) * scale[...]
        return left_mul(spec_out, right_mul(spectral, back_h, back_l))

    def element(rows):
        wide = left_place(pick_place, rows)
        field = wide[:OWN]
        result = left_mul(plane, field * line_stiff) + plane_weight[...] * right_mul(
            wide, z_high, z_low
        )
        return field, result

    def precondition(turn):
        coarse[turn].middle()
        halo_wait(2 * turn)
        result = schwarz(stack(2 * turn))
        halo_start(2 * turn + 1, result)
        plate = coarse_finish(turn)
        own_rows[2 * turn + 1] = result[:OWN] + plate
        halo_drain(2 * turn)
        coarse[turn].drain()

    def dot_line(left, other):
        return jnp.sum(left * other, axis=0, keepdims=True)

    def gathered(turn, own):
        parts = [second_rows(turn, 0), second_rows(turn, 2), corner_rows(turn, 4)]
        return own + left_place(inner, jnp.concatenate(parts + [jnp.zeros_like(parts[0])], axis=0))

    owned = (at_x < 7) & (at_y < 7)

    precondition(0)
    halo_wait(1)
    z_field, w_rows = element(stack(1))
    halo_start(2, w_rows)
    w_local = w_rows[:OWN]
    coarse_start(1, w_local)
    precondition(1)
    field_w[...] = gathered(2, w_local)
    halo_wait(3)
    v_field, av_rows = element(stack(3))
    halo_start(4, av_rows)
    av_local = av_rows[:OWN]
    partial = jnp.concatenate(
        [
            dot_line(right, jnp.where(owned, z_field, 0.0)),
            dot_line(z_field, w_local),
            dot_line(right, jnp.where(owned, v_field, 0.0)),
            dot_line(v_field, w_local),
            dot_line(v_field, av_local),
            dot_line(z_field, av_local),
            jnp.zeros((2, z_pad), jnp.float32),
        ],
        axis=0,
    )
    at_row = lax.broadcasted_iota(jnp.int32, (8, 128), 0)
    at_lane = lax.broadcasted_iota(jnp.int32, (8, 128), 1)
    packed = jnp.where(at_row == at_lane, jnp.sum(partial, axis=1, keepdims=True), 0.0)
    sums.start(jnp.sum(packed, axis=0, keepdims=True))
    sums.middle()
    for turn in (1, 3, 4):
        halo_drain(turn)
    sums.drain()
    halo_wait(4)
    av_field = gathered(4, av_local)
    w_field = field_w[...]
    totals = sums.finish()
    rz, zw, rv, vw, vav, zav = [totals[:, lane : lane + 1] for lane in range(6)]
    step_0 = rz / zw
    rho_1 = rz - step_0 * (rv + zw) + step_0 * step_0 * vw
    momentum = rho_1 / rz
    curve = (
        zw - step_0 * (vw + zav) + step_0 * step_0 * vav
        + momentum * ((zw - step_0 * vw) + (zw - step_0 * zav))
        + momentum * momentum * zw
    )
    step_1 = rho_1 / curve
    next_dir = (z_field - step_0 * v_field) + momentum * z_field
    next_image = (w_field - step_0 * av_field) + momentum * w_field
    final_x = step_0 * z_field + step_1 * next_dir
    final_r = (right - step_0 * w_field) - step_1 * next_image
    for row in range(7):
        out_x[row] = final_x[8 * row : 8 * row + 7, :points]
        out_r[row] = final_r[8 * row : 8 * row + 7, :points]


def move(from_x, from_r, to_x, to_r, sem):
    copies = [
        pltpu.make_async_copy(from_x, to_x, sem.at[0]),
        pltpu.make_async_copy(from_r, to_r, sem.at[1]),
    ]
    for copy in copies:
        copy.start()
    for copy in copies:
        copy.wait()


def local(n_gx, n_gy, right_side, stiff_coef, mass_coef, coarse_factor):
    elements = stiff_coef.shape[2]
    coarse_count, coarse_all = coarse_factor.shape
    tables = {name: jnp.asarray(table) for name, table in constants(elements, coarse_count).items()}
    tables.update(rhs=right_side, stiff=stiff_coef, mass=mass_coef, factor=coarse_factor)
    operands = [tables[name] for name in OPERANDS]
    z_pad = round_up(7 * elements, 128)
    s_pad = round_up(10 * elements, 128)
    dma = pltpu.SemaphoreType.DMA
    single = jnp.float32
    whole = pl.BlockSpec(memory_space=pltpu.VMEM)
    shape = jax.ShapeDtypeStruct(right_side.shape, single)
    lanes = []
    two = ("x", "y")
    for width, stages in ((coarse_all, two), (coarse_all, two), (128, stages_of(n_gx, n_gy))):
        for stage in stages:
            size = stage_size(stage, n_gx, n_gy)
            lanes += [pltpu.VMEM((size, 1, width), single), dma((size,)), dma((size,))]
    result = pl.pallas_call(
        functools.partial(kernel, n_gx, n_gy, len(operands)),
        out_shape=(shape, shape),
        in_specs=[pl.BlockSpec(memory_space=pltpu.HBM)] * len(operands),
        out_specs=(whole, whole),
        scratch_shapes=[pltpu.VMEM(operand.shape, operand.dtype) for operand in operands]
        + [
            dma((len(operands),)),
            pltpu.VMEM((ROUNDS, MESSAGE, 128), single),
            pltpu.VMEM((ROUNDS, MESSAGE, 128), single),
            pltpu.VMEM((ROUNDS, OWN, z_pad), single),
            pltpu.VMEM((z_pad, z_pad), jnp.bfloat16),
            pltpu.VMEM((z_pad, z_pad), jnp.bfloat16),
            pltpu.VMEM((SPEC, s_pad), single),
            pltpu.VMEM((OWN, z_pad), single),
            pltpu.VMEM((OWN, z_pad), single),
            dma((ROUNDS, 8)),
            dma((ROUNDS, 8)),
        ]
        + [
            pltpu.VMEM(tables[name].shape, jnp.bfloat16)
            for name in (
                "spec_in", "spec_out", "pick_place", "plane", "inner", "window", "window", "back", "back",
            )
        ]
        + lanes,
        compiler_params=pltpu.CompilerParams(
            collective_id=0, has_side_effects=True, vmem_limit_bytes=60 * 1024 * 1024
        ),
    )(*operands)
    return pl.pallas_call(
        move,
        out_shape=(shape, shape),
        in_specs=[pl.BlockSpec(memory_space=pltpu.HBM)] * 2,
        out_specs=(pl.BlockSpec(memory_space=pltpu.HBM),) * 2,
        scratch_shapes=[dma((2,))],
        compiler_params=pltpu.CompilerParams(vmem_limit_bytes=60 * 1024 * 1024),
    )(*result)


def solution(mesh):
    placed = (P("gx", "gy", None), P("gx", "gy", None), P("gx", "gy", None), P(("gx", "gy"), None))
    return jax.shard_map(
        functools.partial(local, mesh.shape["gx"], mesh.shape["gy"]),
        mesh=mesh,
        in_specs=placed,
        out_specs=(P("gx", "gy", None), P("gx", "gy", None)),
        check_vma=False,
    )
```

```python
import functools
import math

import jax
import jax.numpy as jnp
import numpy as np
from jax import lax
from jax.experimental import pallas as pl
from jax.experimental.pallas import tpu as pltpu
from jax.sharding import PartitionSpec as P

MESH = pl.DeviceIdType.MESH
exact_mode = lax.Precision.HIGHEST
ROUNDS = 5

OWN = 64
SLOTS = (
    (-1, 0, 64, 16),
    (1, 0, 80, 16),
    (0, -1, 96, 16),
    (0, 1, 112, 16),
    (-1, -1, 128, 8),
    (-1, 1, 136, 8),
    (1, -1, 144, 8),
    (1, 1, 152, 8),
)
STACK = 160
SPEC = 112
PACKED = ((0, 24), (24, 24), (48, 24), (72, 24), (96, 8), (104, 8), (112, 8), (120, 8))
MESSAGE = 128
LAST = ((72, 0), (104, 2), (128, 4))
LAST_PACKED = {0: (8, 16), 2: (56, 16), 4: (96, 8)}
OPERANDS = (
    "rhs", "pick_a", "segments", "factor",
    "stiff", "mass", "spread", "lines", "lam_all", "spec_in", "window", "back", "spec_out",
    "own_cols", "before_cols", "pick_place", "plane", "plane_weight", "inner",
)
DIRECT = 64


def legendre_pair(position, degree):
    p_prev = 1.0
    p_now = position
    for order in range(2, degree + 1):
        p_next = ((2 * order - 1) * position * p_now - (order - 1) * p_prev) / order
        p_prev = p_now
        p_now = p_next
    return (p_now, p_prev)


def jacobi_eigen(matrix):
    size_n = matrix.shape[0]
    current = np.array(matrix)
    vectors = np.eye(size_n)
    for sweep in range(20):
        for row_p in range(size_n - 1):
            for row_q in range(row_p + 1, size_n):
                off_value = current[row_p, row_q]
                if abs(off_value) > 1e-300:
                    theta = (current[row_q, row_q] - current[row_p, row_p]) / (2.0 * off_value)
                    sign_t = 1.0 if theta >= 0.0 else -1.0
                    tangent = sign_t / (abs(theta) + math.sqrt(theta * theta + 1.0))
                    cosine = 1.0 / math.sqrt(tangent * tangent + 1.0)
                    sine = tangent * cosine
                    rotation = np.eye(size_n)
                    rotation[row_p, row_p] = cosine
                    rotation[row_q, row_q] = cosine
                    rotation[row_p, row_q] = sine
                    rotation[row_q, row_p] = -sine
                    current = rotation.T @ current @ rotation
                    vectors = vectors @ rotation
    return (np.array([current[idx, idx] for idx in range(size_n)]), vectors)


def gll_tables():
    degree = 7
    guesses = [
        -0.8717401485096066,
        -0.5917001814331423,
        -0.2092992179024789,
        0.2092992179024789,
        0.5917001814331423,
        0.8717401485096066,
    ]
    interior = []
    for guess in guesses:
        position = guess
        for newton in range(30):
            p_now, p_prev = legendre_pair(position, degree)
            first = degree * (position * p_now - p_prev) / (position * position - 1.0)
            second = (2.0 * position * first - degree * (degree + 1) * p_now) / (
                1.0 - position * position
            )
            position = position - first / second
        interior.append(position)
    points = np.array([-1.0] + interior + [1.0])
    values = np.array([legendre_pair(float(pt), degree)[0] for pt in points])
    weights = 2.0 / (degree * (degree + 1) * values**2)
    deriv_mat = np.zeros((8, 8))
    for left_idx in range(8):
        for right_idx in range(8):
            if left_idx != right_idx:
                deriv_mat[left_idx, right_idx] = values[left_idx] / (
                    values[right_idx] * (points[left_idx] - points[right_idx])
                )
    deriv_mat[0, 0] = -degree * (degree + 1) / 4.0
    deriv_mat[7, 7] = degree * (degree + 1) / 4.0
    stiffness = deriv_mat.T @ (weights[:, None] * deriv_mat)
    ext_stiff = np.zeros((10, 10))
    ext_stiff[1:9, 1:9] += stiffness
    ext_stiff[0:2, 0:2] += stiffness[6:8, 6:8]
    ext_stiff[8:10, 8:10] += stiffness[0:2, 0:2]
    ext_mass = np.zeros(10)
    ext_mass[1:9] += weights
    ext_mass[0:2] += weights[6:8]
    ext_mass[8:10] += weights[0:2]
    inv_root = 1.0 / np.sqrt(ext_mass)
    eigen_vals, eigen_vecs = jacobi_eigen(inv_root[:, None] * ext_stiff * inv_root[None, :])
    eigen_basis = inv_root[:, None] * eigen_vecs
    return stiffness, weights, eigen_basis, eigen_vals


def round_up(count, unit):
    return -(-count // unit) * unit


def stack_map(taken, placed, size_from, size_to):
    pick = np.zeros((STACK, size_from * size_from))
    place = np.zeros((size_to * size_to, STACK))
    for off_x, off_y, start, _ in ((0, 0, 0, OWN),) + SLOTS:
        row = start
        pairs_x = list(zip(taken[off_x], placed[off_x]))
        pairs_y = list(zip(taken[off_y], placed[off_y]))
        pairs = [(one, two) for one in pairs_x for two in pairs_y]
        if off_x == 0 and off_y != 0:
            pairs = [(one, two) for two in pairs_y for one in pairs_x]
        if off_x != 0 and off_y != 0:
            pairs = pairs + pairs
        for (from_x, to_x), (from_y, to_y) in pairs:
            pick[row, from_x * size_from + from_y] = 1.0
            place[to_x * size_to + to_y, row] = 1.0
            row += 1
    return pick, place


def thrice(matrix):
    return np.concatenate([np.asarray(matrix, np.float32)] * 3, axis=1)


def constants(elements, coarse_count):
    stiffness, weights, basis, lam = gll_tables()
    stiffness = np.asarray(stiffness, np.float32).astype(np.float64)
    weights = np.asarray(weights, np.float32).astype(np.float64)
    basis = np.asarray(basis, np.float32).astype(np.float64)
    lam = np.asarray(lam, np.float32).astype(np.float64)
    points = 7 * elements
    z_pad = round_up(points, 128)
    s_pad = round_up(10 * elements, 128)
    every = list(range(8))
    pick_a, place_a = stack_map(
        {-1: [6, 7], 0: every, 1: [0, 1]}, {-1: [0, 1], 0: list(range(1, 9)), 1: [8, 9]}, 8, 10
    )
    pick_s, place_s = stack_map(
        {-1: [8, 9], 0: list(range(1, 9)), 1: [0, 1]}, {-1: [0, 1], 0: every, 1: [6, 7]}, 10, 8
    )
    basis_two = np.kron(basis, basis)
    spectral_in = np.zeros((SPEC, STACK))
    spectral_in[:100] = basis_two.T @ place_a
    spectral_out = np.zeros((STACK, SPEC))
    spectral_out[:, :100] = pick_s @ basis_two
    plane = np.kron(stiffness, np.diag(weights)) + np.kron(np.diag(weights), stiffness)
    plane_weight = np.kron(weights, weights)
    window = np.zeros((z_pad, s_pad))
    own_cols = np.zeros((z_pad, z_pad))
    before_cols = np.zeros((z_pad, z_pad))
    spread = np.zeros((elements, s_pad + 2 * z_pad))
    lines = np.zeros((8, max(z_pad, s_pad)))
    lines[2, 10 * elements :] = 1.0
    for elem in range(elements):
        prior = (elem - 1) % elements
        for col in range(10):
            spread[elem, col * elements + elem] = 1.0
            for row in range(10):
                window[(7 * elem - 1 + row) % points, col * elements + elem] += basis[row, col]
        for step in range(7):
            spread[elem, s_pad + 7 * elem + step] = 1.0
            spread[prior, s_pad + z_pad + 7 * elem + step] = 1.0
            lines[0, 7 * elem + step] = weights[step]
            for row in range(8):
                own_cols[(7 * elem + row) % points, 7 * elem + step] += stiffness[row, step]
        lines[1, 7 * elem] = weights[7]
        for row in range(8):
            before_cols[(7 * prior + row) % points, 7 * elem] += stiffness[row, 7]
    lam_all = np.zeros((SPEC, s_pad))
    lam_two = (lam[:, None] + lam[None, :]).reshape(-1)
    lam_all[:100, : 10 * elements] = lam_two[:, None] + np.repeat(lam, elements)[None, :]
    segments = np.zeros((coarse_count, z_pad))
    for row in range(coarse_count):
        length = points // coarse_count
        segments[row, row * length : (row + 1) * length] = 1.0
    inner = place_a.reshape(10, 10, STACK)[1:9, 1:9].reshape(OWN, STACK)
    inner = np.concatenate([inner[:, start : start + 8] for start, _ in LAST] + [np.zeros((OWN, 8))], axis=1)
    single = lambda value: np.asarray(value, np.float32)
    return {
        "pick_a": thrice(pick_a),
        "spec_in": thrice(spectral_in),
        "spec_out": thrice(spectral_out),
        "pick_place": thrice(pick_a @ place_s),
        "plane": thrice(pick_a @ plane),
        "inner": thrice(inner),
        "window": single(window),
        "back": single(window.T),
        "own_cols": single(own_cols),
        "before_cols": single(before_cols),
        "lam_all": single(lam_all),
        "spread": single(spread),
        "lines": single(lines),
        "segments": single(segments),
        "plane_weight": single((pick_a @ plane_weight)[:, None]),
    }


def split_two(value):
    high = value.astype(jnp.bfloat16)
    return high, (value - high.astype(jnp.float32)).astype(jnp.bfloat16)


def mul(left, right):
    return jnp.dot(left, right, preferred_element_type=jnp.float32)


def left_mul(matrix, value):
    high, low = split_two(value)
    return mul(matrix[...], jnp.concatenate([high, high, low], axis=0))


def left_place(matrix, value):
    high = value.astype(jnp.bfloat16)
    rest = value - high.astype(jnp.float32)
    middle, low = split_two(rest)
    return mul(matrix[...], jnp.concatenate([high, middle, low], axis=0))


def right_mul(value, high_ref, low_ref):
    high, low = split_two(value)
    return mul(high, high_ref[...]) + (mul(high, low_ref[...]) + mul(low, high_ref[...]))


def each_other(count, act):
    if count <= 8:
        for step in range(1, count):
            act(step)
    else:

        def body(step, carry):
            act(step)
            return carry

        lax.fori_loop(1, count, body, 0)


def stages_of(n_gx, n_gy):
    return ("xy",) if n_gx * n_gy <= DIRECT else ("x", "y")


def stage_size(stage, n_gx, n_gy):
    return {"x": n_gx, "y": n_gy, "xy": n_gx * n_gy}[stage]


def kernel(n_gx, n_gy, n_in, *refs):
    sources = refs[:n_in]
    out_x, out_r = refs[n_in : n_in + 2]
    loaded = refs[n_in + 2 : 2 * n_in + 2]
    load_sem, arrived, sending, own_rows, z_high, z_low, scale, first, field_w, halo_send, halo_recv = refs[
        2 * n_in + 2 : 2 * n_in + 13
    ]
    spec_in, spec_out, pick_place, plane, inner, win_h, win_l, back_h, back_l = refs[
        2 * n_in + 13 : 2 * n_in + 22
    ]
    lanes = refs[2 * n_in + 22 :]
    (
        rhs, pick_a_f, segments, factor,
        stiff, mass, spread, lines, lam_all, spec_in_f, window, back, spec_out_f,
        own_cols, before_cols, pick_place_f, plane_f, plane_weight, inner_f,
    ) = loaded
    loads = [
        pltpu.make_async_copy(source, target, load_sem.at[index])
        for index, (source, target) in enumerate(zip(sources, loaded))
    ]
    for load in loads:
        load.start()

    me_x, me_y = lax.axis_index("gx"), lax.axis_index("gy")
    points = rhs.shape[2]
    z_pad, s_pad = window.shape
    stages = stages_of(n_gx, n_gy)

    def beside(off_x, off_y):
        return (lax.rem(me_x + off_x + n_gx, n_gx), lax.rem(me_y + off_y + n_gy, n_gy))

    def each_offset(stage, act):
        if stage == "xy":
            for off_x in range(n_gx):
                for off_y in range(n_gy):
                    if off_x or off_y:
                        act(off_x, off_y)
        elif stage == "x":
            each_other(n_gx, lambda step: act(step, 0))
        else:
            each_other(n_gy, lambda step: act(0, step))

    barrier = pltpu.get_barrier_semaphore()

    def greet(off_x, off_y):
        pl.semaphore_signal(barrier, inc=1, device_id=beside(off_x, off_y), device_id_type=MESH)

    greeted = 0
    for stage in stages:
        each_offset(stage, greet)
        greeted += stage_size(stage, n_gx, n_gy) - 1
    if stages != ("xy",):
        for off_x, off_y, _, _ in SLOTS[4:]:
            greet(off_x, off_y)
        greeted += 4

    def halo_copy(turn, slot, start, rows):
        off_x, off_y, _, _ = SLOTS[slot]
        return pltpu.make_async_remote_copy(
            src_ref=sending.at[turn, pl.ds(start, rows)],
            dst_ref=arrived.at[turn, pl.ds(start, rows)],
            send_sem=halo_send.at[turn, slot],
            recv_sem=halo_recv.at[turn, slot],
            device_id=beside(-off_x, -off_y),
            device_id_type=MESH,
        )

    def halo_copies(turn):
        if turn == ROUNDS - 1:
            return [halo_copy(turn, slot, *LAST_PACKED[slot]) for _, slot in LAST]
        return [halo_copy(turn, slot, *PACKED[slot]) for slot in (4, 5, 6, 7, 0, 1, 2, 3)]

    tile_row = lax.broadcasted_iota(jnp.int32, (8, 128), 0)
    tile_lane = lax.broadcasted_iota(jnp.int32, (8, 128), 1)

    def halo_start(turn, rows):
        for slot, (_, _, start, count) in enumerate(SLOTS):
            at = PACKED[slot][0]
            if count == 8:
                part = rows[start : start + 8]
                sending[turn, pl.ds(at, 8)] = jnp.where(tile_row < 4, part[:, :128], part[:, 128:])
            else:
                sending[turn, pl.ds(at, 16)] = rows[start : start + 16, :128]
                sending[turn, pl.ds(at + 16, 8)] = rows[start : start + 8, 128:] + pltpu.roll(
                    rows[start + 8 : start + 16, 128:], 64, 1
                )
        for copy in halo_copies(turn):
            copy.start()
        own_rows[turn] = rows[:OWN]

    def left_half(tile):
        return jnp.where(tile_lane < 64, tile, 0.0)

    def corner_rows(turn, slot):
        tile = arrived[turn, pl.ds(PACKED[slot][0], 8)]
        upper = jnp.where(tile_row < 4, tile, 0.0)
        return jnp.concatenate([upper, jnp.where(tile_row < 4, 0.0, tile)], axis=1)

    def first_rows(turn, slot):
        at = PACKED[slot][0]
        tail = arrived[turn, pl.ds(at + 16, 8)]
        return jnp.concatenate([arrived[turn, pl.ds(at, 8)], left_half(tail)], axis=1)

    def second_rows(turn, slot):
        at = PACKED[slot][0]
        tail = pltpu.roll(arrived[turn, pl.ds(at + 16, 8)], 64, 1)
        return jnp.concatenate([arrived[turn, pl.ds(at + 8, 8)], left_half(tail)], axis=1)

    def halo_wait(turn):
        for copy in halo_copies(turn):
            copy.wait_recv()

    def stack(turn):
        parts = [own_rows[turn]]
        for slot in range(4):
            parts += [first_rows(turn, slot), second_rows(turn, slot)]
        parts += [corner_rows(turn, slot) for slot in range(4, 8)]
        return jnp.concatenate(parts, axis=0)

    def halo_drain(turn):
        for copy in halo_copies(turn):
            copy.wait_send()

    def slot_of(stage, off_x, off_y):
        at_x, at_y = beside(off_x, off_y)
        return {"x": at_x, "y": at_y, "xy": at_x * n_gy + at_y}[stage]

    class Lane:
        def __init__(self, stages, buffers):
            self.legs = [(stage,) + tuple(buffers[3 * at : 3 * at + 3]) for at, stage in enumerate(stages)]

        def copy(self, leg, off_x, off_y, slot):
            _, buf, send, recv = leg
            return pltpu.make_async_remote_copy(
                src_ref=buf.at[slot],
                dst_ref=buf.at[slot],
                send_sem=send.at[off_x * n_gy + off_y if leg[0] == "xy" else off_x + off_y],
                recv_sem=recv.at[off_x * n_gy + off_y if leg[0] == "xy" else off_x + off_y],
                device_id=beside(off_x, off_y),
                device_id_type=MESH,
            )

        def put(self, leg, value):
            mine = slot_of(leg[0], 0, 0)
            leg[1][mine] = value
            each_offset(leg[0], lambda x, y: self.copy(leg, x, y, mine).start())

        def take(self, leg):
            each_offset(leg[0], lambda x, y: self.copy(leg, x, y, slot_of(leg[0], -x, -y)).wait_recv())
            return jnp.sum(leg[1][...], axis=0)

        def start(self, value):
            self.put(self.legs[0], value)

        def middle(self):
            for before, after in zip(self.legs, self.legs[1:]):
                self.put(after, self.take(before))

        def finish(self):
            return self.take(self.legs[-1])

        def drain(self):
            for leg in self.legs:
                mine = slot_of(leg[0], 0, 0)
                each_offset(leg[0], lambda x, y: self.copy(leg, x, y, mine).wait_send())

    coarse = [Lane(("x", "y"), lanes[:6]), Lane(("x", "y"), lanes[6:12])]
    sums = Lane(stages, lanes[12:])

    point = lax.broadcasted_iota(jnp.int32, (OWN, z_pad), 0)
    at_x, at_y = point // 8, point % 8
    coarse_mask = (at_x >= 1) & (at_x <= 6) & (at_y >= 1) & (at_y <= 6)

    def coarse_start(turn, rows):
        line = jnp.sum(jnp.where(coarse_mask, rows, 0.0), axis=0, keepdims=True)
        held = jnp.sum(segments[...] * line, axis=1, keepdims=True)
        coarse[turn].start(jnp.sum(factor[...] * held, axis=0, keepdims=True))

    def coarse_finish(turn):
        total = coarse[turn].finish()
        values = jnp.sum(factor[...] * total, axis=1, keepdims=True)
        line = jnp.sum(segments[...] * values, axis=0, keepdims=True)
        return jnp.where(coarse_mask, line, 0.0)

    first[...] = jnp.zeros_like(first)
    for load in loads[:4]:
        load.wait()
    for row in range(7):
        first[pl.ds(8 * row, 7), pl.ds(0, points)] = rhs[row]
    right = first[...]
    rows = left_place(pick_a_f[...].astype(jnp.bfloat16), right)
    pl.semaphore_wait(barrier, greeted)
    halo_start(0, rows)
    coarse_start(0, right)

    for load in loads[4:13]:
        load.wait()

    def spread_out(coef, start, size):
        return jnp.dot(
            jnp.broadcast_to(coef[0], (8, coef.shape[2])), spread[:, start : start + size],
            precision=exact_mode, preferred_element_type=jnp.float32,
        )[0:1]

    def three_parts(source, target):
        high, low = split_two(source[...])
        column = lax.broadcasted_iota(jnp.int32, source.shape, 1)
        third = source.shape[1] // 3
        middle = (column >= third) & (column < 2 * third)
        target[...] = jnp.where(
            middle, low.astype(jnp.float32), high.astype(jnp.float32)
        ).astype(jnp.bfloat16)

    stiff_s, mass_s = spread_out(stiff, 0, s_pad), spread_out(mass, 0, s_pad)
    scale[...] = 1.0 / (stiff_s * lam_all[...] + (mass_s + lines[2:3, :s_pad]))
    three_parts(spec_in_f, spec_in)
    three_parts(spec_out_f, spec_out)
    win_h[...], win_l[...] = split_two(window[...])
    back_h[...], back_l[...] = split_two(back[...])

    def prepare_elements():
        for load in loads[13:]:
            load.wait()
        stiff_own, stiff_before = spread_out(stiff, s_pad, z_pad), spread_out(stiff, s_pad + z_pad, z_pad)
        mass_own, mass_before = spread_out(mass, s_pad, z_pad), spread_out(mass, s_pad + z_pad, z_pad)
        weight_own, weight_before = lines[0:1, :z_pad], lines[1:2, :z_pad]
        line_mass = mass_own * weight_own + mass_before * weight_before
        diagonal = lax.broadcasted_iota(jnp.int32, (z_pad, z_pad), 0) == lax.broadcasted_iota(
            jnp.int32, (z_pad, z_pad), 1
        )
        along = own_cols[...] * stiff_own + before_cols[...] * stiff_before
        z_high[...], z_low[...] = split_two(along + jnp.where(diagonal, line_mass, 0.0))
        three_parts(plane_f, plane)
        for source, target in ((pick_place_f, pick_place), (inner_f, inner)):
            target[...] = source[...].astype(jnp.bfloat16)
        return stiff_own * weight_own + stiff_before * weight_before

    def element(rows):
        wide = left_place(pick_place, rows)
        field = wide[:OWN]
        result = left_mul(plane, field * line_stiff) + plane_weight[...] * right_mul(
            wide, z_high, z_low
        )
        return field, result

    def precondition(turn):
        halo_wait(2 * turn)
        spectral = right_mul(left_mul(spec_in, stack(2 * turn)), win_h, win_l) * scale[...]
        coarse[turn].middle()
        result = left_mul(spec_out, right_mul(spectral, back_h, back_l))
        halo_start(2 * turn + 1, result)
        plate = coarse_finish(turn)
        own_rows[2 * turn + 1] = result[:OWN] + plate
        halo_drain(2 * turn)
        coarse[turn].drain()

    def dot_line(left, other):
        return jnp.sum(left * other, axis=0, keepdims=True)

    def gathered(turn, own):
        parts = [second_rows(turn, 0), second_rows(turn, 2), corner_rows(turn, 4)]
        return own + left_place(inner, jnp.concatenate(parts + [jnp.zeros_like(parts[0])], axis=0))

    owned = (at_x < 7) & (at_y < 7)

    precondition(0)
    line_stiff = prepare_elements()
    halo_wait(1)
    z_field, w_rows = element(stack(1))
    halo_start(2, w_rows)
    w_local = w_rows[:OWN]
    coarse_start(1, w_local)
    precondition(1)
    field_w[...] = gathered(2, w_local)
    halo_wait(3)
    v_field, av_rows = element(stack(3))
    halo_start(4, av_rows)
    av_local = av_rows[:OWN]
    partial = jnp.concatenate(
        [
            dot_line(right, jnp.where(owned, z_field, 0.0)),
            dot_line(z_field, w_local),
            dot_line(right, jnp.where(owned, v_field, 0.0)),
            dot_line(v_field, w_local),
            dot_line(v_field, av_local),
            dot_line(z_field, av_local),
            jnp.zeros((2, z_pad), jnp.float32),
        ],
        axis=0,
    )
    at_row = lax.broadcasted_iota(jnp.int32, (8, 128), 0)
    at_lane = lax.broadcasted_iota(jnp.int32, (8, 128), 1)
    packed = jnp.where(at_row == at_lane, jnp.sum(partial, axis=1, keepdims=True), 0.0)
    sums.start(jnp.sum(packed, axis=0, keepdims=True))
    sums.middle()
    for turn in (1, 3, 4):
        halo_drain(turn)
    sums.drain()
    halo_wait(4)
    av_field = gathered(4, av_local)
    w_field = field_w[...]
    totals = sums.finish()
    rz, zw, rv, vw, vav, zav = [totals[:, lane : lane + 1] for lane in range(6)]
    step_0 = rz / zw
    rho_1 = rz - step_0 * (rv + zw) + step_0 * step_0 * vw
    momentum = rho_1 / rz
    curve = (
        zw - step_0 * (vw + zav) + step_0 * step_0 * vav
        + momentum * ((zw - step_0 * vw) + (zw - step_0 * zav))
        + momentum * momentum * zw
    )
    step_1 = rho_1 / curve
    next_dir = (z_field - step_0 * v_field) + momentum * z_field
    next_image = (w_field - step_0 * av_field) + momentum * w_field
    final_x = step_0 * z_field + step_1 * next_dir
    final_r = (right - step_0 * w_field) - step_1 * next_image
    for row in range(7):
        out_x[row] = final_x[8 * row : 8 * row + 7, :points]
        out_r[row] = final_r[8 * row : 8 * row + 7, :points]


def move(from_x, from_r, to_x, to_r):
    to_x[...] = from_x[...]
    to_r[...] = from_r[...]


def local(n_gx, n_gy, right_side, stiff_coef, mass_coef, coarse_factor):
    elements = stiff_coef.shape[2]
    coarse_count, coarse_all = coarse_factor.shape
    tables = {name: jnp.asarray(table) for name, table in constants(elements, coarse_count).items()}
    tables.update(rhs=right_side, stiff=stiff_coef, mass=mass_coef, factor=coarse_factor)
    operands = [tables[name] for name in OPERANDS]
    z_pad = round_up(7 * elements, 128)
    s_pad = round_up(10 * elements, 128)
    dma = pltpu.SemaphoreType.DMA
    single = jnp.float32
    whole = pl.BlockSpec(memory_space=pltpu.VMEM)
    shape = jax.ShapeDtypeStruct(right_side.shape, single)
    lanes = []
    two = ("x", "y")
    for width, stages in ((coarse_all, two), (coarse_all, two), (128, stages_of(n_gx, n_gy))):
        for stage in stages:
            size = stage_size(stage, n_gx, n_gy)
            lanes += [pltpu.VMEM((size, 1, width), single), dma((size,)), dma((size,))]
    result = pl.pallas_call(
        functools.partial(kernel, n_gx, n_gy, len(operands)),
        out_shape=(shape, shape),
        in_specs=[pl.BlockSpec(memory_space=pltpu.HBM)] * len(operands),
        out_specs=(whole, whole),
        scratch_shapes=[pltpu.VMEM(operand.shape, operand.dtype) for operand in operands]
        + [
            dma((len(operands),)),
            pltpu.VMEM((ROUNDS, MESSAGE, 128), single),
            pltpu.VMEM((ROUNDS, MESSAGE, 128), single),
            pltpu.VMEM((ROUNDS, OWN, z_pad), single),
            pltpu.VMEM((z_pad, z_pad), jnp.bfloat16),
            pltpu.VMEM((z_pad, z_pad), jnp.bfloat16),
            pltpu.VMEM((SPEC, s_pad), single),
            pltpu.VMEM((OWN, z_pad), single),
            pltpu.VMEM((OWN, z_pad), single),
            dma((ROUNDS, 8)),
            dma((ROUNDS, 8)),
        ]
        + [
            pltpu.VMEM(tables[name].shape, jnp.bfloat16)
            for name in (
                "spec_in", "spec_out", "pick_place", "plane", "inner", "window", "window", "back", "back",
            )
        ]
        + lanes,
        compiler_params=pltpu.CompilerParams(
            collective_id=0, has_side_effects=True, vmem_limit_bytes=60 * 1024 * 1024
        ),
    )(*operands)
    return pl.pallas_call(
        move,
        out_shape=(shape, shape),
        in_specs=[whole] * 2,
        out_specs=(whole, whole),
        compiler_params=pltpu.CompilerParams(vmem_limit_bytes=60 * 1024 * 1024),
    )(*result)


def solution(mesh):
    placed = (P("gx", "gy", None), P("gx", "gy", None), P("gx", "gy", None), P(("gx", "gy"), None))
    return jax.shard_map(
        functools.partial(local, mesh.shape["gx"], mesh.shape["gy"]),
        mesh=mesh,
        in_specs=placed,
        out_specs=(P("gx", "gy", None), P("gx", "gy", None)),
        check_vma=False,
    )
```

```python
import functools
import math

import jax
import jax.numpy as jnp
import numpy as np
from jax import lax
from jax.experimental import pallas as pl
from jax.experimental.pallas import tpu as pltpu
from jax.sharding import PartitionSpec as P

MESH = pl.DeviceIdType.MESH
exact_mode = lax.Precision.HIGHEST
ROUNDS = 5

OWN = 64
SLOTS = (
    (-1, 0, 64, 16),
    (1, 0, 80, 16),
    (0, -1, 96, 16),
    (0, 1, 112, 16),
    (-1, -1, 128, 8),
    (-1, 1, 136, 8),
    (1, -1, 144, 8),
    (1, 1, 152, 8),
)
STACK = 160
SPEC = 112
PACKED = ((0, 24), (24, 24), (48, 24), (72, 24), (96, 8), (104, 8), (112, 8), (120, 8))
MESSAGE = 128
LAST = ((72, 0), (104, 2), (128, 4))
LAST_PACKED = {0: (8, 16), 2: (56, 16), 4: (96, 8)}
OPERANDS = (
    "rhs", "pick_a", "segments", "factor",
    "stiff", "mass", "spread", "lines", "lam_all", "spec_in", "win_h", "win_l", "back_h", "back_l", "spec_out",
    "own_cols", "before_cols", "pick_place", "plane", "plane_weight", "inner",
)
STAGES = ("x", "y")


def legendre_pair(position, degree):
    p_prev = 1.0
    p_now = position
    for order in range(2, degree + 1):
        p_next = ((2 * order - 1) * position * p_now - (order - 1) * p_prev) / order
        p_prev = p_now
        p_now = p_next
    return (p_now, p_prev)


def jacobi_eigen(matrix):
    size_n = matrix.shape[0]
    current = np.array(matrix)
    vectors = np.eye(size_n)
    for sweep in range(20):
        for row_p in range(size_n - 1):
            for row_q in range(row_p + 1, size_n):
                off_value = current[row_p, row_q]
                if abs(off_value) > 1e-300:
                    theta = (current[row_q, row_q] - current[row_p, row_p]) / (2.0 * off_value)
                    sign_t = 1.0 if theta >= 0.0 else -1.0
                    tangent = sign_t / (abs(theta) + math.sqrt(theta * theta + 1.0))
                    cosine = 1.0 / math.sqrt(tangent * tangent + 1.0)
                    sine = tangent * cosine
                    rotation = np.eye(size_n)
                    rotation[row_p, row_p] = cosine
                    rotation[row_q, row_q] = cosine
                    rotation[row_p, row_q] = sine
                    rotation[row_q, row_p] = -sine
                    current = rotation.T @ current @ rotation
                    vectors = vectors @ rotation
    return (np.array([current[idx, idx] for idx in range(size_n)]), vectors)


def gll_tables():
    degree = 7
    guesses = [
        -0.8717401485096066,
        -0.5917001814331423,
        -0.2092992179024789,
        0.2092992179024789,
        0.5917001814331423,
        0.8717401485096066,
    ]
    interior = []
    for guess in guesses:
        position = guess
        for newton in range(30):
            p_now, p_prev = legendre_pair(position, degree)
            first = degree * (position * p_now - p_prev) / (position * position - 1.0)
            second = (2.0 * position * first - degree * (degree + 1) * p_now) / (
                1.0 - position * position
            )
            position = position - first / second
        interior.append(position)
    points = np.array([-1.0] + interior + [1.0])
    values = np.array([legendre_pair(float(pt), degree)[0] for pt in points])
    weights = 2.0 / (degree * (degree + 1) * values**2)
    deriv_mat = np.zeros((8, 8))
    for left_idx in range(8):
        for right_idx in range(8):
            if left_idx != right_idx:
                deriv_mat[left_idx, right_idx] = values[left_idx] / (
                    values[right_idx] * (points[left_idx] - points[right_idx])
                )
    deriv_mat[0, 0] = -degree * (degree + 1) / 4.0
    deriv_mat[7, 7] = degree * (degree + 1) / 4.0
    stiffness = deriv_mat.T @ (weights[:, None] * deriv_mat)
    ext_stiff = np.zeros((10, 10))
    ext_stiff[1:9, 1:9] += stiffness
    ext_stiff[0:2, 0:2] += stiffness[6:8, 6:8]
    ext_stiff[8:10, 8:10] += stiffness[0:2, 0:2]
    ext_mass = np.zeros(10)
    ext_mass[1:9] += weights
    ext_mass[0:2] += weights[6:8]
    ext_mass[8:10] += weights[0:2]
    inv_root = 1.0 / np.sqrt(ext_mass)
    eigen_vals, eigen_vecs = jacobi_eigen(inv_root[:, None] * ext_stiff * inv_root[None, :])
    eigen_basis = inv_root[:, None] * eigen_vecs
    return stiffness, weights, eigen_basis, eigen_vals


def round_up(count, unit):
    return -(-count // unit) * unit


def stack_map(taken, placed, size_from, size_to):
    pick = np.zeros((STACK, size_from * size_from))
    place = np.zeros((size_to * size_to, STACK))
    for off_x, off_y, start, _ in ((0, 0, 0, OWN),) + SLOTS:
        row = start
        pairs_x = list(zip(taken[off_x], placed[off_x]))
        pairs_y = list(zip(taken[off_y], placed[off_y]))
        pairs = [(one, two) for one in pairs_x for two in pairs_y]
        if off_x == 0 and off_y != 0:
            pairs = [(one, two) for two in pairs_y for one in pairs_x]
        if off_x != 0 and off_y != 0:
            pairs = pairs + pairs
        for (from_x, to_x), (from_y, to_y) in pairs:
            pick[row, from_x * size_from + from_y] = 1.0
            place[to_x * size_to + to_y, row] = 1.0
            row += 1
    return pick, place


def halves(matrix):
    exact = np.asarray(matrix, np.float32)
    high = exact.astype(jnp.bfloat16)
    low = (exact - high.astype(np.float32)).astype(jnp.bfloat16)
    return high, low


def left_split(matrix):
    high, low = halves(matrix)
    return np.concatenate([high, low, high], axis=1)


def left_exact(matrix):
    return np.concatenate([np.asarray(matrix).astype(jnp.bfloat16)] * 3, axis=1)


def constants(elements, coarse_count):
    stiffness, weights, basis, lam = gll_tables()
    stiffness = np.asarray(stiffness, np.float32).astype(np.float64)
    weights = np.asarray(weights, np.float32).astype(np.float64)
    basis = np.asarray(basis, np.float32).astype(np.float64)
    lam = np.asarray(lam, np.float32).astype(np.float64)
    points = 7 * elements
    z_pad = round_up(points, 128)
    s_pad = round_up(10 * elements, 128)
    every = list(range(8))
    pick_a, place_a = stack_map(
        {-1: [6, 7], 0: every, 1: [0, 1]}, {-1: [0, 1], 0: list(range(1, 9)), 1: [8, 9]}, 8, 10
    )
    pick_s, place_s = stack_map(
        {-1: [8, 9], 0: list(range(1, 9)), 1: [0, 1]}, {-1: [0, 1], 0: every, 1: [6, 7]}, 10, 8
    )
    basis_two = np.kron(basis, basis)
    spectral_in = np.zeros((SPEC, STACK))
    spectral_in[:100] = basis_two.T @ place_a
    spectral_out = np.zeros((STACK, SPEC))
    spectral_out[:, :100] = pick_s @ basis_two
    plane = np.kron(stiffness, np.diag(weights)) + np.kron(np.diag(weights), stiffness)
    plane_weight = np.kron(weights, weights)
    window = np.zeros((z_pad, s_pad))
    own_cols = np.zeros((z_pad, z_pad))
    before_cols = np.zeros((z_pad, z_pad))
    spread = np.zeros((elements, s_pad + 2 * z_pad))
    lines = np.zeros((8, max(z_pad, s_pad)))
    lines[2, 10 * elements :] = 1.0
    for elem in range(elements):
        prior = (elem - 1) % elements
        for col in range(10):
            spread[elem, col * elements + elem] = 1.0
            for row in range(10):
                window[(7 * elem - 1 + row) % points, col * elements + elem] += basis[row, col]
        for step in range(7):
            spread[elem, s_pad + 7 * elem + step] = 1.0
            spread[prior, s_pad + z_pad + 7 * elem + step] = 1.0
            lines[0, 7 * elem + step] = weights[step]
            for row in range(8):
                own_cols[(7 * elem + row) % points, 7 * elem + step] += stiffness[row, step]
        lines[1, 7 * elem] = weights[7]
        for row in range(8):
            before_cols[(7 * prior + row) % points, 7 * elem] += stiffness[row, 7]
    lam_all = np.zeros((SPEC, s_pad))
    lam_two = (lam[:, None] + lam[None, :]).reshape(-1)
    lam_all[:100, : 10 * elements] = lam_two[:, None] + np.repeat(lam, elements)[None, :]
    segments = np.zeros((coarse_count, z_pad))
    for row in range(coarse_count):
        length = points // coarse_count
        segments[row, row * length : (row + 1) * length] = 1.0
    inner = place_a.reshape(10, 10, STACK)[1:9, 1:9].reshape(OWN, STACK)
    inner = np.concatenate([inner[:, start : start + 8] for start, _ in LAST] + [np.zeros((OWN, 8))], axis=1)
    window_high, window_low = halves(window)
    back_high, back_low = halves(window.T)
    single = lambda value: np.asarray(value, np.float32)
    return {
        "pick_a": left_exact(pick_a),
        "spec_in": left_split(spectral_in),
        "spec_out": left_split(spectral_out),
        "pick_place": left_exact(pick_a @ place_s),
        "plane": left_split(pick_a @ plane),
        "inner": left_exact(inner),
        "win_h": window_high,
        "win_l": window_low,
        "back_h": back_high,
        "back_l": back_low,
        "own_cols": single(own_cols),
        "before_cols": single(before_cols),
        "lam_all": single(lam_all),
        "spread": single(spread),
        "lines": single(lines),
        "segments": single(segments),
        "plane_weight": single((pick_a @ plane_weight)[:, None]),
    }


def split_two(value):
    high = value.astype(jnp.bfloat16)
    return high, (value - high.astype(jnp.float32)).astype(jnp.bfloat16)


def mul(left, right):
    return jnp.dot(left, right, preferred_element_type=jnp.float32)


def left_mul(matrix, value):
    high, low = split_two(value)
    return mul(matrix[...], jnp.concatenate([high, high, low], axis=0))


def left_place(matrix, value):
    high = value.astype(jnp.bfloat16)
    rest = value - high.astype(jnp.float32)
    middle, low = split_two(rest)
    return mul(matrix[...], jnp.concatenate([high, middle, low], axis=0))


def right_mul(value, high_ref, low_ref):
    high, low = split_two(value)
    return mul(high, high_ref[...]) + (mul(high, low_ref[...]) + mul(low, high_ref[...]))


def each_other(count, act):
    if count <= 8:
        for step in range(1, count):
            act(step)
    else:

        def body(step, carry):
            act(step)
            return carry

        lax.fori_loop(1, count, body, 0)


def stage_size(stage, n_gx, n_gy):
    return {"x": n_gx, "y": n_gy}[stage]


def kernel(n_gx, n_gy, n_in, *refs):
    sources = refs[:n_in]
    out_x, out_r = refs[n_in : n_in + 2]
    loaded = refs[n_in + 2 : 2 * n_in + 2]
    load_sem, arrived, sending, own_rows, z_high, z_low, scale, first, field_w, halo_send, halo_recv = refs[
        2 * n_in + 2 : 2 * n_in + 13
    ]
    lanes = refs[2 * n_in + 13 :]
    (
        rhs, pick_a, segments, factor,
        stiff, mass, spread, lines, lam_all, spec_in, win_h, win_l, back_h, back_l, spec_out,
        own_cols, before_cols, pick_place, plane, plane_weight, inner,
    ) = loaded
    loads = [
        pltpu.make_async_copy(source, target, load_sem.at[index])
        for index, (source, target) in enumerate(zip(sources, loaded))
    ]
    for load in loads:
        load.start()

    me_x, me_y = lax.axis_index("gx"), lax.axis_index("gy")
    points = rhs.shape[2]
    z_pad, s_pad = win_h.shape

    def beside(off_x, off_y):
        return (lax.rem(me_x + off_x + n_gx, n_gx), lax.rem(me_y + off_y + n_gy, n_gy))

    def each_offset(stage, act):
        if stage == "x":
            each_other(n_gx, lambda step: act(step, 0))
        else:
            each_other(n_gy, lambda step: act(0, step))

    barrier = pltpu.get_barrier_semaphore()

    def greet(off_x, off_y):
        pl.semaphore_signal(barrier, inc=1, device_id=beside(off_x, off_y), device_id_type=MESH)

    greeted = 0
    for stage in STAGES:
        each_offset(stage, greet)
        greeted += stage_size(stage, n_gx, n_gy) - 1
    for off_x, off_y, _, _ in SLOTS[4:]:
        greet(off_x, off_y)
        greeted += 1

    def halo_copy(turn, slot, start, rows):
        off_x, off_y, _, _ = SLOTS[slot]
        return pltpu.make_async_remote_copy(
            src_ref=sending.at[turn, pl.ds(start, rows)],
            dst_ref=arrived.at[turn, pl.ds(start, rows)],
            send_sem=halo_send.at[turn, slot],
            recv_sem=halo_recv.at[turn, slot],
            device_id=beside(-off_x, -off_y),
            device_id_type=MESH,
        )

    def halo_copies(turn):
        if turn == ROUNDS - 1:
            return [halo_copy(turn, slot, *LAST_PACKED[slot]) for _, slot in LAST]
        return [halo_copy(turn, slot, *PACKED[slot]) for slot in (4, 5, 6, 7, 0, 1, 2, 3)]

    tile_row = lax.broadcasted_iota(jnp.int32, (8, 128), 0)
    tile_lane = lax.broadcasted_iota(jnp.int32, (8, 128), 1)

    def halo_start(turn, rows):
        for slot, (_, _, start, count) in enumerate(SLOTS):
            at = PACKED[slot][0]
            if count == 8:
                part = rows[start : start + 8]
                sending[turn, pl.ds(at, 8)] = jnp.where(tile_row < 4, part[:, :128], part[:, 128:])
            else:
                sending[turn, pl.ds(at, 16)] = rows[start : start + 16, :128]
                sending[turn, pl.ds(at + 16, 8)] = rows[start : start + 8, 128:] + pltpu.roll(
                    rows[start + 8 : start + 16, 128:], 64, 1
                )
        for copy in halo_copies(turn):
            copy.start()
        own_rows[turn] = rows[:OWN]

    def left_half(tile):
        return jnp.where(tile_lane < 64, tile, 0.0)

    def corner_rows(turn, slot):
        tile = arrived[turn, pl.ds(PACKED[slot][0], 8)]
        upper = jnp.where(tile_row < 4, tile, 0.0)
        return jnp.concatenate([upper, jnp.where(tile_row < 4, 0.0, tile)], axis=1)

    def first_rows(turn, slot):
        at = PACKED[slot][0]
        tail = arrived[turn, pl.ds(at + 16, 8)]
        return jnp.concatenate([arrived[turn, pl.ds(at, 8)], left_half(tail)], axis=1)

    def second_rows(turn, slot):
        at = PACKED[slot][0]
        tail = pltpu.roll(arrived[turn, pl.ds(at + 16, 8)], 64, 1)
        return jnp.concatenate([arrived[turn, pl.ds(at + 8, 8)], left_half(tail)], axis=1)

    def halo_wait(turn):
        for copy in halo_copies(turn):
            copy.wait_recv()

    def stack(turn):
        parts = [own_rows[turn]]
        for slot in range(4):
            parts += [first_rows(turn, slot), second_rows(turn, slot)]
        parts += [corner_rows(turn, slot) for slot in range(4, 8)]
        return jnp.concatenate(parts, axis=0)

    def halo_drain(turn):
        for copy in halo_copies(turn):
            copy.wait_send()

    def slot_of(stage, off_x, off_y):
        at_x, at_y = beside(off_x, off_y)
        return {"x": at_x, "y": at_y}[stage]

    class Lane:
        def __init__(self, buffers):
            self.legs = [(stage,) + tuple(buffers[3 * at : 3 * at + 3]) for at, stage in enumerate(STAGES)]

        def copy(self, leg, off_x, off_y, slot):
            _, buf, send, recv = leg
            return pltpu.make_async_remote_copy(
                src_ref=buf.at[slot],
                dst_ref=buf.at[slot],
                send_sem=send.at[off_x + off_y],
                recv_sem=recv.at[off_x + off_y],
                device_id=beside(off_x, off_y),
                device_id_type=MESH,
            )

        def put(self, leg, value):
            mine = slot_of(leg[0], 0, 0)
            leg[1][mine] = value
            each_offset(leg[0], lambda x, y: self.copy(leg, x, y, mine).start())

        def take(self, leg):
            each_offset(leg[0], lambda x, y: self.copy(leg, x, y, slot_of(leg[0], -x, -y)).wait_recv())
            return jnp.sum(leg[1][...], axis=0)

        def start(self, value):
            self.put(self.legs[0], value)

        def middle(self):
            for before, after in zip(self.legs, self.legs[1:]):
                self.put(after, self.take(before))

        def finish(self):
            return self.take(self.legs[-1])

        def drain(self):
            for leg in self.legs:
                mine = slot_of(leg[0], 0, 0)
                each_offset(leg[0], lambda x, y: self.copy(leg, x, y, mine).wait_send())

    coarse = [Lane(lanes[:6]), Lane(lanes[6:12])]
    sums = Lane(lanes[12:])

    point = lax.broadcasted_iota(jnp.int32, (OWN, z_pad), 0)
    at_x, at_y = point // 8, point % 8
    coarse_mask = (at_x >= 1) & (at_x <= 6) & (at_y >= 1) & (at_y <= 6)

    def coarse_start(turn, rows):
        line = jnp.sum(jnp.where(coarse_mask, rows, 0.0), axis=0, keepdims=True)
        held = jnp.sum(segments[...] * line, axis=1, keepdims=True)
        coarse[turn].start(jnp.sum(factor[...] * held, axis=0, keepdims=True))

    def coarse_finish(turn):
        total = coarse[turn].finish()
        values = jnp.sum(factor[...] * total, axis=1, keepdims=True)
        line = jnp.sum(segments[...] * values, axis=0, keepdims=True)
        return jnp.where(coarse_mask, line, 0.0)

    first[...] = jnp.zeros_like(first)
    for load in loads[:4]:
        load.wait()
    for row in range(7):
        first[pl.ds(8 * row, 7), pl.ds(0, points)] = rhs[row]
    right = first[...]
    rows = left_place(pick_a, right)
    pl.semaphore_wait(barrier, greeted)
    halo_start(0, rows)
    coarse_start(0, right)

    for load in loads[4:15]:
        load.wait()

    def spread_out(coef, start, size):
        return jnp.dot(
            jnp.broadcast_to(coef[0], (8, coef.shape[2])), spread[:, start : start + size],
            precision=exact_mode, preferred_element_type=jnp.float32,
        )[0:1]

    stiff_s, mass_s = spread_out(stiff, 0, s_pad), spread_out(mass, 0, s_pad)
    scale[...] = 1.0 / (stiff_s * lam_all[...] + (mass_s + lines[2:3, :s_pad]))

    def prepare_elements():
        for load in loads[15:]:
            load.wait()
        stiff_own, stiff_before = spread_out(stiff, s_pad, z_pad), spread_out(stiff, s_pad + z_pad, z_pad)
        mass_own, mass_before = spread_out(mass, s_pad, z_pad), spread_out(mass, s_pad + z_pad, z_pad)
        weight_own, weight_before = lines[0:1, :z_pad], lines[1:2, :z_pad]
        line_mass = mass_own * weight_own + mass_before * weight_before
        diagonal = lax.broadcasted_iota(jnp.int32, (z_pad, z_pad), 0) == lax.broadcasted_iota(
            jnp.int32, (z_pad, z_pad), 1
        )
        along = own_cols[...] * stiff_own + before_cols[...] * stiff_before
        z_high[...], z_low[...] = split_two(along + jnp.where(diagonal, line_mass, 0.0))
        return stiff_own * weight_own + stiff_before * weight_before

    def element(rows):
        wide = left_place(pick_place, rows)
        field = wide[:OWN]
        result = left_mul(plane, field * line_stiff) + plane_weight[...] * right_mul(
            wide, z_high, z_low
        )
        return field, result

    def precondition(turn):
        halo_wait(2 * turn)
        spectral = right_mul(left_mul(spec_in, stack(2 * turn)), win_h, win_l) * scale[...]
        coarse[turn].middle()
        result = left_mul(spec_out, right_mul(spectral, back_h, back_l))
        halo_start(2 * turn + 1, result)
        plate = coarse_finish(turn)
        own_rows[2 * turn + 1] = result[:OWN] + plate
        halo_drain(2 * turn)
        coarse[turn].drain()

    def dot_line(left, other):
        return jnp.sum(left * other, axis=0, keepdims=True)

    def gathered(turn, own):
        parts = [second_rows(turn, 0), second_rows(turn, 2), corner_rows(turn, 4)]
        return own + left_place(inner, jnp.concatenate(parts + [jnp.zeros_like(parts[0])], axis=0))

    owned = (at_x < 7) & (at_y < 7)

    precondition(0)
    line_stiff = prepare_elements()
    halo_wait(1)
    z_field, w_rows = element(stack(1))
    halo_start(2, w_rows)
    w_local = w_rows[:OWN]
    coarse_start(1, w_local)
    precondition(1)
    field_w[...] = gathered(2, w_local)
    halo_wait(3)
    v_field, av_rows = element(stack(3))
    halo_start(4, av_rows)
    av_local = av_rows[:OWN]
    partial = jnp.concatenate(
        [
            dot_line(right, jnp.where(owned, z_field, 0.0)),
            dot_line(z_field, w_local),
            dot_line(right, jnp.where(owned, v_field, 0.0)),
            dot_line(v_field, w_local),
            dot_line(v_field, av_local),
            dot_line(z_field, av_local),
            jnp.zeros((2, z_pad), jnp.float32),
        ],
        axis=0,
    )
    at_row = lax.broadcasted_iota(jnp.int32, (8, 128), 0)
    at_lane = lax.broadcasted_iota(jnp.int32, (8, 128), 1)
    packed = jnp.where(at_row == at_lane, jnp.sum(partial, axis=1, keepdims=True), 0.0)
    sums.start(jnp.sum(packed, axis=0, keepdims=True))
    sums.middle()
    for turn in (1, 3, 4):
        halo_drain(turn)
    sums.drain()
    halo_wait(4)
    av_field = gathered(4, av_local)
    w_field = field_w[...]
    totals = sums.finish()
    rz, zw, rv, vw, vav, zav = [totals[:, lane : lane + 1] for lane in range(6)]
    step_0 = rz / zw
    rho_1 = rz - step_0 * (rv + zw) + step_0 * step_0 * vw
    momentum = rho_1 / rz
    curve = (
        zw - step_0 * (vw + zav) + step_0 * step_0 * vav
        + momentum * ((zw - step_0 * vw) + (zw - step_0 * zav))
        + momentum * momentum * zw
    )
    step_1 = rho_1 / curve
    next_dir = (z_field - step_0 * v_field) + momentum * z_field
    next_image = (w_field - step_0 * av_field) + momentum * w_field
    final_x = step_0 * z_field + step_1 * next_dir
    final_r = (right - step_0 * w_field) - step_1 * next_image
    for row in range(7):
        out_x[row] = final_x[8 * row : 8 * row + 7, :points]
        out_r[row] = final_r[8 * row : 8 * row + 7, :points]


def move(from_x, from_r, to_x, to_r):
    to_x[...] = from_x[...]
    to_r[...] = from_r[...]


def local(n_gx, n_gy, right_side, stiff_coef, mass_coef, coarse_factor):
    elements = stiff_coef.shape[2]
    coarse_count, coarse_all = coarse_factor.shape
    tables = {name: jnp.asarray(table) for name, table in constants(elements, coarse_count).items()}
    tables.update(rhs=right_side, stiff=stiff_coef, mass=mass_coef, factor=coarse_factor)
    operands = [tables[name] for name in OPERANDS]
    z_pad = round_up(7 * elements, 128)
    s_pad = round_up(10 * elements, 128)
    dma = pltpu.SemaphoreType.DMA
    single = jnp.float32
    whole = pl.BlockSpec(memory_space=pltpu.VMEM)
    shape = jax.ShapeDtypeStruct(right_side.shape, single)
    lanes = []
    for width in (coarse_all, coarse_all, 128):
        for stage in STAGES:
            size = stage_size(stage, n_gx, n_gy)
            lanes += [pltpu.VMEM((size, 1, width), single), dma((size,)), dma((size,))]
    result = pl.pallas_call(
        functools.partial(kernel, n_gx, n_gy, len(operands)),
        out_shape=(shape, shape),
        in_specs=[pl.BlockSpec(memory_space=pltpu.HBM)] * len(operands),
        out_specs=(whole, whole),
        scratch_shapes=[pltpu.VMEM(operand.shape, operand.dtype) for operand in operands]
        + [
            dma((len(operands),)),
            pltpu.VMEM((ROUNDS, MESSAGE, 128), single),
            pltpu.VMEM((ROUNDS, MESSAGE, 128), single),
            pltpu.VMEM((ROUNDS, OWN, z_pad), single),
            pltpu.VMEM((z_pad, z_pad), jnp.bfloat16),
            pltpu.VMEM((z_pad, z_pad), jnp.bfloat16),
            pltpu.VMEM((SPEC, s_pad), single),
            pltpu.VMEM((OWN, z_pad), single),
            pltpu.VMEM((OWN, z_pad), single),
            dma((ROUNDS, 8)),
            dma((ROUNDS, 8)),
        ]
        + lanes,
        compiler_params=pltpu.CompilerParams(
            collective_id=0, has_side_effects=True, vmem_limit_bytes=60 * 1024 * 1024
        ),
    )(*operands)
    return pl.pallas_call(
        move,
        out_shape=(shape, shape),
        in_specs=[whole] * 2,
        out_specs=(whole, whole),
        compiler_params=pltpu.CompilerParams(vmem_limit_bytes=60 * 1024 * 1024),
    )(*result)


def solution(mesh):
    placed = (P("gx", "gy", None), P("gx", "gy", None), P("gx", "gy", None), P(("gx", "gy"), None))
    return jax.shard_map(
        functools.partial(local, mesh.shape["gx"], mesh.shape["gy"]),
        mesh=mesh,
        in_specs=placed,
        out_specs=(P("gx", "gy", None), P("gx", "gy", None)),
        check_vma=False,
    )
```

```python
import functools
import math

import jax
import jax.numpy as jnp
import numpy as np
from jax import lax
from jax.experimental import pallas as pl
from jax.experimental.pallas import tpu as pltpu
from jax.sharding import PartitionSpec as P

MESH = pl.DeviceIdType.MESH
exact_mode = lax.Precision.HIGHEST
ROUNDS = 5

OWN = 64
SLOTS = (
    (-1, 0, 64, 16),
    (1, 0, 80, 16),
    (0, -1, 96, 16),
    (0, 1, 112, 16),
    (-1, -1, 128, 8),
    (-1, 1, 136, 8),
    (1, -1, 144, 8),
    (1, 1, 152, 8),
)
STACK = 160
SPEC = 112
PACKED = ((0, 24), (24, 24), (48, 24), (72, 24), (96, 8), (104, 8), (112, 8), (120, 8))
MESSAGE = 128
LAST = ((72, 0), (104, 2), (128, 4))
LAST_PACKED = {0: (8, 16), 2: (56, 16), 4: (96, 8)}
OPERANDS = (
    "rhs", "pick_a", "segments", "factor",
    "stiff", "mass", "spread", "lines", "lam_all", "spec_own", "spec_in", "win_h", "win_l", "back_h", "back_l", "spec_out",
    "own_cols", "before_cols", "pick_own", "pick_place", "plane", "plane_weight", "inner",
)
STAGES = ("x", "y")
DIRECT = 64


def legendre_pair(position, degree):
    p_prev = 1.0
    p_now = position
    for order in range(2, degree + 1):
        p_next = ((2 * order - 1) * position * p_now - (order - 1) * p_prev) / order
        p_prev = p_now
        p_now = p_next
    return (p_now, p_prev)


def jacobi_eigen(matrix):
    size_n = matrix.shape[0]
    current = np.array(matrix)
    vectors = np.eye(size_n)
    for sweep in range(20):
        for row_p in range(size_n - 1):
            for row_q in range(row_p + 1, size_n):
                off_value = current[row_p, row_q]
                if abs(off_value) > 1e-300:
                    theta = (current[row_q, row_q] - current[row_p, row_p]) / (2.0 * off_value)
                    sign_t = 1.0 if theta >= 0.0 else -1.0
                    tangent = sign_t / (abs(theta) + math.sqrt(theta * theta + 1.0))
                    cosine = 1.0 / math.sqrt(tangent * tangent + 1.0)
                    sine = tangent * cosine
                    rotation = np.eye(size_n)
                    rotation[row_p, row_p] = cosine
                    rotation[row_q, row_q] = cosine
                    rotation[row_p, row_q] = sine
                    rotation[row_q, row_p] = -sine
                    current = rotation.T @ current @ rotation
                    vectors = vectors @ rotation
    return (np.array([current[idx, idx] for idx in range(size_n)]), vectors)


def gll_tables():
    degree = 7
    guesses = [
        -0.8717401485096066,
        -0.5917001814331423,
        -0.2092992179024789,
        0.2092992179024789,
        0.5917001814331423,
        0.8717401485096066,
    ]
    interior = []
    for guess in guesses:
        position = guess
        for newton in range(30):
            p_now, p_prev = legendre_pair(position, degree)
            first = degree * (position * p_now - p_prev) / (position * position - 1.0)
            second = (2.0 * position * first - degree * (degree + 1) * p_now) / (
                1.0 - position * position
            )
            position = position - first / second
        interior.append(position)
    points = np.array([-1.0] + interior + [1.0])
    values = np.array([legendre_pair(float(pt), degree)[0] for pt in points])
    weights = 2.0 / (degree * (degree + 1) * values**2)
    deriv_mat = np.zeros((8, 8))
    for left_idx in range(8):
        for right_idx in range(8):
            if left_idx != right_idx:
                deriv_mat[left_idx, right_idx] = values[left_idx] / (
                    values[right_idx] * (points[left_idx] - points[right_idx])
                )
    deriv_mat[0, 0] = -degree * (degree + 1) / 4.0
    deriv_mat[7, 7] = degree * (degree + 1) / 4.0
    stiffness = deriv_mat.T @ (weights[:, None] * deriv_mat)
    ext_stiff = np.zeros((10, 10))
    ext_stiff[1:9, 1:9] += stiffness
    ext_stiff[0:2, 0:2] += stiffness[6:8, 6:8]
    ext_stiff[8:10, 8:10] += stiffness[0:2, 0:2]
    ext_mass = np.zeros(10)
    ext_mass[1:9] += weights
    ext_mass[0:2] += weights[6:8]
    ext_mass[8:10] += weights[0:2]
    inv_root = 1.0 / np.sqrt(ext_mass)
    eigen_vals, eigen_vecs = jacobi_eigen(inv_root[:, None] * ext_stiff * inv_root[None, :])
    eigen_basis = inv_root[:, None] * eigen_vecs
    return stiffness, weights, eigen_basis, eigen_vals


def round_up(count, unit):
    return -(-count // unit) * unit


def stack_map(taken, placed, size_from, size_to):
    pick = np.zeros((STACK, size_from * size_from))
    place = np.zeros((size_to * size_to, STACK))
    for off_x, off_y, start, _ in ((0, 0, 0, OWN),) + SLOTS:
        row = start
        pairs_x = list(zip(taken[off_x], placed[off_x]))
        pairs_y = list(zip(taken[off_y], placed[off_y]))
        pairs = [(one, two) for one in pairs_x for two in pairs_y]
        if off_x == 0 and off_y != 0:
            pairs = [(one, two) for two in pairs_y for one in pairs_x]
        if off_x != 0 and off_y != 0:
            pairs = pairs + pairs
        for (from_x, to_x), (from_y, to_y) in pairs:
            pick[row, from_x * size_from + from_y] = 1.0
            place[to_x * size_to + to_y, row] = 1.0
            row += 1
    return pick, place


def halves(matrix):
    exact = np.asarray(matrix, np.float32)
    high = exact.astype(jnp.bfloat16)
    low = (exact - high.astype(np.float32)).astype(jnp.bfloat16)
    return high, low


def left_split(matrix):
    high, low = halves(matrix)
    return np.concatenate([high, low, high], axis=1)


def left_exact(matrix):
    return np.concatenate([np.asarray(matrix).astype(jnp.bfloat16)] * 3, axis=1)


def constants(elements, coarse_count):
    stiffness, weights, basis, lam = gll_tables()
    stiffness = np.asarray(stiffness, np.float32).astype(np.float64)
    weights = np.asarray(weights, np.float32).astype(np.float64)
    basis = np.asarray(basis, np.float32).astype(np.float64)
    lam = np.asarray(lam, np.float32).astype(np.float64)
    points = 7 * elements
    z_pad = round_up(points, 128)
    s_pad = round_up(10 * elements, 128)
    every = list(range(8))
    pick_a, place_a = stack_map(
        {-1: [6, 7], 0: every, 1: [0, 1]}, {-1: [0, 1], 0: list(range(1, 9)), 1: [8, 9]}, 8, 10
    )
    pick_s, place_s = stack_map(
        {-1: [8, 9], 0: list(range(1, 9)), 1: [0, 1]}, {-1: [0, 1], 0: every, 1: [6, 7]}, 10, 8
    )
    basis_two = np.kron(basis, basis)
    spectral_in = np.zeros((SPEC, STACK))
    spectral_in[:100] = basis_two.T @ place_a
    spectral_out = np.zeros((STACK, SPEC))
    spectral_out[:, :100] = pick_s @ basis_two
    plane = np.kron(stiffness, np.diag(weights)) + np.kron(np.diag(weights), stiffness)
    plane_weight = np.kron(weights, weights)
    window = np.zeros((z_pad, s_pad))
    own_cols = np.zeros((z_pad, z_pad))
    before_cols = np.zeros((z_pad, z_pad))
    spread = np.zeros((elements, s_pad + 2 * z_pad))
    lines = np.zeros((8, max(z_pad, s_pad)))
    lines[2, 10 * elements :] = 1.0
    for elem in range(elements):
        prior = (elem - 1) % elements
        for col in range(10):
            spread[elem, col * elements + elem] = 1.0
            for row in range(10):
                window[(7 * elem - 1 + row) % points, col * elements + elem] += basis[row, col]
        for step in range(7):
            spread[elem, s_pad + 7 * elem + step] = 1.0
            spread[prior, s_pad + z_pad + 7 * elem + step] = 1.0
            lines[0, 7 * elem + step] = weights[step]
            for row in range(8):
                own_cols[(7 * elem + row) % points, 7 * elem + step] += stiffness[row, step]
        lines[1, 7 * elem] = weights[7]
        for row in range(8):
            before_cols[(7 * prior + row) % points, 7 * elem] += stiffness[row, 7]
    lam_all = np.zeros((SPEC, s_pad))
    lam_two = (lam[:, None] + lam[None, :]).reshape(-1)
    lam_all[:100, : 10 * elements] = lam_two[:, None] + np.repeat(lam, elements)[None, :]
    segments = np.zeros((coarse_count, z_pad))
    for row in range(coarse_count):
        length = points // coarse_count
        segments[row, row * length : (row + 1) * length] = 1.0
    inner = place_a.reshape(10, 10, STACK)[1:9, 1:9].reshape(OWN, STACK)
    inner = np.concatenate([inner[:, start : start + 8] for start, _ in LAST] + [np.zeros((OWN, 8))], axis=1)
    window_high, window_low = halves(window)
    back_high, back_low = halves(window.T)
    single = lambda value: np.asarray(value, np.float32)
    return {
        "pick_a": left_exact(pick_a),
        "spec_in": left_split(spectral_in[:, OWN:]),
        "spec_own": left_split(spectral_in[:, :OWN]),
        "spec_out": left_split(spectral_out),
        "pick_place": left_exact((pick_a @ place_s)[:, OWN:]),
        "pick_own": left_exact((pick_a @ place_s)[:, :OWN]),
        "plane": left_split(pick_a @ plane),
        "inner": left_exact(inner),
        "win_h": window_high,
        "win_l": window_low,
        "back_h": back_high,
        "back_l": back_low,
        "own_cols": single(own_cols),
        "before_cols": single(before_cols),
        "lam_all": single(lam_all),
        "spread": single(spread),
        "lines": single(lines),
        "segments": single(segments),
        "plane_weight": single((pick_a @ plane_weight)[:, None]),
    }


def split_two(value):
    high = value.astype(jnp.bfloat16)
    return high, (value - high.astype(jnp.float32)).astype(jnp.bfloat16)


def mul(left, right):
    return jnp.dot(left, right, preferred_element_type=jnp.float32)


def left_mul(matrix, value):
    high, low = split_two(value)
    return mul(matrix[...], jnp.concatenate([high, high, low], axis=0))


def left_place(matrix, value):
    high = value.astype(jnp.bfloat16)
    rest = value - high.astype(jnp.float32)
    middle, low = split_two(rest)
    return mul(matrix[...], jnp.concatenate([high, middle, low], axis=0))


def right_mul(value, high_ref, low_ref):
    high, low = split_two(value)
    both = mul(jnp.concatenate([high, low], axis=0), high_ref[...])
    rows = value.shape[0]
    return both[:rows] + (mul(high, low_ref[...]) + both[rows:])


def each_other(count, act):
    if count <= 8:
        for step in range(1, count):
            act(step)
    else:

        def body(step, carry):
            act(step)
            return carry

        lax.fori_loop(1, count, body, 0)


def stage_size(stage, n_gx, n_gy):
    return {"x": n_gx, "y": n_gy, "xy": n_gx * n_gy}[stage]


def last_stages(n_gx, n_gy):
    return ("xy",) if n_gx * n_gy <= DIRECT else STAGES


def kernel(n_gx, n_gy, n_in, *refs):
    sources = refs[:n_in]
    out = refs[n_in]
    loaded = refs[n_in + 1 : 2 * n_in + 1]
    load_sem, arrived, sending, own_rows, z_high, z_low, scale, first, field_w, halo_send, halo_recv = refs[
        2 * n_in + 1 : 2 * n_in + 12
    ]
    lanes = refs[2 * n_in + 12 :]
    (
        rhs, pick_a, segments, factor,
        stiff, mass, spread, lines, lam_all, spec_own, spec_in, win_h, win_l, back_h, back_l, spec_out,
        own_cols, before_cols, pick_own, pick_place, plane, plane_weight, inner,
    ) = loaded
    loads = [
        pltpu.make_async_copy(source, target, load_sem.at[index])
        for index, (source, target) in enumerate(zip(sources, loaded))
    ]
    for load in loads:
        load.start()

    me_x, me_y = lax.axis_index("gx"), lax.axis_index("gy")
    points = rhs.shape[2]
    z_pad, s_pad = win_h.shape

    def beside(off_x, off_y):
        return (lax.rem(me_x + off_x + n_gx, n_gx), lax.rem(me_y + off_y + n_gy, n_gy))

    def each_offset(stage, act):
        if stage == "xy":
            for off_x in range(n_gx):
                for off_y in range(n_gy):
                    if off_x or off_y:
                        act(off_x, off_y)
        elif stage == "x":
            each_other(n_gx, lambda step: act(step, 0))
        else:
            each_other(n_gy, lambda step: act(0, step))

    barrier = pltpu.get_barrier_semaphore()

    def greet(off_x, off_y):
        pl.semaphore_signal(barrier, inc=1, device_id=beside(off_x, off_y), device_id_type=MESH)

    greeted = 0
    for stage in last_stages(n_gx, n_gy):
        each_offset(stage, greet)
        greeted += stage_size(stage, n_gx, n_gy) - 1
    if last_stages(n_gx, n_gy) == STAGES:
        for off_x, off_y, _, _ in SLOTS[4:]:
            greet(off_x, off_y)
            greeted += 1

    def halo_copy(turn, slot, start, rows):
        off_x, off_y, _, _ = SLOTS[slot]
        return pltpu.make_async_remote_copy(
            src_ref=sending.at[turn, pl.ds(start, rows)],
            dst_ref=arrived.at[turn, pl.ds(start, rows)],
            send_sem=halo_send.at[turn, slot],
            recv_sem=halo_recv.at[turn, slot],
            device_id=beside(-off_x, -off_y),
            device_id_type=MESH,
        )

    def halo_copies(turn):
        if turn == ROUNDS - 1:
            return [halo_copy(turn, slot, *LAST_PACKED[slot]) for _, slot in LAST]
        return [halo_copy(turn, slot, *PACKED[slot]) for slot in (4, 5, 6, 7, 0, 1, 2, 3)]

    tile_row = lax.broadcasted_iota(jnp.int32, (8, 128), 0)
    tile_lane = lax.broadcasted_iota(jnp.int32, (8, 128), 1)

    def halo_start(turn, rows):
        for slot, (_, _, start, count) in enumerate(SLOTS):
            at = PACKED[slot][0]
            if count == 8:
                part = rows[start : start + 8]
                sending[turn, pl.ds(at, 8)] = jnp.where(tile_row < 4, part[:, :128], part[:, 128:])
            else:
                sending[turn, pl.ds(at, 16)] = rows[start : start + 16, :128]
                sending[turn, pl.ds(at + 16, 8)] = rows[start : start + 8, 128:] + pltpu.roll(
                    rows[start + 8 : start + 16, 128:], 64, 1
                )
        for copy in halo_copies(turn):
            copy.start()
        own_rows[turn] = rows[:OWN]

    def left_half(tile):
        return jnp.where(tile_lane < 64, tile, 0.0)

    def corner_rows(turn, slot):
        tile = arrived[turn, pl.ds(PACKED[slot][0], 8)]
        upper = jnp.where(tile_row < 4, tile, 0.0)
        return jnp.concatenate([upper, jnp.where(tile_row < 4, 0.0, tile)], axis=1)

    def first_rows(turn, slot):
        at = PACKED[slot][0]
        tail = arrived[turn, pl.ds(at + 16, 8)]
        return jnp.concatenate([arrived[turn, pl.ds(at, 8)], left_half(tail)], axis=1)

    def second_rows(turn, slot):
        at = PACKED[slot][0]
        tail = pltpu.roll(arrived[turn, pl.ds(at + 16, 8)], 64, 1)
        return jnp.concatenate([arrived[turn, pl.ds(at + 8, 8)], left_half(tail)], axis=1)

    def halo_wait(turn):
        for copy in halo_copies(turn):
            copy.wait_recv()

    def stack(turn):
        parts = []
        for slot in range(4):
            parts += [first_rows(turn, slot), second_rows(turn, slot)]
        parts += [corner_rows(turn, slot) for slot in range(4, 8)]
        return jnp.concatenate(parts, axis=0)

    def halo_drain(turn):
        for copy in halo_copies(turn):
            copy.wait_send()

    def slot_of(stage, off_x, off_y):
        at_x, at_y = beside(off_x, off_y)
        return {"x": at_x, "y": at_y, "xy": at_x * n_gy + at_y}[stage]

    class Lane:
        def __init__(self, stages, buffers):
            self.legs = [(stage,) + tuple(buffers[3 * at : 3 * at + 3]) for at, stage in enumerate(stages)]

        def copy(self, leg, off_x, off_y, slot):
            stage, buf, send, recv = leg
            index = off_x * n_gy + off_y if stage == "xy" else off_x + off_y
            return pltpu.make_async_remote_copy(
                src_ref=buf.at[slot],
                dst_ref=buf.at[slot],
                send_sem=send.at[index],
                recv_sem=recv.at[index],
                device_id=beside(off_x, off_y),
                device_id_type=MESH,
            )

        def put(self, leg, value):
            mine = slot_of(leg[0], 0, 0)
            leg[1][mine] = value
            each_offset(leg[0], lambda x, y: self.copy(leg, x, y, mine).start())

        def take(self, leg):
            each_offset(leg[0], lambda x, y: self.copy(leg, x, y, slot_of(leg[0], -x, -y)).wait_recv())
            return jnp.sum(leg[1][...], axis=0)

        def start(self, value):
            self.put(self.legs[0], value)

        def middle(self):
            for before, after in zip(self.legs, self.legs[1:]):
                self.put(after, self.take(before))

        def finish(self):
            return self.take(self.legs[-1])

        def drain(self):
            for leg in self.legs:
                mine = slot_of(leg[0], 0, 0)
                each_offset(leg[0], lambda x, y: self.copy(leg, x, y, mine).wait_send())

    coarse = [Lane(STAGES, lanes[:6]), Lane(STAGES, lanes[6:12])]
    sums = Lane(last_stages(n_gx, n_gy), lanes[12:])

    point = lax.broadcasted_iota(jnp.int32, (OWN, z_pad), 0)
    at_x, at_y = point // 8, point % 8
    coarse_mask = (at_x >= 1) & (at_x <= 6) & (at_y >= 1) & (at_y <= 6)

    def coarse_start(turn, rows):
        line = jnp.sum(jnp.where(coarse_mask, rows, 0.0), axis=0, keepdims=True)
        held = jnp.sum(segments[...] * line, axis=1, keepdims=True)
        coarse[turn].start(jnp.sum(factor[...] * held, axis=0, keepdims=True))

    def coarse_finish(turn):
        total = coarse[turn].finish()
        values = jnp.sum(factor[...] * total, axis=1, keepdims=True)
        line = jnp.sum(segments[...] * values, axis=0, keepdims=True)
        return jnp.where(coarse_mask, line, 0.0)

    first[...] = jnp.zeros_like(first)
    for load in loads[:4]:
        load.wait()
    for row in range(7):
        first[pl.ds(8 * row, 7), pl.ds(0, points)] = rhs[row]
    right = first[...]
    rows = left_place(pick_a, right)
    pl.semaphore_wait(barrier, greeted)
    halo_start(0, rows)
    coarse_start(0, right)

    for load in loads[4:16]:
        load.wait()

    def spread_out(coef, start, size):
        return jnp.dot(
            jnp.broadcast_to(coef[0], (8, coef.shape[2])), spread[:, start : start + size],
            precision=exact_mode, preferred_element_type=jnp.float32,
        )[0:1]

    stiff_s, mass_s = spread_out(stiff, 0, s_pad), spread_out(mass, 0, s_pad)
    scale[...] = 1.0 / (stiff_s * lam_all[...] + (mass_s + lines[2:3, :s_pad]))

    def prepare_elements():
        for load in loads[16:]:
            load.wait()
        stiff_own, stiff_before = spread_out(stiff, s_pad, z_pad), spread_out(stiff, s_pad + z_pad, z_pad)
        mass_own, mass_before = spread_out(mass, s_pad, z_pad), spread_out(mass, s_pad + z_pad, z_pad)
        weight_own, weight_before = lines[0:1, :z_pad], lines[1:2, :z_pad]
        line_mass = mass_own * weight_own + mass_before * weight_before
        diagonal = lax.broadcasted_iota(jnp.int32, (z_pad, z_pad), 0) == lax.broadcasted_iota(
            jnp.int32, (z_pad, z_pad), 1
        )
        along = own_cols[...] * stiff_own + before_cols[...] * stiff_before
        z_high[...], z_low[...] = split_two(along + jnp.where(diagonal, line_mass, 0.0))
        return stiff_own * weight_own + stiff_before * weight_before

    def element(turn):
        held = left_place(pick_own, own_rows[turn])
        halo_wait(turn)
        wide = held + left_place(pick_place, stack(turn))
        field = wide[:OWN]
        result = left_mul(plane, field * line_stiff) + plane_weight[...] * right_mul(
            wide, z_high, z_low
        )
        return field, result

    def precondition(turn):
        held = left_mul(spec_own, own_rows[2 * turn])
        halo_wait(2 * turn)
        spectral = right_mul(held + left_mul(spec_in, stack(2 * turn)), win_h, win_l) * scale[...]
        coarse[turn].middle()
        result = left_mul(spec_out, right_mul(spectral, back_h, back_l))
        halo_start(2 * turn + 1, result)
        plate = coarse_finish(turn)
        own_rows[2 * turn + 1] = result[:OWN] + plate
        halo_drain(2 * turn)
        coarse[turn].drain()

    def dot_line(left, other):
        return jnp.sum(left * other, axis=0, keepdims=True)

    def gathered(turn, own):
        parts = [second_rows(turn, 0), second_rows(turn, 2), corner_rows(turn, 4)]
        return own + left_place(inner, jnp.concatenate(parts + [jnp.zeros_like(parts[0])], axis=0))

    owned = (at_x < 7) & (at_y < 7)

    precondition(0)
    line_stiff = prepare_elements()
    z_field, w_rows = element(1)
    halo_start(2, w_rows)
    w_local = w_rows[:OWN]
    coarse_start(1, w_local)
    precondition(1)
    field_w[...] = gathered(2, w_local)
    v_field, av_rows = element(3)
    halo_start(4, av_rows)
    av_local = av_rows[:OWN]
    partial = jnp.concatenate(
        [
            dot_line(right, jnp.where(owned, z_field, 0.0)),
            dot_line(z_field, w_local),
            dot_line(right, jnp.where(owned, v_field, 0.0)),
            dot_line(v_field, w_local),
            dot_line(v_field, av_local),
            dot_line(z_field, av_local),
            jnp.zeros((2, z_pad), jnp.float32),
        ],
        axis=0,
    )
    at_row = lax.broadcasted_iota(jnp.int32, (8, 128), 0)
    at_lane = lax.broadcasted_iota(jnp.int32, (8, 128), 1)
    packed = jnp.where(at_row == at_lane, jnp.sum(partial, axis=1, keepdims=True), 0.0)
    sums.start(jnp.sum(packed, axis=0, keepdims=True))
    sums.middle()
    for turn in (1, 3, 4):
        halo_drain(turn)
    sums.drain()
    halo_wait(4)
    av_field = gathered(4, av_local)
    w_field = field_w[...]
    totals = sums.finish()
    rz, zw, rv, vw, vav, zav = [totals[:, lane : lane + 1] for lane in range(6)]
    step_0 = rz / zw
    rho_1 = rz - step_0 * (rv + zw) + step_0 * step_0 * vw
    momentum = rho_1 / rz
    curve = (
        zw - step_0 * (vw + zav) + step_0 * step_0 * vav
        + momentum * ((zw - step_0 * vw) + (zw - step_0 * zav))
        + momentum * momentum * zw
    )
    step_1 = rho_1 / curve
    next_dir = (z_field - step_0 * v_field) + momentum * z_field
    next_image = (w_field - step_0 * av_field) + momentum * w_field
    final_x = step_0 * z_field + step_1 * next_dir
    final_r = (right - step_0 * w_field) - step_1 * next_image
    out[0] = final_x
    out[1] = final_r


def move(both, to_x, to_r):
    points = to_x.shape[2]
    for row in range(7):
        to_x[row] = both[0, pl.ds(8 * row, 7), pl.ds(0, points)]
        to_r[row] = both[1, pl.ds(8 * row, 7), pl.ds(0, points)]


def local(n_gx, n_gy, right_side, stiff_coef, mass_coef, coarse_factor):
    elements = stiff_coef.shape[2]
    coarse_count, coarse_all = coarse_factor.shape
    tables = {name: jnp.asarray(table) for name, table in constants(elements, coarse_count).items()}
    tables.update(rhs=right_side, stiff=stiff_coef, mass=mass_coef, factor=coarse_factor)
    operands = [tables[name] for name in OPERANDS]
    z_pad = round_up(7 * elements, 128)
    s_pad = round_up(10 * elements, 128)
    dma = pltpu.SemaphoreType.DMA
    single = jnp.float32
    whole = pl.BlockSpec(memory_space=pltpu.VMEM)
    shape = jax.ShapeDtypeStruct(right_side.shape, single)
    lanes = []
    last = last_stages(n_gx, n_gy)
    for width, stages in ((coarse_all, STAGES), (coarse_all, STAGES), (128, last)):
        for stage in stages:
            size = stage_size(stage, n_gx, n_gy)
            lanes += [pltpu.VMEM((size, 1, width), single), dma((size,)), dma((size,))]
    result = pl.pallas_call(
        functools.partial(kernel, n_gx, n_gy, len(operands)),
        out_shape=jax.ShapeDtypeStruct((2, OWN, z_pad), single),
        in_specs=[pl.BlockSpec(memory_space=pltpu.HBM)] * len(operands),
        out_specs=whole,
        scratch_shapes=[pltpu.VMEM(operand.shape, operand.dtype) for operand in operands]
        + [
            dma((len(operands),)),
            pltpu.VMEM((ROUNDS, MESSAGE, 128), single),
            pltpu.VMEM((ROUNDS, MESSAGE, 128), single),
            pltpu.VMEM((ROUNDS, OWN, z_pad), single),
            pltpu.VMEM((z_pad, z_pad), jnp.bfloat16),
            pltpu.VMEM((z_pad, z_pad), jnp.bfloat16),
            pltpu.VMEM((SPEC, s_pad), single),
            pltpu.VMEM((OWN, z_pad), single),
            pltpu.VMEM((OWN, z_pad), single),
            dma((ROUNDS, 8)),
            dma((ROUNDS, 8)),
        ]
        + lanes,
        compiler_params=pltpu.CompilerParams(
            collective_id=0, has_side_effects=True, vmem_limit_bytes=60 * 1024 * 1024
        ),
    )(*operands)
    return pl.pallas_call(
        move,
        out_shape=(shape, shape),
        in_specs=[whole],
        out_specs=(whole, whole),
        compiler_params=pltpu.CompilerParams(vmem_limit_bytes=60 * 1024 * 1024),
    )(result)


def solution(mesh):
    placed = (P("gx", "gy", None), P("gx", "gy", None), P("gx", "gy", None), P(("gx", "gy"), None))
    return jax.shard_map(
        functools.partial(local, mesh.shape["gx"], mesh.shape["gy"]),
        mesh=mesh,
        in_specs=placed,
        out_specs=(P("gx", "gy", None), P("gx", "gy", None)),
        check_vma=False,
    )
```

```python
import functools
import math

import jax
import jax.numpy as jnp
import numpy as np
from jax import lax
from jax.experimental import pallas as pl
from jax.experimental.pallas import tpu as pltpu
from jax.sharding import PartitionSpec as P

MESH = pl.DeviceIdType.MESH
exact_mode = lax.Precision.HIGHEST
ROUNDS = 5

OWN = 64
SLOTS = (
    (-1, 0, 64, 16),
    (1, 0, 80, 16),
    (0, -1, 96, 16),
    (0, 1, 112, 16),
    (-1, -1, 128, 8),
    (-1, 1, 136, 8),
    (1, -1, 144, 8),
    (1, 1, 152, 8),
)
STACK = 160
SPEC = 112
PACKED = ((0, 24), (24, 24), (48, 24), (72, 24), (96, 8), (104, 8), (112, 8), (120, 8))
MESSAGE = 128
LAST = ((72, 0), (104, 2), (128, 4))
LAST_PACKED = {0: (8, 16), 2: (56, 16), 4: (96, 8)}
OPERANDS = (
    "rhs", "pick_a", "segments", "factor",
    "stiff", "mass", "spread", "lines", "lam_all", "spec_own", "spec_in", "win_h", "win_l", "back_h", "back_l", "spec_out",
    "own_cols", "before_cols", "pick_own", "pick_place", "plane", "plane_weight", "inner",
)
STAGES = ("x", "y")
DIRECT = 64


def legendre_pair(position, degree):
    p_prev = 1.0
    p_now = position
    for order in range(2, degree + 1):
        p_next = ((2 * order - 1) * position * p_now - (order - 1) * p_prev) / order
        p_prev = p_now
        p_now = p_next
    return (p_now, p_prev)


def jacobi_eigen(matrix):
    size_n = matrix.shape[0]
    current = np.array(matrix)
    vectors = np.eye(size_n)
    for sweep in range(20):
        for row_p in range(size_n - 1):
            for row_q in range(row_p + 1, size_n):
                off_value = current[row_p, row_q]
                if abs(off_value) > 1e-300:
                    theta = (current[row_q, row_q] - current[row_p, row_p]) / (2.0 * off_value)
                    sign_t = 1.0 if theta >= 0.0 else -1.0
                    tangent = sign_t / (abs(theta) + math.sqrt(theta * theta + 1.0))
                    cosine = 1.0 / math.sqrt(tangent * tangent + 1.0)
                    sine = tangent * cosine
                    rotation = np.eye(size_n)
                    rotation[row_p, row_p] = cosine
                    rotation[row_q, row_q] = cosine
                    rotation[row_p, row_q] = sine
                    rotation[row_q, row_p] = -sine
                    current = rotation.T @ current @ rotation
                    vectors = vectors @ rotation
    return (np.array([current[idx, idx] for idx in range(size_n)]), vectors)


def gll_tables():
    degree = 7
    guesses = [
        -0.8717401485096066,
        -0.5917001814331423,
        -0.2092992179024789,
        0.2092992179024789,
        0.5917001814331423,
        0.8717401485096066,
    ]
    interior = []
    for guess in guesses:
        position = guess
        for newton in range(30):
            p_now, p_prev = legendre_pair(position, degree)
            first = degree * (position * p_now - p_prev) / (position * position - 1.0)
            second = (2.0 * position * first - degree * (degree + 1) * p_now) / (
                1.0 - position * position
            )
            position = position - first / second
        interior.append(position)
    points = np.array([-1.0] + interior + [1.0])
    values = np.array([legendre_pair(float(pt), degree)[0] for pt in points])
    weights = 2.0 / (degree * (degree + 1) * values**2)
    deriv_mat = np.zeros((8, 8))
    for left_idx in range(8):
        for right_idx in range(8):
            if left_idx != right_idx:
                deriv_mat[left_idx, right_idx] = values[left_idx] / (
                    values[right_idx] * (points[left_idx] - points[right_idx])
                )
    deriv_mat[0, 0] = -degree * (degree + 1) / 4.0
    deriv_mat[7, 7] = degree * (degree + 1) / 4.0
    stiffness = deriv_mat.T @ (weights[:, None] * deriv_mat)
    ext_stiff = np.zeros((10, 10))
    ext_stiff[1:9, 1:9] += stiffness
    ext_stiff[0:2, 0:2] += stiffness[6:8, 6:8]
    ext_stiff[8:10, 8:10] += stiffness[0:2, 0:2]
    ext_mass = np.zeros(10)
    ext_mass[1:9] += weights
    ext_mass[0:2] += weights[6:8]
    ext_mass[8:10] += weights[0:2]
    inv_root = 1.0 / np.sqrt(ext_mass)
    eigen_vals, eigen_vecs = jacobi_eigen(inv_root[:, None] * ext_stiff * inv_root[None, :])
    eigen_basis = inv_root[:, None] * eigen_vecs
    return stiffness, weights, eigen_basis, eigen_vals


def round_up(count, unit):
    return -(-count // unit) * unit


def stack_map(taken, placed, size_from, size_to):
    pick = np.zeros((STACK, size_from * size_from))
    place = np.zeros((size_to * size_to, STACK))
    for off_x, off_y, start, _ in ((0, 0, 0, OWN),) + SLOTS:
        row = start
        pairs_x = list(zip(taken[off_x], placed[off_x]))
        pairs_y = list(zip(taken[off_y], placed[off_y]))
        pairs = [(one, two) for one in pairs_x for two in pairs_y]
        if off_x == 0 and off_y != 0:
            pairs = [(one, two) for two in pairs_y for one in pairs_x]
        if off_x != 0 and off_y != 0:
            pairs = pairs + pairs
        for (from_x, to_x), (from_y, to_y) in pairs:
            pick[row, from_x * size_from + from_y] = 1.0
            place[to_x * size_to + to_y, row] = 1.0
            row += 1
    return pick, place


def halves(matrix):
    exact = np.asarray(matrix, np.float32)
    high = exact.astype(jnp.bfloat16)
    low = (exact - high.astype(np.float32)).astype(jnp.bfloat16)
    return high, low


def left_split(matrix):
    high, low = halves(matrix)
    return np.concatenate([high, low, high], axis=1)


def left_exact(matrix):
    return np.concatenate([np.asarray(matrix).astype(jnp.bfloat16)] * 3, axis=1)


def constants(elements, coarse_count):
    stiffness, weights, basis, lam = gll_tables()
    stiffness = np.asarray(stiffness, np.float32).astype(np.float64)
    weights = np.asarray(weights, np.float32).astype(np.float64)
    basis = np.asarray(basis, np.float32).astype(np.float64)
    lam = np.asarray(lam, np.float32).astype(np.float64)
    points = 7 * elements
    z_pad = round_up(points, 128)
    s_pad = round_up(10 * elements, 128)
    every = list(range(8))
    pick_a, place_a = stack_map(
        {-1: [6, 7], 0: every, 1: [0, 1]}, {-1: [0, 1], 0: list(range(1, 9)), 1: [8, 9]}, 8, 10
    )
    pick_s, place_s = stack_map(
        {-1: [8, 9], 0: list(range(1, 9)), 1: [0, 1]}, {-1: [0, 1], 0: every, 1: [6, 7]}, 10, 8
    )
    basis_two = np.kron(basis, basis)
    spectral_in = np.zeros((SPEC, STACK))
    spectral_in[:100] = basis_two.T @ place_a
    spectral_out = np.zeros((STACK, SPEC))
    spectral_out[:, :100] = pick_s @ basis_two
    plane = np.kron(stiffness, np.diag(weights)) + np.kron(np.diag(weights), stiffness)
    plane_weight = np.kron(weights, weights)
    window = np.zeros((z_pad, s_pad))
    own_cols = np.zeros((z_pad, z_pad))
    before_cols = np.zeros((z_pad, z_pad))
    spread = np.zeros((elements, s_pad + 2 * z_pad))
    lines = np.zeros((8, max(z_pad, s_pad)))
    lines[2, 10 * elements :] = 1.0
    for elem in range(elements):
        prior = (elem - 1) % elements
        for col in range(10):
            spread[elem, col * elements + elem] = 1.0
            for row in range(10):
                window[(7 * elem - 1 + row) % points, col * elements + elem] += basis[row, col]
        for step in range(7):
            spread[elem, s_pad + 7 * elem + step] = 1.0
            spread[prior, s_pad + z_pad + 7 * elem + step] = 1.0
            lines[0, 7 * elem + step] = weights[step]
            for row in range(8):
                own_cols[(7 * elem + row) % points, 7 * elem + step] += stiffness[row, step]
        lines[1, 7 * elem] = weights[7]
        for row in range(8):
            before_cols[(7 * prior + row) % points, 7 * elem] += stiffness[row, 7]
    lam_all = np.zeros((SPEC, s_pad))
    lam_two = (lam[:, None] + lam[None, :]).reshape(-1)
    lam_all[:100, : 10 * elements] = lam_two[:, None] + np.repeat(lam, elements)[None, :]
    segments = np.zeros((coarse_count, z_pad))
    for row in range(coarse_count):
        length = points // coarse_count
        segments[row, row * length : (row + 1) * length] = 1.0
    inner = place_a.reshape(10, 10, STACK)[1:9, 1:9].reshape(OWN, STACK)
    inner = np.concatenate([inner[:, start : start + 8] for start, _ in LAST] + [np.zeros((OWN, 8))], axis=1)
    window_high, window_low = halves(window)
    back_high, back_low = halves(window.T)
    single = lambda value: np.asarray(value, np.float32)
    return {
        "pick_a": left_exact(pick_a),
        "spec_in": left_split(spectral_in[:, OWN:]),
        "spec_own": left_split(spectral_in[:, :OWN]),
        "spec_out": left_split(spectral_out),
        "pick_place": left_exact((pick_a @ place_s)[:, OWN:]),
        "pick_own": left_exact((pick_a @ place_s)[:, :OWN]),
        "plane": left_split(pick_a @ plane),
        "inner": left_exact(inner),
        "win_h": window_high,
        "win_l": window_low,
        "back_h": back_high,
        "back_l": back_low,
        "own_cols": single(own_cols),
        "before_cols": single(before_cols),
        "lam_all": single(lam_all),
        "spread": single(spread),
        "lines": single(lines),
        "segments": single(segments),
        "plane_weight": single((pick_a @ plane_weight)[:, None]),
    }


def split_two(value):
    high = value.astype(jnp.bfloat16)
    return high, (value - high.astype(jnp.float32)).astype(jnp.bfloat16)


def mul(left, right):
    return jnp.dot(left, right, preferred_element_type=jnp.float32)


def left_mul(matrix, value):
    high, low = split_two(value)
    return mul(matrix[...], jnp.concatenate([high, high, low], axis=0))


def left_place(matrix, value):
    high = value.astype(jnp.bfloat16)
    rest = value - high.astype(jnp.float32)
    middle, low = split_two(rest)
    return mul(matrix[...], jnp.concatenate([high, middle, low], axis=0))


def right_mul(value, high_ref, low_ref):
    high, low = split_two(value)
    both = mul(jnp.concatenate([high, low], axis=0), high_ref[...])
    rows = value.shape[0]
    return both[:rows] + (mul(high, low_ref[...]) + both[rows:])


def each_other(count, act):
    if count <= 8:
        for step in range(1, count):
            act(step)
    else:

        def body(step, carry):
            act(step)
            return carry

        lax.fori_loop(1, count, body, 0)


def stage_size(stage, n_gx, n_gy):
    return {"x": n_gx, "y": n_gy, "xy": n_gx * n_gy}[stage]


def last_stages(n_gx, n_gy):
    return ("xy",) if n_gx * n_gy <= DIRECT else STAGES


def kernel(n_gx, n_gy, n_in, *refs):
    sources = refs[:n_in]
    out = refs[n_in]
    loaded = refs[n_in + 1 : 2 * n_in + 1]
    load_sem, arrived, sending, own_rows, z_high, z_low, scale, first, field_w, halo_send, halo_recv = refs[
        2 * n_in + 1 : 2 * n_in + 12
    ]
    lanes = refs[2 * n_in + 12 :]
    (
        rhs, pick_a, segments, factor,
        stiff, mass, spread, lines, lam_all, spec_own, spec_in, win_h, win_l, back_h, back_l, spec_out,
        own_cols, before_cols, pick_own, pick_place, plane, plane_weight, inner,
    ) = loaded
    loads = [
        pltpu.make_async_copy(source, target, load_sem.at[index])
        for index, (source, target) in enumerate(zip(sources, loaded))
    ]
    for load in loads:
        load.start()

    me_x, me_y = lax.axis_index("gx"), lax.axis_index("gy")
    points = rhs.shape[2]
    z_pad, s_pad = win_h.shape

    def beside(off_x, off_y):
        return (lax.rem(me_x + off_x + n_gx, n_gx), lax.rem(me_y + off_y + n_gy, n_gy))

    def each_offset(stage, act):
        if stage == "xy":
            for off_x in range(n_gx):
                for off_y in range(n_gy):
                    if off_x or off_y:
                        act(off_x, off_y)
        elif stage == "x":
            each_other(n_gx, lambda step: act(step, 0))
        else:
            each_other(n_gy, lambda step: act(0, step))

    barrier = pltpu.get_barrier_semaphore()

    def greet(off_x, off_y):
        pl.semaphore_signal(barrier, inc=1, device_id=beside(off_x, off_y), device_id_type=MESH)

    greeted = 0
    for stage in last_stages(n_gx, n_gy):
        each_offset(stage, greet)
        greeted += stage_size(stage, n_gx, n_gy) - 1
    if last_stages(n_gx, n_gy) == STAGES:
        for off_x, off_y, _, _ in SLOTS[4:]:
            greet(off_x, off_y)
            greeted += 1

    def halo_copy(turn, slot, start, rows):
        off_x, off_y, _, _ = SLOTS[slot]
        return pltpu.make_async_remote_copy(
            src_ref=sending.at[turn, pl.ds(start, rows)],
            dst_ref=arrived.at[turn, pl.ds(start, rows)],
            send_sem=halo_send.at[turn, slot],
            recv_sem=halo_recv.at[turn, slot],
            device_id=beside(-off_x, -off_y),
            device_id_type=MESH,
        )

    def halo_copies(turn):
        if turn == ROUNDS - 1:
            return [halo_copy(turn, slot, *LAST_PACKED[slot]) for _, slot in LAST]
        return [halo_copy(turn, slot, *PACKED[slot]) for slot in (4, 5, 6, 7, 0, 1, 2, 3)]

    tile_row = lax.broadcasted_iota(jnp.int32, (8, 128), 0)
    tile_lane = lax.broadcasted_iota(jnp.int32, (8, 128), 1)

    def halo_start(turn, rows):
        for slot, (_, _, start, count) in enumerate(SLOTS):
            at = PACKED[slot][0]
            if count == 8:
                part = rows[start : start + 8]
                sending[turn, pl.ds(at, 8)] = jnp.where(tile_row < 4, part[:, :128], part[:, 128:])
            else:
                sending[turn, pl.ds(at, 16)] = rows[start : start + 16, :128]
                sending[turn, pl.ds(at + 16, 8)] = rows[start : start + 8, 128:] + pltpu.roll(
                    rows[start + 8 : start + 16, 128:], 64, 1
                )
        for copy in halo_copies(turn):
            copy.start()
        own_rows[turn] = rows[:OWN]

    def left_half(tile):
        return jnp.where(tile_lane < 64, tile, 0.0)

    def corner_rows(turn, slot):
        tile = arrived[turn, pl.ds(PACKED[slot][0], 8)]
        upper = jnp.where(tile_row < 4, tile, 0.0)
        return jnp.concatenate([upper, jnp.where(tile_row < 4, 0.0, tile)], axis=1)

    def first_rows(turn, slot):
        at = PACKED[slot][0]
        tail = arrived[turn, pl.ds(at + 16, 8)]
        return jnp.concatenate([arrived[turn, pl.ds(at, 8)], left_half(tail)], axis=1)

    def second_rows(turn, slot):
        at = PACKED[slot][0]
        tail = pltpu.roll(arrived[turn, pl.ds(at + 16, 8)], 64, 1)
        return jnp.concatenate([arrived[turn, pl.ds(at + 8, 8)], left_half(tail)], axis=1)

    def halo_wait(turn):
        for copy in halo_copies(turn):
            copy.wait_recv()

    def stack(turn):
        parts = []
        for slot in range(4):
            parts += [first_rows(turn, slot), second_rows(turn, slot)]
        parts += [corner_rows(turn, slot) for slot in range(4, 8)]
        return jnp.concatenate(parts, axis=0)

    def halo_drain(turn):
        for copy in halo_copies(turn):
            copy.wait_send()

    def slot_of(stage, off_x, off_y):
        at_x, at_y = beside(off_x, off_y)
        return {"x": at_x, "y": at_y, "xy": at_x * n_gy + at_y}[stage]

    class Lane:
        def __init__(self, stages, buffers):
            self.legs = [(stage,) + tuple(buffers[3 * at : 3 * at + 3]) for at, stage in enumerate(stages)]

        def copy(self, leg, off_x, off_y, slot):
            stage, buf, send, recv = leg
            index = off_x * n_gy + off_y if stage == "xy" else off_x + off_y
            return pltpu.make_async_remote_copy(
                src_ref=buf.at[slot],
                dst_ref=buf.at[slot],
                send_sem=send.at[index],
                recv_sem=recv.at[index],
                device_id=beside(off_x, off_y),
                device_id_type=MESH,
            )

        def put(self, leg, value):
            mine = slot_of(leg[0], 0, 0)
            leg[1][mine] = value
            each_offset(leg[0], lambda x, y: self.copy(leg, x, y, mine).start())

        def take(self, leg):
            each_offset(leg[0], lambda x, y: self.copy(leg, x, y, slot_of(leg[0], -x, -y)).wait_recv())
            return jnp.sum(leg[1][...], axis=0)

        def start(self, value):
            self.put(self.legs[0], value)

        def middle(self):
            for before, after in zip(self.legs, self.legs[1:]):
                self.put(after, self.take(before))

        def finish(self):
            return self.take(self.legs[-1])

        def drain(self):
            for leg in self.legs:
                mine = slot_of(leg[0], 0, 0)
                each_offset(leg[0], lambda x, y: self.copy(leg, x, y, mine).wait_send())

    ways = last_stages(n_gx, n_gy)
    each = 3 * len(ways)
    coarse = [Lane(ways, lanes[:each]), Lane(ways, lanes[each : 2 * each])]
    sums = Lane(ways, lanes[2 * each :])

    point = lax.broadcasted_iota(jnp.int32, (OWN, z_pad), 0)
    at_x, at_y = point // 8, point % 8
    coarse_mask = (at_x >= 1) & (at_x <= 6) & (at_y >= 1) & (at_y <= 6)

    def coarse_start(turn, rows):
        line = jnp.sum(jnp.where(coarse_mask, rows, 0.0), axis=0, keepdims=True)
        held = jnp.sum(segments[...] * line, axis=1, keepdims=True)
        coarse[turn].start(jnp.sum(factor[...] * held, axis=0, keepdims=True))

    def coarse_finish(turn):
        total = coarse[turn].finish()
        values = jnp.sum(factor[...] * total, axis=1, keepdims=True)
        line = jnp.sum(segments[...] * values, axis=0, keepdims=True)
        return jnp.where(coarse_mask, line, 0.0)

    first[...] = jnp.zeros_like(first)
    for load in loads[:4]:
        load.wait()
    for row in range(7):
        first[pl.ds(8 * row, 7), pl.ds(0, points)] = rhs[row]
    right = first[...]
    rows = left_place(pick_a, right)
    pl.semaphore_wait(barrier, greeted)
    halo_start(0, rows)
    coarse_start(0, right)

    for load in loads[4:16]:
        load.wait()

    def spread_out(coef, start, size):
        return jnp.dot(
            jnp.broadcast_to(coef[0], (8, coef.shape[2])), spread[:, start : start + size],
            precision=exact_mode, preferred_element_type=jnp.float32,
        )[0:1]

    stiff_s, mass_s = spread_out(stiff, 0, s_pad), spread_out(mass, 0, s_pad)
    scale[...] = 1.0 / (stiff_s * lam_all[...] + (mass_s + lines[2:3, :s_pad]))

    def prepare_elements():
        for load in loads[16:]:
            load.wait()
        stiff_own, stiff_before = spread_out(stiff, s_pad, z_pad), spread_out(stiff, s_pad + z_pad, z_pad)
        mass_own, mass_before = spread_out(mass, s_pad, z_pad), spread_out(mass, s_pad + z_pad, z_pad)
        weight_own, weight_before = lines[0:1, :z_pad], lines[1:2, :z_pad]
        line_mass = mass_own * weight_own + mass_before * weight_before
        diagonal = lax.broadcasted_iota(jnp.int32, (z_pad, z_pad), 0) == lax.broadcasted_iota(
            jnp.int32, (z_pad, z_pad), 1
        )
        along = own_cols[...] * stiff_own + before_cols[...] * stiff_before
        z_high[...], z_low[...] = split_two(along + jnp.where(diagonal, line_mass, 0.0))
        return stiff_own * weight_own + stiff_before * weight_before

    def element(turn):
        held = left_place(pick_own, own_rows[turn])
        halo_wait(turn)
        wide = held + left_place(pick_place, stack(turn))
        field = wide[:OWN]
        result = left_mul(plane, field * line_stiff) + plane_weight[...] * right_mul(
            wide, z_high, z_low
        )
        return field, result

    def precondition(turn):
        held = left_mul(spec_own, own_rows[2 * turn])
        halo_wait(2 * turn)
        spectral = right_mul(held + left_mul(spec_in, stack(2 * turn)), win_h, win_l) * scale[...]
        coarse[turn].middle()
        result = left_mul(spec_out, right_mul(spectral, back_h, back_l))
        halo_start(2 * turn + 1, result)
        plate = coarse_finish(turn)
        own_rows[2 * turn + 1] = result[:OWN] + plate
        halo_drain(2 * turn)
        coarse[turn].drain()

    def dot_line(left, other):
        return jnp.sum(left * other, axis=0, keepdims=True)

    def gathered(turn, own):
        parts = [second_rows(turn, 0), second_rows(turn, 2), corner_rows(turn, 4)]
        return own + left_place(inner, jnp.concatenate(parts + [jnp.zeros_like(parts[0])], axis=0))

    owned = (at_x < 7) & (at_y < 7)

    precondition(0)
    line_stiff = prepare_elements()
    z_field, w_rows = element(1)
    halo_start(2, w_rows)
    w_local = w_rows[:OWN]
    coarse_start(1, w_local)
    precondition(1)
    field_w[...] = gathered(2, w_local)
    v_field, av_rows = element(3)
    halo_start(4, av_rows)
    av_local = av_rows[:OWN]
    partial = jnp.concatenate(
        [
            dot_line(right, jnp.where(owned, z_field, 0.0)),
            dot_line(z_field, w_local),
            dot_line(right, jnp.where(owned, v_field, 0.0)),
            dot_line(v_field, w_local),
            dot_line(v_field, av_local),
            dot_line(z_field, av_local),
            jnp.zeros((2, z_pad), jnp.float32),
        ],
        axis=0,
    )
    at_row = lax.broadcasted_iota(jnp.int32, (8, 128), 0)
    at_lane = lax.broadcasted_iota(jnp.int32, (8, 128), 1)
    packed = jnp.where(at_row == at_lane, jnp.sum(partial, axis=1, keepdims=True), 0.0)
    sums.start(jnp.sum(packed, axis=0, keepdims=True))
    sums.middle()
    for turn in (1, 3, 4):
        halo_drain(turn)
    sums.drain()
    halo_wait(4)
    av_field = gathered(4, av_local)
    w_field = field_w[...]
    totals = sums.finish()
    rz, zw, rv, vw, vav, zav = [totals[:, lane : lane + 1] for lane in range(6)]
    step_0 = rz / zw
    rho_1 = rz - step_0 * (rv + zw) + step_0 * step_0 * vw
    momentum = rho_1 / rz
    curve = (
        zw - step_0 * (vw + zav) + step_0 * step_0 * vav
        + momentum * ((zw - step_0 * vw) + (zw - step_0 * zav))
        + momentum * momentum * zw
    )
    step_1 = rho_1 / curve
    next_dir = (z_field - step_0 * v_field) + momentum * z_field
    next_image = (w_field - step_0 * av_field) + momentum * w_field
    final_x = step_0 * z_field + step_1 * next_dir
    final_r = (right - step_0 * w_field) - step_1 * next_image
    out[0] = final_x
    out[1] = final_r


def move(both, to_x, to_r):
    points = to_x.shape[2]
    for row in range(7):
        to_x[row] = both[0, pl.ds(8 * row, 7), pl.ds(0, points)]
        to_r[row] = both[1, pl.ds(8 * row, 7), pl.ds(0, points)]


def local(n_gx, n_gy, right_side, stiff_coef, mass_coef, coarse_factor):
    elements = stiff_coef.shape[2]
    coarse_count, coarse_all = coarse_factor.shape
    tables = {name: jnp.asarray(table) for name, table in constants(elements, coarse_count).items()}
    tables.update(rhs=right_side, stiff=stiff_coef, mass=mass_coef, factor=coarse_factor)
    operands = [tables[name] for name in OPERANDS]
    z_pad = round_up(7 * elements, 128)
    s_pad = round_up(10 * elements, 128)
    dma = pltpu.SemaphoreType.DMA
    single = jnp.float32
    whole = pl.BlockSpec(memory_space=pltpu.VMEM)
    shape = jax.ShapeDtypeStruct(right_side.shape, single)
    lanes = []
    for width in (coarse_all, coarse_all, 128):
        for stage in last_stages(n_gx, n_gy):
            size = stage_size(stage, n_gx, n_gy)
            lanes += [pltpu.VMEM((size, 1, width), single), dma((size,)), dma((size,))]
    result = pl.pallas_call(
        functools.partial(kernel, n_gx, n_gy, len(operands)),
        out_shape=jax.ShapeDtypeStruct((2, OWN, z_pad), single),
        in_specs=[pl.BlockSpec(memory_space=pltpu.HBM)] * len(operands),
        out_specs=whole,
        scratch_shapes=[pltpu.VMEM(operand.shape, operand.dtype) for operand in operands]
        + [
            dma((len(operands),)),
            pltpu.VMEM((ROUNDS, MESSAGE, 128), single),
            pltpu.VMEM((ROUNDS, MESSAGE, 128), single),
            pltpu.VMEM((ROUNDS, OWN, z_pad), single),
            pltpu.VMEM((z_pad, z_pad), jnp.bfloat16),
            pltpu.VMEM((z_pad, z_pad), jnp.bfloat16),
            pltpu.VMEM((SPEC, s_pad), single),
            pltpu.VMEM((OWN, z_pad), single),
            pltpu.VMEM((OWN, z_pad), single),
            dma((ROUNDS, 8)),
            dma((ROUNDS, 8)),
        ]
        + lanes,
        compiler_params=pltpu.CompilerParams(
            collective_id=0, has_side_effects=True, vmem_limit_bytes=60 * 1024 * 1024
        ),
    )(*operands)
    return pl.pallas_call(
        move,
        out_shape=(shape, shape),
        in_specs=[whole],
        out_specs=(whole, whole),
        compiler_params=pltpu.CompilerParams(vmem_limit_bytes=60 * 1024 * 1024),
    )(result)


def solution(mesh):
    placed = (P("gx", "gy", None), P("gx", "gy", None), P("gx", "gy", None), P(("gx", "gy"), None))
    return jax.shard_map(
        functools.partial(local, mesh.shape["gx"], mesh.shape["gy"]),
        mesh=mesh,
        in_specs=placed,
        out_specs=(P("gx", "gy", None), P("gx", "gy", None)),
        check_vma=False,
    )
```

```python
import functools
import math

import jax
import jax.numpy as jnp
import numpy as np
from jax import lax
from jax.experimental import pallas as pl
from jax.experimental.pallas import tpu as pltpu
from jax.sharding import PartitionSpec as P

MESH = pl.DeviceIdType.MESH
exact_mode = lax.Precision.HIGHEST
ROUNDS = 5

OWN = 64
SLOTS = (
    (-1, 0, 64, 16),
    (1, 0, 80, 16),
    (0, -1, 96, 16),
    (0, 1, 112, 16),
    (-1, -1, 128, 8),
    (-1, 1, 136, 8),
    (1, -1, 144, 8),
    (1, 1, 152, 8),
)
STACK = 160
SPEC = 112
PACKED = ((0, 24), (24, 24), (48, 24), (72, 24), (96, 8), (104, 8), (112, 8), (120, 8))
MESSAGE = 128
LAST = ((72, 0), (104, 2), (128, 4))
LAST_PACKED = {0: (8, 16), 2: (56, 16), 4: (96, 8)}
OPERANDS = (
    "rhs", "pick_a", "segments", "factor",
    "stiff", "mass", "spread", "lines", "lam_all", "spec_own", "spec_in", "win_h", "win_l", "back_h", "back_l", "spec_out",
    "own_cols", "before_cols", "pick_own", "pick_place", "plane", "plane_weight", "inner",
)
STAGES = ("x", "y")
DIRECT = 64


def legendre_pair(position, degree):
    p_prev = 1.0
    p_now = position
    for order in range(2, degree + 1):
        p_next = ((2 * order - 1) * position * p_now - (order - 1) * p_prev) / order
        p_prev = p_now
        p_now = p_next
    return (p_now, p_prev)


def jacobi_eigen(matrix):
    size_n = matrix.shape[0]
    current = np.array(matrix)
    vectors = np.eye(size_n)
    for sweep in range(20):
        for row_p in range(size_n - 1):
            for row_q in range(row_p + 1, size_n):
                off_value = current[row_p, row_q]
                if abs(off_value) > 1e-300:
                    theta = (current[row_q, row_q] - current[row_p, row_p]) / (2.0 * off_value)
                    sign_t = 1.0 if theta >= 0.0 else -1.0
                    tangent = sign_t / (abs(theta) + math.sqrt(theta * theta + 1.0))
                    cosine = 1.0 / math.sqrt(tangent * tangent + 1.0)
                    sine = tangent * cosine
                    rotation = np.eye(size_n)
                    rotation[row_p, row_p] = cosine
                    rotation[row_q, row_q] = cosine
                    rotation[row_p, row_q] = sine
                    rotation[row_q, row_p] = -sine
                    current = rotation.T @ current @ rotation
                    vectors = vectors @ rotation
    return (np.array([current[idx, idx] for idx in range(size_n)]), vectors)


def gll_tables():
    degree = 7
    guesses = [
        -0.8717401485096066,
        -0.5917001814331423,
        -0.2092992179024789,
        0.2092992179024789,
        0.5917001814331423,
        0.8717401485096066,
    ]
    interior = []
    for guess in guesses:
        position = guess
        for newton in range(30):
            p_now, p_prev = legendre_pair(position, degree)
            first = degree * (position * p_now - p_prev) / (position * position - 1.0)
            second = (2.0 * position * first - degree * (degree + 1) * p_now) / (
                1.0 - position * position
            )
            position = position - first / second
        interior.append(position)
    points = np.array([-1.0] + interior + [1.0])
    values = np.array([legendre_pair(float(pt), degree)[0] for pt in points])
    weights = 2.0 / (degree * (degree + 1) * values**2)
    deriv_mat = np.zeros((8, 8))
    for left_idx in range(8):
        for right_idx in range(8):
            if left_idx != right_idx:
                deriv_mat[left_idx, right_idx] = values[left_idx] / (
                    values[right_idx] * (points[left_idx] - points[right_idx])
                )
    deriv_mat[0, 0] = -degree * (degree + 1) / 4.0
    deriv_mat[7, 7] = degree * (degree + 1) / 4.0
    stiffness = deriv_mat.T @ (weights[:, None] * deriv_mat)
    ext_stiff = np.zeros((10, 10))
    ext_stiff[1:9, 1:9] += stiffness
    ext_stiff[0:2, 0:2] += stiffness[6:8, 6:8]
    ext_stiff[8:10, 8:10] += stiffness[0:2, 0:2]
    ext_mass = np.zeros(10)
    ext_mass[1:9] += weights
    ext_mass[0:2] += weights[6:8]
    ext_mass[8:10] += weights[0:2]
    inv_root = 1.0 / np.sqrt(ext_mass)
    eigen_vals, eigen_vecs = jacobi_eigen(inv_root[:, None] * ext_stiff * inv_root[None, :])
    eigen_basis = inv_root[:, None] * eigen_vecs
    return stiffness, weights, eigen_basis, eigen_vals


def round_up(count, unit):
    return -(-count // unit) * unit


def stack_map(taken, placed, size_from, size_to):
    pick = np.zeros((STACK, size_from * size_from))
    place = np.zeros((size_to * size_to, STACK))
    for off_x, off_y, start, _ in ((0, 0, 0, OWN),) + SLOTS:
        row = start
        pairs_x = list(zip(taken[off_x], placed[off_x]))
        pairs_y = list(zip(taken[off_y], placed[off_y]))
        pairs = [(one, two) for one in pairs_x for two in pairs_y]
        if off_x == 0 and off_y != 0:
            pairs = [(one, two) for two in pairs_y for one in pairs_x]
        if off_x != 0 and off_y != 0:
            pairs = pairs + pairs
        for (from_x, to_x), (from_y, to_y) in pairs:
            pick[row, from_x * size_from + from_y] = 1.0
            place[to_x * size_to + to_y, row] = 1.0
            row += 1
    return pick, place


def halves(matrix):
    exact = np.asarray(matrix, np.float32)
    high = exact.astype(jnp.bfloat16)
    low = (exact - high.astype(np.float32)).astype(jnp.bfloat16)
    return high, low


def left_split(matrix):
    high, low = halves(matrix)
    return np.concatenate([high, low, high], axis=1)


def left_exact(matrix):
    return np.concatenate([np.asarray(matrix).astype(jnp.bfloat16)] * 3, axis=1)


def constants(elements, coarse_count):
    stiffness, weights, basis, lam = gll_tables()
    stiffness = np.asarray(stiffness, np.float32).astype(np.float64)
    weights = np.asarray(weights, np.float32).astype(np.float64)
    basis = np.asarray(basis, np.float32).astype(np.float64)
    lam = np.asarray(lam, np.float32).astype(np.float64)
    points = 7 * elements
    z_pad = round_up(points, 128)
    s_pad = round_up(10 * elements, 128)
    every = list(range(8))
    pick_a, place_a = stack_map(
        {-1: [6, 7], 0: every, 1: [0, 1]}, {-1: [0, 1], 0: list(range(1, 9)), 1: [8, 9]}, 8, 10
    )
    pick_s, place_s = stack_map(
        {-1: [8, 9], 0: list(range(1, 9)), 1: [0, 1]}, {-1: [0, 1], 0: every, 1: [6, 7]}, 10, 8
    )
    basis_two = np.kron(basis, basis)
    spectral_in = np.zeros((SPEC, STACK))
    spectral_in[:100] = basis_two.T @ place_a
    spectral_out = np.zeros((STACK, SPEC))
    spectral_out[:, :100] = pick_s @ basis_two
    plane = np.kron(stiffness, np.diag(weights)) + np.kron(np.diag(weights), stiffness)
    plane_weight = np.kron(weights, weights)
    window = np.zeros((z_pad, s_pad))
    own_cols = np.zeros((z_pad, z_pad))
    before_cols = np.zeros((z_pad, z_pad))
    spread = np.zeros((elements, s_pad + 2 * z_pad))
    lines = np.zeros((8, max(z_pad, s_pad)))
    lines[2, 10 * elements :] = 1.0
    for elem in range(elements):
        prior = (elem - 1) % elements
        for col in range(10):
            spread[elem, col * elements + elem] = 1.0
            for row in range(10):
                window[(7 * elem - 1 + row) % points, col * elements + elem] += basis[row, col]
        for step in range(7):
            spread[elem, s_pad + 7 * elem + step] = 1.0
            spread[prior, s_pad + z_pad + 7 * elem + step] = 1.0
            lines[0, 7 * elem + step] = weights[step]
            for row in range(8):
                own_cols[(7 * elem + row) % points, 7 * elem + step] += stiffness[row, step]
        lines[1, 7 * elem] = weights[7]
        for row in range(8):
            before_cols[(7 * prior + row) % points, 7 * elem] += stiffness[row, 7]
    lam_all = np.zeros((SPEC, s_pad))
    lam_two = (lam[:, None] + lam[None, :]).reshape(-1)
    lam_all[:100, : 10 * elements] = lam_two[:, None] + np.repeat(lam, elements)[None, :]
    segments = np.zeros((coarse_count, z_pad))
    for row in range(coarse_count):
        length = points // coarse_count
        segments[row, row * length : (row + 1) * length] = 1.0
    inner = place_a.reshape(10, 10, STACK)[1:9, 1:9].reshape(OWN, STACK)
    inner = np.concatenate([inner[:, start : start + 8] for start, _ in LAST] + [np.zeros((OWN, 8))], axis=1)
    window_high, window_low = halves(window)
    back_high, back_low = halves(window.T)
    single = lambda value: np.asarray(value, np.float32)
    return {
        "pick_a": left_exact(pick_a),
        "spec_in": left_split(spectral_in[:, OWN:]),
        "spec_own": left_split(spectral_in[:, :OWN]),
        "spec_out": left_split(spectral_out),
        "pick_place": left_exact((pick_a @ place_s)[:, OWN:]),
        "pick_own": left_exact((pick_a @ place_s)[:, :OWN]),
        "plane": left_split(pick_a @ plane),
        "inner": left_exact(inner),
        "win_h": window_high,
        "win_l": window_low,
        "back_h": back_high,
        "back_l": back_low,
        "own_cols": single(own_cols),
        "before_cols": single(before_cols),
        "lam_all": single(lam_all),
        "spread": single(spread),
        "lines": single(lines),
        "segments": single(segments),
        "plane_weight": single((pick_a @ plane_weight)[:, None]),
    }


def split_two(value):
    high = value.astype(jnp.bfloat16)
    return high, (value - high.astype(jnp.float32)).astype(jnp.bfloat16)


def mul(left, right):
    return jnp.dot(left, right, preferred_element_type=jnp.float32)


def left_mul(matrix, value):
    high, low = split_two(value)
    return mul(matrix[...], jnp.concatenate([high, high, low], axis=0))


def left_place(matrix, value):
    high = value.astype(jnp.bfloat16)
    rest = value - high.astype(jnp.float32)
    middle, low = split_two(rest)
    return mul(matrix[...], jnp.concatenate([high, middle, low], axis=0))


def right_mul(value, high_ref, low_ref):
    high, low = split_two(value)
    both = mul(jnp.concatenate([high, low], axis=0), high_ref[...])
    rows = value.shape[0]
    return both[:rows] + (mul(high, low_ref[...]) + both[rows:])


def each_other(count, act):
    if count <= 8:
        for step in range(1, count):
            act(step)
    else:

        def body(step, carry):
            act(step)
            return carry

        lax.fori_loop(1, count, body, 0)


def stage_size(stage, n_gx, n_gy):
    return {"x": n_gx, "y": n_gy, "xy": n_gx * n_gy}[stage]


def last_stages(n_gx, n_gy):
    return ("xy",) if n_gx * n_gy <= DIRECT else STAGES


def kernel(n_gx, n_gy, n_in, *refs):
    sources = refs[:n_in]
    out = refs[n_in]
    loaded = refs[n_in + 1 : 2 * n_in + 1]
    load_sem, arrived, sending, own_rows, z_high, z_low, scale, first, field_w, halo_send, halo_recv = refs[
        2 * n_in + 1 : 2 * n_in + 12
    ]
    lanes = refs[2 * n_in + 12 :]
    (
        rhs, pick_a, segments, factor,
        stiff, mass, spread, lines, lam_all, spec_own, spec_in, win_h, win_l, back_h, back_l, spec_out,
        own_cols, before_cols, pick_own, pick_place, plane, plane_weight, inner,
    ) = loaded
    loads = [
        pltpu.make_async_copy(source, target, load_sem.at[index])
        for index, (source, target) in enumerate(zip(sources, loaded))
    ]
    for load in loads[:4]:
        load.start()

    me_x, me_y = lax.axis_index("gx"), lax.axis_index("gy")
    points = rhs.shape[2]
    z_pad, s_pad = win_h.shape

    def beside(off_x, off_y):
        return (lax.rem(me_x + off_x + n_gx, n_gx), lax.rem(me_y + off_y + n_gy, n_gy))

    def each_offset(stage, act):
        if stage == "xy":
            for off_x in range(n_gx):
                for off_y in range(n_gy):
                    if off_x or off_y:
                        act(off_x, off_y)
        elif stage == "x":
            each_other(n_gx, lambda step: act(step, 0))
        else:
            each_other(n_gy, lambda step: act(0, step))

    barrier = pltpu.get_barrier_semaphore()

    def greet(off_x, off_y):
        pl.semaphore_signal(barrier, inc=1, device_id=beside(off_x, off_y), device_id_type=MESH)

    greeted = 0
    for stage in last_stages(n_gx, n_gy):
        each_offset(stage, greet)
        greeted += stage_size(stage, n_gx, n_gy) - 1
    if last_stages(n_gx, n_gy) == STAGES:
        for off_x, off_y, _, _ in SLOTS[4:]:
            greet(off_x, off_y)
            greeted += 1

    def halo_copy(turn, slot, start, rows):
        off_x, off_y, _, _ = SLOTS[slot]
        return pltpu.make_async_remote_copy(
            src_ref=sending.at[turn, pl.ds(start, rows)],
            dst_ref=arrived.at[turn, pl.ds(start, rows)],
            send_sem=halo_send.at[turn, slot],
            recv_sem=halo_recv.at[turn, slot],
            device_id=beside(-off_x, -off_y),
            device_id_type=MESH,
        )

    def halo_copies(turn):
        if turn == ROUNDS - 1:
            return [halo_copy(turn, slot, *LAST_PACKED[slot]) for _, slot in LAST]
        return [halo_copy(turn, slot, *PACKED[slot]) for slot in (4, 5, 6, 7, 0, 1, 2, 3)]

    tile_row = lax.broadcasted_iota(jnp.int32, (8, 128), 0)
    tile_lane = lax.broadcasted_iota(jnp.int32, (8, 128), 1)

    def halo_start(turn, rows):
        for slot, (_, _, start, count) in enumerate(SLOTS):
            at = PACKED[slot][0]
            if turn == ROUNDS - 1 and slot not in LAST_PACKED:
                continue
            if count == 8:
                part = rows[start : start + 8]
                sending[turn, pl.ds(at, 8)] = jnp.where(tile_row < 4, part[:, :128], part[:, 128:])
            else:
                sending[turn, pl.ds(at, 16)] = rows[start : start + 16, :128]
                sending[turn, pl.ds(at + 16, 8)] = rows[start : start + 8, 128:] + pltpu.roll(
                    rows[start + 8 : start + 16, 128:], 64, 1
                )
        for copy in halo_copies(turn):
            copy.start()
        own_rows[turn] = rows[:OWN]

    def left_half(tile):
        return jnp.where(tile_lane < 64, tile, 0.0)

    def corner_rows(turn, slot):
        tile = arrived[turn, pl.ds(PACKED[slot][0], 8)]
        upper = jnp.where(tile_row < 4, tile, 0.0)
        return jnp.concatenate([upper, jnp.where(tile_row < 4, 0.0, tile)], axis=1)

    def first_rows(turn, slot):
        at = PACKED[slot][0]
        tail = arrived[turn, pl.ds(at + 16, 8)]
        return jnp.concatenate([arrived[turn, pl.ds(at, 8)], left_half(tail)], axis=1)

    def second_rows(turn, slot):
        at = PACKED[slot][0]
        tail = pltpu.roll(arrived[turn, pl.ds(at + 16, 8)], 64, 1)
        return jnp.concatenate([arrived[turn, pl.ds(at + 8, 8)], left_half(tail)], axis=1)

    def halo_wait(turn):
        for copy in halo_copies(turn):
            copy.wait_recv()

    def stack(turn):
        parts = []
        for slot in range(4):
            parts += [first_rows(turn, slot), second_rows(turn, slot)]
        parts += [corner_rows(turn, slot) for slot in range(4, 8)]
        return jnp.concatenate(parts, axis=0)

    def halo_drain(turn):
        for copy in halo_copies(turn):
            copy.wait_send()

    def slot_of(stage, off_x, off_y):
        at_x, at_y = beside(off_x, off_y)
        return {"x": at_x, "y": at_y, "xy": at_x * n_gy + at_y}[stage]

    class Lane:
        def __init__(self, stages, buffers):
            self.legs = [(stage,) + tuple(buffers[3 * at : 3 * at + 3]) for at, stage in enumerate(stages)]

        def copy(self, leg, off_x, off_y, slot):
            stage, buf, send, recv = leg
            index = off_x * n_gy + off_y if stage == "xy" else off_x + off_y
            return pltpu.make_async_remote_copy(
                src_ref=buf.at[slot],
                dst_ref=buf.at[slot],
                send_sem=send.at[index],
                recv_sem=recv.at[index],
                device_id=beside(off_x, off_y),
                device_id_type=MESH,
            )

        def put(self, leg, value):
            mine = slot_of(leg[0], 0, 0)
            leg[1][mine] = value
            each_offset(leg[0], lambda x, y: self.copy(leg, x, y, mine).start())

        def take(self, leg):
            each_offset(leg[0], lambda x, y: self.copy(leg, x, y, slot_of(leg[0], -x, -y)).wait_recv())
            return jnp.sum(leg[1][...], axis=0)

        def start(self, value):
            self.put(self.legs[0], value)

        def middle(self):
            for before, after in zip(self.legs, self.legs[1:]):
                self.put(after, self.take(before))

        def finish(self):
            return self.take(self.legs[-1])

        def drain(self):
            for leg in self.legs:
                mine = slot_of(leg[0], 0, 0)
                each_offset(leg[0], lambda x, y: self.copy(leg, x, y, mine).wait_send())

    coarse = [Lane(STAGES, lanes[:6]), Lane(STAGES, lanes[6:12])]
    sums = Lane(last_stages(n_gx, n_gy), lanes[12:])

    point = lax.broadcasted_iota(jnp.int32, (OWN, z_pad), 0)
    at_x, at_y = point // 8, point % 8
    coarse_mask = (at_x >= 1) & (at_x <= 6) & (at_y >= 1) & (at_y <= 6)

    def coarse_start(turn, rows):
        line = jnp.sum(jnp.where(coarse_mask, rows, 0.0), axis=0, keepdims=True)
        held = jnp.sum(segments[...] * line, axis=1, keepdims=True)
        coarse[turn].start(jnp.sum(factor[...] * held, axis=0, keepdims=True))

    def coarse_finish(turn):
        total = coarse[turn].finish()
        values = jnp.sum(factor[...] * total, axis=1, keepdims=True)
        line = jnp.sum(segments[...] * values, axis=0, keepdims=True)
        return jnp.where(coarse_mask, line, 0.0)

    first[...] = jnp.zeros_like(first)
    for load in loads[:4]:
        load.wait()
    for row in range(7):
        first[pl.ds(8 * row, 7), pl.ds(0, points)] = rhs[row]
    right = first[...]
    rows = left_place(pick_a, right)
    pl.semaphore_wait(barrier, greeted)
    halo_start(0, rows)
    coarse_start(0, right)

    for load in loads[4:]:
        load.start()
    for load in loads[4:16]:
        load.wait()

    def spread_out(coef, start, size):
        return jnp.dot(
            jnp.broadcast_to(coef[0], (8, coef.shape[2])), spread[:, start : start + size],
            precision=exact_mode, preferred_element_type=jnp.float32,
        )[0:1]

    stiff_s, mass_s = spread_out(stiff, 0, s_pad), spread_out(mass, 0, s_pad)
    scale[...] = 1.0 / (stiff_s * lam_all[...] + (mass_s + lines[2:3, :s_pad]))

    def prepare_elements():
        for load in loads[16:]:
            load.wait()
        stiff_own, stiff_before = spread_out(stiff, s_pad, z_pad), spread_out(stiff, s_pad + z_pad, z_pad)
        mass_own, mass_before = spread_out(mass, s_pad, z_pad), spread_out(mass, s_pad + z_pad, z_pad)
        weight_own, weight_before = lines[0:1, :z_pad], lines[1:2, :z_pad]
        line_mass = mass_own * weight_own + mass_before * weight_before
        diagonal = lax.broadcasted_iota(jnp.int32, (z_pad, z_pad), 0) == lax.broadcasted_iota(
            jnp.int32, (z_pad, z_pad), 1
        )
        along = own_cols[...] * stiff_own + before_cols[...] * stiff_before
        z_high[...], z_low[...] = split_two(along + jnp.where(diagonal, line_mass, 0.0))
        return stiff_own * weight_own + stiff_before * weight_before

    def element(turn):
        held = left_place(pick_own, own_rows[turn])
        halo_wait(turn)
        wide = held + left_place(pick_place, stack(turn))
        field = wide[:OWN]
        result = left_mul(plane, field * line_stiff) + plane_weight[...] * right_mul(
            wide, z_high, z_low
        )
        return field, result

    def precondition(turn):
        held = left_mul(spec_own, own_rows[2 * turn])
        halo_wait(2 * turn)
        spectral = right_mul(held + left_mul(spec_in, stack(2 * turn)), win_h, win_l) * scale[...]
        coarse[turn].middle()
        result = left_mul(spec_out, right_mul(spectral, back_h, back_l))
        halo_start(2 * turn + 1, result)
        plate = coarse_finish(turn)
        own_rows[2 * turn + 1] = result[:OWN] + plate
        halo_drain(2 * turn)
        coarse[turn].drain()

    def dot_line(left, other):
        return jnp.sum(left * other, axis=0, keepdims=True)

    def gathered(turn, own):
        parts = [second_rows(turn, 0), second_rows(turn, 2), corner_rows(turn, 4)]
        return own + left_place(inner, jnp.concatenate(parts + [jnp.zeros_like(parts[0])], axis=0))

    owned = (at_x < 7) & (at_y < 7)

    precondition(0)
    line_stiff = prepare_elements()
    z_field, w_rows = element(1)
    halo_start(2, w_rows)
    w_local = w_rows[:OWN]
    coarse_start(1, w_local)
    precondition(1)
    field_w[...] = gathered(2, w_local)
    v_field, av_rows = element(3)
    halo_start(4, av_rows)
    av_local = av_rows[:OWN]
    partial = jnp.concatenate(
        [
            dot_line(right, jnp.where(owned, z_field, 0.0)),
            dot_line(z_field, w_local),
            dot_line(right, jnp.where(owned, v_field, 0.0)),
            dot_line(v_field, w_local),
            dot_line(v_field, av_local),
            dot_line(z_field, av_local),
            jnp.zeros((2, z_pad), jnp.float32),
        ],
        axis=0,
    )
    at_row = lax.broadcasted_iota(jnp.int32, (8, 128), 0)
    at_lane = lax.broadcasted_iota(jnp.int32, (8, 128), 1)
    packed = jnp.where(at_row == at_lane, jnp.sum(partial, axis=1, keepdims=True), 0.0)
    sums.start(jnp.sum(packed, axis=0, keepdims=True))
    sums.middle()
    for turn in (1, 3, 4):
        halo_drain(turn)
    sums.drain()
    halo_wait(4)
    av_field = gathered(4, av_local)
    w_field = field_w[...]
    totals = sums.finish()
    rz, zw, rv, vw, vav, zav = [totals[:, lane : lane + 1] for lane in range(6)]
    step_0 = rz / zw
    rho_1 = rz - step_0 * (rv + zw) + step_0 * step_0 * vw
    momentum = rho_1 / rz
    curve = (
        zw - step_0 * (vw + zav) + step_0 * step_0 * vav
        + momentum * ((zw - step_0 * vw) + (zw - step_0 * zav))
        + momentum * momentum * zw
    )
    step_1 = rho_1 / curve
    next_dir = (z_field - step_0 * v_field) + momentum * z_field
    next_image = (w_field - step_0 * av_field) + momentum * w_field
    final_x = step_0 * z_field + step_1 * next_dir
    final_r = (right - step_0 * w_field) - step_1 * next_image
    out[0] = final_x
    out[1] = final_r


def move(both, to_x, to_r):
    points = to_x.shape[2]
    for row in range(7):
        to_x[row] = both[0, pl.ds(8 * row, 7), pl.ds(0, points)]
        to_r[row] = both[1, pl.ds(8 * row, 7), pl.ds(0, points)]


def local(n_gx, n_gy, right_side, stiff_coef, mass_coef, coarse_factor):
    elements = stiff_coef.shape[2]
    coarse_count, coarse_all = coarse_factor.shape
    tables = {name: jnp.asarray(table) for name, table in constants(elements, coarse_count).items()}
    tables.update(rhs=right_side, stiff=stiff_coef, mass=mass_coef, factor=coarse_factor)
    operands = [tables[name] for name in OPERANDS]
    z_pad = round_up(7 * elements, 128)
    s_pad = round_up(10 * elements, 128)
    dma = pltpu.SemaphoreType.DMA
    single = jnp.float32
    whole = pl.BlockSpec(memory_space=pltpu.VMEM)
    shape = jax.ShapeDtypeStruct(right_side.shape, single)
    lanes = []
    last = last_stages(n_gx, n_gy)
    for width, stages in ((coarse_all, STAGES), (coarse_all, STAGES), (128, last)):
        for stage in stages:
            size = stage_size(stage, n_gx, n_gy)
            lanes += [pltpu.VMEM((size, 1, width), single), dma((size,)), dma((size,))]
    result = pl.pallas_call(
        functools.partial(kernel, n_gx, n_gy, len(operands)),
        out_shape=jax.ShapeDtypeStruct((2, OWN, z_pad), single),
        in_specs=[pl.BlockSpec(memory_space=pltpu.HBM)] * len(operands),
        out_specs=whole,
        scratch_shapes=[pltpu.VMEM(operand.shape, operand.dtype) for operand in operands]
        + [
            dma((len(operands),)),
            pltpu.VMEM((ROUNDS, MESSAGE, 128), single),
            pltpu.VMEM((ROUNDS, MESSAGE, 128), single),
            pltpu.VMEM((ROUNDS, OWN, z_pad), single),
            pltpu.VMEM((z_pad, z_pad), jnp.bfloat16),
            pltpu.VMEM((z_pad, z_pad), jnp.bfloat16),
            pltpu.VMEM((SPEC, s_pad), single),
            pltpu.VMEM((OWN, z_pad), single),
            pltpu.VMEM((OWN, z_pad), single),
            dma((ROUNDS, 8)),
            dma((ROUNDS, 8)),
        ]
        + lanes,
        compiler_params=pltpu.CompilerParams(
            collective_id=0, has_side_effects=True, vmem_limit_bytes=60 * 1024 * 1024
        ),
    )(*operands)
    return pl.pallas_call(
        move,
        out_shape=(shape, shape),
        in_specs=[whole],
        out_specs=(whole, whole),
        compiler_params=pltpu.CompilerParams(vmem_limit_bytes=60 * 1024 * 1024),
    )(result)


def solution(mesh):
    placed = (P("gx", "gy", None), P("gx", "gy", None), P("gx", "gy", None), P(("gx", "gy"), None))
    return jax.shard_map(
        functools.partial(local, mesh.shape["gx"], mesh.shape["gy"]),
        mesh=mesh,
        in_specs=placed,
        out_specs=(P("gx", "gy", None), P("gx", "gy", None)),
        check_vma=False,
    )
```

```python
import functools
import math

import jax
import jax.numpy as jnp
import numpy as np
from jax import lax
from jax.experimental import pallas as pl
from jax.experimental.pallas import tpu as pltpu
from jax.sharding import PartitionSpec as P

MESH = pl.DeviceIdType.MESH
exact_mode = lax.Precision.HIGHEST
ROUNDS = 5

OWN = 64
SLOTS = (
    (-1, 0, 64, 16),
    (1, 0, 80, 16),
    (0, -1, 96, 16),
    (0, 1, 112, 16),
    (-1, -1, 128, 8),
    (-1, 1, 136, 8),
    (1, -1, 144, 8),
    (1, 1, 152, 8),
)
STACK = 160
SPEC = 112
PACKED = ((0, 24), (24, 24), (48, 24), (72, 24), (96, 8), (104, 8), (112, 8), (120, 8))
MESSAGE = 128
LAST = ((72, 0), (104, 2), (128, 4))
LAST_PACKED = {0: (8, 16), 2: (56, 16), 4: (96, 8)}
OPERANDS = (
    "rhs", "pick_a", "segments", "factor",
    "stiff", "mass", "spread", "lines", "lam_all", "spec_own", "spec_in", "win_h", "win_l", "back_h", "back_l", "spec_out",
    "own_cols", "before_cols", "pick_own", "pick_place", "plane", "plane_weight", "inner",
)
STAGES = ("x", "y")
DIRECT = 64


def legendre_pair(position, degree):
    p_prev = 1.0
    p_now = position
    for order in range(2, degree + 1):
        p_next = ((2 * order - 1) * position * p_now - (order - 1) * p_prev) / order
        p_prev = p_now
        p_now = p_next
    return (p_now, p_prev)


def jacobi_eigen(matrix):
    size_n = matrix.shape[0]
    current = np.array(matrix)
    vectors = np.eye(size_n)
    for sweep in range(20):
        for row_p in range(size_n - 1):
            for row_q in range(row_p + 1, size_n):
                off_value = current[row_p, row_q]
                if abs(off_value) > 1e-300:
                    theta = (current[row_q, row_q] - current[row_p, row_p]) / (2.0 * off_value)
                    sign_t = 1.0 if theta >= 0.0 else -1.0
                    tangent = sign_t / (abs(theta) + math.sqrt(theta * theta + 1.0))
                    cosine = 1.0 / math.sqrt(tangent * tangent + 1.0)
                    sine = tangent * cosine
                    rotation = np.eye(size_n)
                    rotation[row_p, row_p] = cosine
                    rotation[row_q, row_q] = cosine
                    rotation[row_p, row_q] = sine
                    rotation[row_q, row_p] = -sine
                    current = rotation.T @ current @ rotation
                    vectors = vectors @ rotation
    return (np.array([current[idx, idx] for idx in range(size_n)]), vectors)


def gll_tables():
    degree = 7
    guesses = [
        -0.8717401485096066,
        -0.5917001814331423,
        -0.2092992179024789,
        0.2092992179024789,
        0.5917001814331423,
        0.8717401485096066,
    ]
    interior = []
    for guess in guesses:
        position = guess
        for newton in range(30):
            p_now, p_prev = legendre_pair(position, degree)
            first = degree * (position * p_now - p_prev) / (position * position - 1.0)
            second = (2.0 * position * first - degree * (degree + 1) * p_now) / (
                1.0 - position * position
            )
            position = position - first / second
        interior.append(position)
    points = np.array([-1.0] + interior + [1.0])
    values = np.array([legendre_pair(float(pt), degree)[0] for pt in points])
    weights = 2.0 / (degree * (degree + 1) * values**2)
    deriv_mat = np.zeros((8, 8))
    for left_idx in range(8):
        for right_idx in range(8):
            if left_idx != right_idx:
                deriv_mat[left_idx, right_idx] = values[left_idx] / (
                    values[right_idx] * (points[left_idx] - points[right_idx])
                )
    deriv_mat[0, 0] = -degree * (degree + 1) / 4.0
    deriv_mat[7, 7] = degree * (degree + 1) / 4.0
    stiffness = deriv_mat.T @ (weights[:, None] * deriv_mat)
    ext_stiff = np.zeros((10, 10))
    ext_stiff[1:9, 1:9] += stiffness
    ext_stiff[0:2, 0:2] += stiffness[6:8, 6:8]
    ext_stiff[8:10, 8:10] += stiffness[0:2, 0:2]
    ext_mass = np.zeros(10)
    ext_mass[1:9] += weights
    ext_mass[0:2] += weights[6:8]
    ext_mass[8:10] += weights[0:2]
    inv_root = 1.0 / np.sqrt(ext_mass)
    eigen_vals, eigen_vecs = jacobi_eigen(inv_root[:, None] * ext_stiff * inv_root[None, :])
    eigen_basis = inv_root[:, None] * eigen_vecs
    return stiffness, weights, eigen_basis, eigen_vals


def round_up(count, unit):
    return -(-count // unit) * unit


def stack_map(taken, placed, size_from, size_to):
    pick = np.zeros((STACK, size_from * size_from))
    place = np.zeros((size_to * size_to, STACK))
    for off_x, off_y, start, _ in ((0, 0, 0, OWN),) + SLOTS:
        row = start
        pairs_x = list(zip(taken[off_x], placed[off_x]))
        pairs_y = list(zip(taken[off_y], placed[off_y]))
        pairs = [(one, two) for one in pairs_x for two in pairs_y]
        if off_x == 0 and off_y != 0:
            pairs = [(one, two) for two in pairs_y for one in pairs_x]
        if off_x != 0 and off_y != 0:
            pairs = pairs + pairs
        for (from_x, to_x), (from_y, to_y) in pairs:
            pick[row, from_x * size_from + from_y] = 1.0
            place[to_x * size_to + to_y, row] = 1.0
            row += 1
    return pick, place


def halves(matrix):
    exact = np.asarray(matrix, np.float32)
    high = exact.astype(jnp.bfloat16)
    low = (exact - high.astype(np.float32)).astype(jnp.bfloat16)
    return high, low


def left_split(matrix):
    high, low = halves(matrix)
    return np.concatenate([high, low, high], axis=1)


def left_whole(matrix):
    return np.concatenate([np.asarray(matrix).astype(jnp.bfloat16)] * 2, axis=1)


def constants(elements, coarse_count):
    stiffness, weights, basis, lam = gll_tables()
    stiffness = np.asarray(stiffness, np.float32).astype(np.float64)
    weights = np.asarray(weights, np.float32).astype(np.float64)
    basis = np.asarray(basis, np.float32).astype(np.float64)
    lam = np.asarray(lam, np.float32).astype(np.float64)
    points = 7 * elements
    z_pad = round_up(points, 128)
    s_pad = round_up(10 * elements, 128)
    every = list(range(8))
    pick_a, place_a = stack_map(
        {-1: [6, 7], 0: every, 1: [0, 1]}, {-1: [0, 1], 0: list(range(1, 9)), 1: [8, 9]}, 8, 10
    )
    pick_s, place_s = stack_map(
        {-1: [8, 9], 0: list(range(1, 9)), 1: [0, 1]}, {-1: [0, 1], 0: every, 1: [6, 7]}, 10, 8
    )
    basis_two = np.kron(basis, basis)
    spectral_in = np.zeros((SPEC, STACK))
    spectral_in[:100] = basis_two.T @ place_a
    spectral_out = np.zeros((STACK, SPEC))
    spectral_out[:, :100] = pick_s @ basis_two
    plane = np.kron(stiffness, np.diag(weights)) + np.kron(np.diag(weights), stiffness)
    plane_weight = np.kron(weights, weights)
    window = np.zeros((z_pad, s_pad))
    own_cols = np.zeros((z_pad, z_pad))
    before_cols = np.zeros((z_pad, z_pad))
    spread = np.zeros((elements, s_pad + 2 * z_pad))
    lines = np.zeros((8, max(z_pad, s_pad)))
    lines[2, 10 * elements :] = 1.0
    for elem in range(elements):
        prior = (elem - 1) % elements
        for col in range(10):
            spread[elem, col * elements + elem] = 1.0
            for row in range(10):
                window[(7 * elem - 1 + row) % points, col * elements + elem] += basis[row, col]
        for step in range(7):
            spread[elem, s_pad + 7 * elem + step] = 1.0
            spread[prior, s_pad + z_pad + 7 * elem + step] = 1.0
            lines[0, 7 * elem + step] = weights[step]
            for row in range(8):
                own_cols[(7 * elem + row) % points, 7 * elem + step] += stiffness[row, step]
        lines[1, 7 * elem] = weights[7]
        for row in range(8):
            before_cols[(7 * prior + row) % points, 7 * elem] += stiffness[row, 7]
    lam_all = np.zeros((SPEC, s_pad))
    lam_two = (lam[:, None] + lam[None, :]).reshape(-1)
    lam_all[:100, : 10 * elements] = lam_two[:, None] + np.repeat(lam, elements)[None, :]
    segments = np.zeros((coarse_count, z_pad))
    for row in range(coarse_count):
        length = points // coarse_count
        segments[row, row * length : (row + 1) * length] = 1.0
    inner = place_a.reshape(10, 10, STACK)[1:9, 1:9].reshape(OWN, STACK)
    inner = np.concatenate([inner[:, start : start + 8] for start, _ in LAST] + [np.zeros((OWN, 8))], axis=1)
    window_high, window_low = halves(window)
    back_high, back_low = halves(window.T)
    single = lambda value: np.asarray(value, np.float32)
    return {
        "pick_a": left_whole(pick_a),
        "spec_in": left_split(spectral_in[:, OWN:]),
        "spec_own": left_split(spectral_in[:, :OWN]),
        "spec_out": left_split(spectral_out),
        "pick_place": left_whole((pick_a @ place_s)[:, OWN:]),
        "pick_own": left_whole((pick_a @ place_s)[:, :OWN]),
        "plane": left_split(pick_a @ plane),
        "inner": left_whole(inner),
        "win_h": window_high,
        "win_l": window_low,
        "back_h": back_high,
        "back_l": back_low,
        "own_cols": single(own_cols),
        "before_cols": single(before_cols),
        "lam_all": single(lam_all),
        "spread": single(spread),
        "lines": single(lines),
        "segments": single(segments),
        "plane_weight": single((pick_a @ plane_weight)[:, None]),
    }


def split_two(value):
    high = value.astype(jnp.bfloat16)
    return high, (value - high.astype(jnp.float32)).astype(jnp.bfloat16)


def mul(left, right):
    return jnp.dot(left, right, preferred_element_type=jnp.float32)


def left_mul(matrix, value):
    high, low = split_two(value)
    return mul(matrix[...], jnp.concatenate([high, high, low], axis=0))


def left_place(matrix, value):
    return mul(matrix[...], jnp.concatenate(split_two(value), axis=0))


def right_mul(value, high_ref, low_ref):
    high, low = split_two(value)
    both = mul(jnp.concatenate([high, low], axis=0), high_ref[...])
    rows = value.shape[0]
    return both[:rows] + (mul(high, low_ref[...]) + both[rows:])


def each_other(count, act):
    if count <= 8:
        for step in range(1, count):
            act(step)
    else:

        def body(step, carry):
            act(step)
            return carry

        lax.fori_loop(1, count, body, 0)


def stage_size(stage, n_gx, n_gy):
    return {"x": n_gx, "y": n_gy, "xy": n_gx * n_gy}[stage]


def last_stages(n_gx, n_gy):
    return ("xy",) if n_gx * n_gy <= DIRECT else STAGES


def kernel(n_gx, n_gy, n_in, *refs):
    sources = refs[:n_in]
    out = refs[n_in]
    loaded = refs[n_in + 1 : 2 * n_in + 1]
    load_sem, arrived, sending, own_rows, z_high, z_low, scale, first, field_w, halo_send, halo_recv = refs[
        2 * n_in + 1 : 2 * n_in + 12
    ]
    lanes = refs[2 * n_in + 12 :]
    (
        rhs, pick_a, segments, factor,
        stiff, mass, spread, lines, lam_all, spec_own, spec_in, win_h, win_l, back_h, back_l, spec_out,
        own_cols, before_cols, pick_own, pick_place, plane, plane_weight, inner,
    ) = loaded
    loads = [
        pltpu.make_async_copy(source, target, load_sem.at[index])
        for index, (source, target) in enumerate(zip(sources, loaded))
    ]
    for load in loads[:4]:
        load.start()

    me_x, me_y = lax.axis_index("gx"), lax.axis_index("gy")
    points = rhs.shape[2]
    z_pad, s_pad = win_h.shape

    def beside(off_x, off_y):
        return (lax.rem(me_x + off_x + n_gx, n_gx), lax.rem(me_y + off_y + n_gy, n_gy))

    def each_offset(stage, act):
        if stage == "xy":
            for off_x in range(n_gx):
                for off_y in range(n_gy):
                    if off_x or off_y:
                        act(off_x, off_y)
        elif stage == "x":
            each_other(n_gx, lambda step: act(step, 0))
        else:
            each_other(n_gy, lambda step: act(0, step))

    barrier = pltpu.get_barrier_semaphore()

    def greet(off_x, off_y):
        pl.semaphore_signal(barrier, inc=1, device_id=beside(off_x, off_y), device_id_type=MESH)

    greeted = 0
    for stage in last_stages(n_gx, n_gy):
        each_offset(stage, greet)
        greeted += stage_size(stage, n_gx, n_gy) - 1
    if last_stages(n_gx, n_gy) == STAGES:
        for off_x, off_y, _, _ in SLOTS[4:]:
            greet(off_x, off_y)
            greeted += 1

    def halo_copy(turn, slot, start, rows):
        off_x, off_y, _, _ = SLOTS[slot]
        return pltpu.make_async_remote_copy(
            src_ref=sending.at[turn, pl.ds(start, rows)],
            dst_ref=arrived.at[turn, pl.ds(start, rows)],
            send_sem=halo_send.at[turn, slot],
            recv_sem=halo_recv.at[turn, slot],
            device_id=beside(-off_x, -off_y),
            device_id_type=MESH,
        )

    def halo_copies(turn):
        if turn == ROUNDS - 1:
            return [halo_copy(turn, slot, *LAST_PACKED[slot]) for _, slot in LAST]
        return [halo_copy(turn, slot, *PACKED[slot]) for slot in (4, 5, 6, 7, 0, 1, 2, 3)]

    tile_row = lax.broadcasted_iota(jnp.int32, (8, 128), 0)
    tile_lane = lax.broadcasted_iota(jnp.int32, (8, 128), 1)

    def halo_start(turn, rows):
        for slot, (_, _, start, count) in enumerate(SLOTS):
            at = PACKED[slot][0]
            if turn == ROUNDS - 1 and slot not in LAST_PACKED:
                continue
            if count == 8:
                part = rows[start : start + 8]
                sending[turn, pl.ds(at, 8)] = jnp.where(tile_row < 4, part[:, :128], part[:, 128:])
            else:
                sending[turn, pl.ds(at, 16)] = rows[start : start + 16, :128]
                sending[turn, pl.ds(at + 16, 8)] = rows[start : start + 8, 128:] + pltpu.roll(
                    rows[start + 8 : start + 16, 128:], 64, 1
                )
        for copy in halo_copies(turn):
            copy.start()
        own_rows[turn] = rows[:OWN]

    def left_half(tile):
        return jnp.where(tile_lane < 64, tile, 0.0)

    def corner_rows(turn, slot):
        tile = arrived[turn, pl.ds(PACKED[slot][0], 8)]
        upper = jnp.where(tile_row < 4, tile, 0.0)
        return jnp.concatenate([upper, jnp.where(tile_row < 4, 0.0, tile)], axis=1)

    def first_rows(turn, slot):
        at = PACKED[slot][0]
        tail = arrived[turn, pl.ds(at + 16, 8)]
        return jnp.concatenate([arrived[turn, pl.ds(at, 8)], left_half(tail)], axis=1)

    def second_rows(turn, slot):
        at = PACKED[slot][0]
        tail = pltpu.roll(arrived[turn, pl.ds(at + 16, 8)], 64, 1)
        return jnp.concatenate([arrived[turn, pl.ds(at + 8, 8)], left_half(tail)], axis=1)

    def halo_wait(turn):
        for copy in halo_copies(turn):
            copy.wait_recv()

    def stack(turn):
        parts = []
        for slot in range(4):
            parts += [first_rows(turn, slot), second_rows(turn, slot)]
        parts += [corner_rows(turn, slot) for slot in range(4, 8)]
        return jnp.concatenate(parts, axis=0)

    def halo_drain(turn):
        for copy in halo_copies(turn):
            copy.wait_send()

    def slot_of(stage, off_x, off_y):
        at_x, at_y = beside(off_x, off_y)
        return {"x": at_x, "y": at_y, "xy": at_x * n_gy + at_y}[stage]

    class Lane:
        def __init__(self, stages, buffers):
            self.legs = [(stage,) + tuple(buffers[3 * at : 3 * at + 3]) for at, stage in enumerate(stages)]

        def copy(self, leg, off_x, off_y, slot):
            stage, buf, send, recv = leg
            index = off_x * n_gy + off_y if stage == "xy" else off_x + off_y
            return pltpu.make_async_remote_copy(
                src_ref=buf.at[slot],
                dst_ref=buf.at[slot],
                send_sem=send.at[index],
                recv_sem=recv.at[index],
                device_id=beside(off_x, off_y),
                device_id_type=MESH,
            )

        def put(self, leg, value):
            mine = slot_of(leg[0], 0, 0)
            leg[1][mine] = value
            each_offset(leg[0], lambda x, y: self.copy(leg, x, y, mine).start())

        def take(self, leg):
            each_offset(leg[0], lambda x, y: self.copy(leg, x, y, slot_of(leg[0], -x, -y)).wait_recv())
            return jnp.sum(leg[1][...], axis=0)

        def start(self, value):
            self.put(self.legs[0], value)

        def middle(self):
            for before, after in zip(self.legs, self.legs[1:]):
                self.put(after, self.take(before))

        def finish(self):
            return self.take(self.legs[-1])

        def drain(self):
            for leg in self.legs:
                mine = slot_of(leg[0], 0, 0)
                each_offset(leg[0], lambda x, y: self.copy(leg, x, y, mine).wait_send())

    coarse = [Lane(STAGES, lanes[:6]), Lane(STAGES, lanes[6:12])]
    sums = Lane(last_stages(n_gx, n_gy), lanes[12:])

    point = lax.broadcasted_iota(jnp.int32, (OWN, z_pad), 0)
    at_x, at_y = point // 8, point % 8
    coarse_mask = (at_x >= 1) & (at_x <= 6) & (at_y >= 1) & (at_y <= 6)

    def coarse_start(turn, rows):
        line = jnp.sum(jnp.where(coarse_mask, rows, 0.0), axis=0, keepdims=True)
        held = jnp.sum(segments[...] * line, axis=1, keepdims=True)
        coarse[turn].start(jnp.sum(factor[...] * held, axis=0, keepdims=True))

    def coarse_finish(turn):
        total = coarse[turn].finish()
        values = jnp.sum(factor[...] * total, axis=1, keepdims=True)
        line = jnp.sum(segments[...] * values, axis=0, keepdims=True)
        return jnp.where(coarse_mask, line, 0.0)

    first[...] = jnp.zeros_like(first)
    for load in loads[:4]:
        load.wait()
    for row in range(7):
        first[pl.ds(8 * row, 7), pl.ds(0, points)] = rhs[row]
    right = first[...]
    rows = left_place(pick_a, right)
    pl.semaphore_wait(barrier, greeted)
    halo_start(0, rows)
    coarse_start(0, right)

    for load in loads[4:]:
        load.start()
    for load in loads[4:16]:
        load.wait()

    def spread_out(coef, start, size):
        return jnp.dot(
            jnp.broadcast_to(coef[0], (8, coef.shape[2])), spread[:, start : start + size],
            precision=exact_mode, preferred_element_type=jnp.float32,
        )[0:1]

    stiff_s, mass_s = spread_out(stiff, 0, s_pad), spread_out(mass, 0, s_pad)
    scale[...] = 1.0 / (stiff_s * lam_all[...] + (mass_s + lines[2:3, :s_pad]))

    def prepare_elements():
        for load in loads[16:]:
            load.wait()
        stiff_own, stiff_before = spread_out(stiff, s_pad, z_pad), spread_out(stiff, s_pad + z_pad, z_pad)
        mass_own, mass_before = spread_out(mass, s_pad, z_pad), spread_out(mass, s_pad + z_pad, z_pad)
        weight_own, weight_before = lines[0:1, :z_pad], lines[1:2, :z_pad]
        line_mass = mass_own * weight_own + mass_before * weight_before
        diagonal = lax.broadcasted_iota(jnp.int32, (z_pad, z_pad), 0) == lax.broadcasted_iota(
            jnp.int32, (z_pad, z_pad), 1
        )
        along = own_cols[...] * stiff_own + before_cols[...] * stiff_before
        z_high[...], z_low[...] = split_two(along + jnp.where(diagonal, line_mass, 0.0))
        return stiff_own * weight_own + stiff_before * weight_before

    def element(turn):
        held = left_place(pick_own, own_rows[turn])
        halo_wait(turn)
        wide = held + left_place(pick_place, stack(turn))
        field = wide[:OWN]
        result = left_mul(plane, field * line_stiff) + plane_weight[...] * right_mul(
            wide, z_high, z_low
        )
        return field, result

    def precondition(turn):
        held = left_mul(spec_own, own_rows[2 * turn])
        halo_wait(2 * turn)
        spectral = right_mul(held + left_mul(spec_in, stack(2 * turn)), win_h, win_l) * scale[...]
        coarse[turn].middle()
        result = left_mul(spec_out, right_mul(spectral, back_h, back_l))
        halo_start(2 * turn + 1, result)
        plate = coarse_finish(turn)
        own_rows[2 * turn + 1] = result[:OWN] + plate
        halo_drain(2 * turn)
        coarse[turn].drain()

    def dot_line(left, other):
        return jnp.sum(left * other, axis=0, keepdims=True)

    def gathered(turn, own):
        parts = [second_rows(turn, 0), second_rows(turn, 2), corner_rows(turn, 4)]
        return own + left_place(inner, jnp.concatenate(parts + [jnp.zeros_like(parts[0])], axis=0))

    owned = (at_x < 7) & (at_y < 7)

    precondition(0)
    line_stiff = prepare_elements()
    z_field, w_rows = element(1)
    halo_start(2, w_rows)
    w_local = w_rows[:OWN]
    coarse_start(1, w_local)
    precondition(1)
    field_w[...] = gathered(2, w_local)
    v_field, av_rows = element(3)
    halo_start(4, av_rows)
    av_local = av_rows[:OWN]
    partial = jnp.concatenate(
        [
            dot_line(right, jnp.where(owned, z_field, 0.0)),
            dot_line(z_field, w_local),
            dot_line(right, jnp.where(owned, v_field, 0.0)),
            dot_line(v_field, w_local),
            dot_line(v_field, av_local),
            dot_line(z_field, av_local),
            jnp.zeros((2, z_pad), jnp.float32),
        ],
        axis=0,
    )
    at_row = lax.broadcasted_iota(jnp.int32, (8, 128), 0)
    at_lane = lax.broadcasted_iota(jnp.int32, (8, 128), 1)
    packed = jnp.where(at_row == at_lane, jnp.sum(partial, axis=1, keepdims=True), 0.0)
    sums.start(jnp.sum(packed, axis=0, keepdims=True))
    sums.middle()
    for turn in (1, 3, 4):
        halo_drain(turn)
    sums.drain()
    halo_wait(4)
    av_field = gathered(4, av_local)
    w_field = field_w[...]
    totals = sums.finish()
    rz, zw, rv, vw, vav, zav = [
        jnp.broadcast_to(totals[:, lane : lane + 1], (1, z_pad)) for lane in range(6)
    ]
    step_0 = rz / zw
    rho_1 = rz - step_0 * (rv + zw) + step_0 * step_0 * vw
    momentum = rho_1 / rz
    curve = (
        zw - step_0 * (vw + zav) + step_0 * step_0 * vav
        + momentum * ((zw - step_0 * vw) + (zw - step_0 * zav))
        + momentum * momentum * zw
    )
    step_1 = rho_1 / curve
    next_dir = (z_field - step_0 * v_field) + momentum * z_field
    next_image = (w_field - step_0 * av_field) + momentum * w_field
    final_x = step_0 * z_field + step_1 * next_dir
    final_r = (right - step_0 * w_field) - step_1 * next_image
    out[0] = final_x
    out[1] = final_r


def move(both, to_x, to_r):
    points = to_x.shape[2]
    for row in range(7):
        to_x[row] = both[0, pl.ds(8 * row, 7), pl.ds(0, points)]
        to_r[row] = both[1, pl.ds(8 * row, 7), pl.ds(0, points)]


def local(n_gx, n_gy, right_side, stiff_coef, mass_coef, coarse_factor):
    elements = stiff_coef.shape[2]
    coarse_count, coarse_all = coarse_factor.shape
    tables = {name: jnp.asarray(table) for name, table in constants(elements, coarse_count).items()}
    tables.update(rhs=right_side, stiff=stiff_coef, mass=mass_coef, factor=coarse_factor)
    operands = [tables[name] for name in OPERANDS]
    z_pad = round_up(7 * elements, 128)
    s_pad = round_up(10 * elements, 128)
    dma = pltpu.SemaphoreType.DMA
    single = jnp.float32
    whole = pl.BlockSpec(memory_space=pltpu.VMEM)
    shape = jax.ShapeDtypeStruct(right_side.shape, single)
    lanes = []
    last = last_stages(n_gx, n_gy)
    for width, stages in ((coarse_all, STAGES), (coarse_all, STAGES), (128, last)):
        for stage in stages:
            size = stage_size(stage, n_gx, n_gy)
            lanes += [pltpu.VMEM((size, 1, width), single), dma((size,)), dma((size,))]
    result = pl.pallas_call(
        functools.partial(kernel, n_gx, n_gy, len(operands)),
        out_shape=jax.ShapeDtypeStruct((2, OWN, z_pad), single),
        in_specs=[pl.BlockSpec(memory_space=pltpu.HBM)] * len(operands),
        out_specs=whole,
        scratch_shapes=[pltpu.VMEM(operand.shape, operand.dtype) for operand in operands]
        + [
            dma((len(operands),)),
            pltpu.VMEM((ROUNDS, MESSAGE, 128), single),
            pltpu.VMEM((ROUNDS, MESSAGE, 128), single),
            pltpu.VMEM((ROUNDS, OWN, z_pad), single),
            pltpu.VMEM((z_pad, z_pad), jnp.bfloat16),
            pltpu.VMEM((z_pad, z_pad), jnp.bfloat16),
            pltpu.VMEM((SPEC, s_pad), single),
            pltpu.VMEM((OWN, z_pad), single),
            pltpu.VMEM((OWN, z_pad), single),
            dma((ROUNDS, 8)),
            dma((ROUNDS, 8)),
        ]
        + lanes,
        compiler_params=pltpu.CompilerParams(
            collective_id=0, has_side_effects=True, vmem_limit_bytes=60 * 1024 * 1024
        ),
    )(*operands)
    return pl.pallas_call(
        move,
        out_shape=(shape, shape),
        in_specs=[whole],
        out_specs=(whole, whole),
        compiler_params=pltpu.CompilerParams(vmem_limit_bytes=60 * 1024 * 1024),
    )(result)


def solution(mesh):
    placed = (P("gx", "gy", None), P("gx", "gy", None), P("gx", "gy", None), P(("gx", "gy"), None))
    return jax.shard_map(
        functools.partial(local, mesh.shape["gx"], mesh.shape["gy"]),
        mesh=mesh,
        in_specs=placed,
        out_specs=(P("gx", "gy", None), P("gx", "gy", None)),
        check_vma=False,
    )
```

```python
import functools
import math

import jax
import jax.numpy as jnp
import numpy as np
from jax import lax
from jax.experimental import pallas as pl
from jax.experimental.pallas import tpu as pltpu
from jax.sharding import PartitionSpec as P

MESH = pl.DeviceIdType.MESH
exact_mode = lax.Precision.HIGHEST
ROUNDS = 5

OWN = 64
SLOTS = (
    (-1, 0, 64, 16),
    (1, 0, 80, 16),
    (0, -1, 96, 16),
    (0, 1, 112, 16),
    (-1, -1, 128, 8),
    (-1, 1, 136, 8),
    (1, -1, 144, 8),
    (1, 1, 152, 8),
)
STACK = 160
SPEC = 112
PACKED = ((0, 24), (24, 24), (48, 24), (72, 24), (96, 8), (104, 8), (112, 8), (120, 8))
MESSAGE = 128
LAST = ((72, 0), (104, 2), (128, 4))
LAST_PACKED = {0: (8, 16), 2: (56, 16), 4: (96, 8)}
OPERANDS = (
    "rhs", "pick_a", "segments", "factor",
    "stiff", "mass", "spread", "lines", "lam_all", "spec_own", "spec_in", "win_h", "win_l", "back_h", "back_l", "spec_out",
    "own_cols", "before_cols", "pick_own", "pick_place", "plane", "plane_weight", "inner",
)
STAGES = ("x", "y")
DIRECT = 64


def legendre_pair(position, degree):
    p_prev = 1.0
    p_now = position
    for order in range(2, degree + 1):
        p_next = ((2 * order - 1) * position * p_now - (order - 1) * p_prev) / order
        p_prev = p_now
        p_now = p_next
    return (p_now, p_prev)


def jacobi_eigen(matrix):
    size_n = matrix.shape[0]
    current = np.array(matrix)
    vectors = np.eye(size_n)
    for sweep in range(20):
        for row_p in range(size_n - 1):
            for row_q in range(row_p + 1, size_n):
                off_value = current[row_p, row_q]
                if abs(off_value) > 1e-300:
                    theta = (current[row_q, row_q] - current[row_p, row_p]) / (2.0 * off_value)
                    sign_t = 1.0 if theta >= 0.0 else -1.0
                    tangent = sign_t / (abs(theta) + math.sqrt(theta * theta + 1.0))
                    cosine = 1.0 / math.sqrt(tangent * tangent + 1.0)
                    sine = tangent * cosine
                    rotation = np.eye(size_n)
                    rotation[row_p, row_p] = cosine
                    rotation[row_q, row_q] = cosine
                    rotation[row_p, row_q] = sine
                    rotation[row_q, row_p] = -sine
                    current = rotation.T @ current @ rotation
                    vectors = vectors @ rotation
    return (np.array([current[idx, idx] for idx in range(size_n)]), vectors)


def gll_tables():
    degree = 7
    guesses = [
        -0.8717401485096066,
        -0.5917001814331423,
        -0.2092992179024789,
        0.2092992179024789,
        0.5917001814331423,
        0.8717401485096066,
    ]
    interior = []
    for guess in guesses:
        position = guess
        for newton in range(30):
            p_now, p_prev = legendre_pair(position, degree)
            first = degree * (position * p_now - p_prev) / (position * position - 1.0)
            second = (2.0 * position * first - degree * (degree + 1) * p_now) / (
                1.0 - position * position
            )
            position = position - first / second
        interior.append(position)
    points = np.array([-1.0] + interior + [1.0])
    values = np.array([legendre_pair(float(pt), degree)[0] for pt in points])
    weights = 2.0 / (degree * (degree + 1) * values**2)
    deriv_mat = np.zeros((8, 8))
    for left_idx in range(8):
        for right_idx in range(8):
            if left_idx != right_idx:
                deriv_mat[left_idx, right_idx] = values[left_idx] / (
                    values[right_idx] * (points[left_idx] - points[right_idx])
                )
    deriv_mat[0, 0] = -degree * (degree + 1) / 4.0
    deriv_mat[7, 7] = degree * (degree + 1) / 4.0
    stiffness = deriv_mat.T @ (weights[:, None] * deriv_mat)
    ext_stiff = np.zeros((10, 10))
    ext_stiff[1:9, 1:9] += stiffness
    ext_stiff[0:2, 0:2] += stiffness[6:8, 6:8]
    ext_stiff[8:10, 8:10] += stiffness[0:2, 0:2]
    ext_mass = np.zeros(10)
    ext_mass[1:9] += weights
    ext_mass[0:2] += weights[6:8]
    ext_mass[8:10] += weights[0:2]
    inv_root = 1.0 / np.sqrt(ext_mass)
    eigen_vals, eigen_vecs = jacobi_eigen(inv_root[:, None] * ext_stiff * inv_root[None, :])
    eigen_basis = inv_root[:, None] * eigen_vecs
    return stiffness, weights, eigen_basis, eigen_vals


def round_up(count, unit):
    return -(-count // unit) * unit


def stack_map(taken, placed, size_from, size_to):
    pick = np.zeros((STACK, size_from * size_from))
    place = np.zeros((size_to * size_to, STACK))
    for off_x, off_y, start, _ in ((0, 0, 0, OWN),) + SLOTS:
        row = start
        pairs_x = list(zip(taken[off_x], placed[off_x]))
        pairs_y = list(zip(taken[off_y], placed[off_y]))
        pairs = [(one, two) for one in pairs_x for two in pairs_y]
        if off_x == 0 and off_y != 0:
            pairs = [(one, two) for two in pairs_y for one in pairs_x]
        if off_x != 0 and off_y != 0:
            pairs = pairs + pairs
        for (from_x, to_x), (from_y, to_y) in pairs:
            pick[row, from_x * size_from + from_y] = 1.0
            place[to_x * size_to + to_y, row] = 1.0
            row += 1
    return pick, place


def halves(matrix):
    exact = np.asarray(matrix, np.float32)
    high = exact.astype(jnp.bfloat16)
    low = (exact - high.astype(np.float32)).astype(jnp.bfloat16)
    return high, low


def left_split(matrix):
    high, low = halves(matrix)
    return np.concatenate([high, low, high], axis=1)


def left_whole(matrix):
    return np.concatenate([np.asarray(matrix).astype(jnp.bfloat16)] * 2, axis=1)


def constants(elements, coarse_count):
    stiffness, weights, basis, lam = gll_tables()
    stiffness = np.asarray(stiffness, np.float32).astype(np.float64)
    weights = np.asarray(weights, np.float32).astype(np.float64)
    basis = np.asarray(basis, np.float32).astype(np.float64)
    lam = np.asarray(lam, np.float32).astype(np.float64)
    points = 7 * elements
    z_pad = round_up(points, 128)
    s_pad = round_up(10 * elements, 128)
    every = list(range(8))
    pick_a, place_a = stack_map(
        {-1: [6, 7], 0: every, 1: [0, 1]}, {-1: [0, 1], 0: list(range(1, 9)), 1: [8, 9]}, 8, 10
    )
    pick_s, place_s = stack_map(
        {-1: [8, 9], 0: list(range(1, 9)), 1: [0, 1]}, {-1: [0, 1], 0: every, 1: [6, 7]}, 10, 8
    )
    basis_two = np.kron(basis, basis)
    spectral_in = np.zeros((SPEC, STACK))
    spectral_in[:100] = basis_two.T @ place_a
    spectral_out = np.zeros((STACK, SPEC))
    spectral_out[:, :100] = pick_s @ basis_two
    plane = np.kron(stiffness, np.diag(weights)) + np.kron(np.diag(weights), stiffness)
    plane_weight = np.kron(weights, weights)
    window = np.zeros((z_pad, s_pad))
    own_cols = np.zeros((z_pad, z_pad))
    before_cols = np.zeros((z_pad, z_pad))
    spread = np.zeros((elements, s_pad + 2 * z_pad))
    lines = np.zeros((8, max(z_pad, s_pad)))
    lines[2, 10 * elements :] = 1.0
    for elem in range(elements):
        prior = (elem - 1) % elements
        for col in range(10):
            spread[elem, col * elements + elem] = 1.0
            for row in range(10):
                window[(7 * elem - 1 + row) % points, col * elements + elem] += basis[row, col]
        for step in range(7):
            spread[elem, s_pad + 7 * elem + step] = 1.0
            spread[prior, s_pad + z_pad + 7 * elem + step] = 1.0
            lines[0, 7 * elem + step] = weights[step]
            for row in range(8):
                own_cols[(7 * elem + row) % points, 7 * elem + step] += stiffness[row, step]
        lines[1, 7 * elem] = weights[7]
        for row in range(8):
            before_cols[(7 * prior + row) % points, 7 * elem] += stiffness[row, 7]
    lam_all = np.zeros((SPEC, s_pad))
    lam_two = (lam[:, None] + lam[None, :]).reshape(-1)
    lam_all[:100, : 10 * elements] = lam_two[:, None] + np.repeat(lam, elements)[None, :]
    segments = np.zeros((coarse_count, z_pad))
    for row in range(coarse_count):
        length = points // coarse_count
        segments[row, row * length : (row + 1) * length] = 1.0
    inner = place_a.reshape(10, 10, STACK)[1:9, 1:9].reshape(OWN, STACK)
    inner = np.concatenate([inner[:, start : start + 8] for start, _ in LAST] + [np.zeros((OWN, 8))], axis=1)
    window_high, window_low = halves(window)
    back_high, back_low = halves(window.T)
    single = lambda value: np.asarray(value, np.float32)
    return {
        "pick_a": left_whole(pick_a),
        "spec_in": left_split(spectral_in[:, OWN:]),
        "spec_own": left_split(spectral_in[:, :OWN]),
        "spec_out": left_split(spectral_out),
        "pick_place": left_whole((pick_a @ place_s)[:, OWN:]),
        "pick_own": left_whole((pick_a @ place_s)[:, :OWN]),
        "plane": left_split(pick_a @ plane),
        "inner": left_whole(inner),
        "win_h": window_high,
        "win_l": window_low,
        "back_h": back_high,
        "back_l": back_low,
        "own_cols": single(own_cols),
        "before_cols": single(before_cols),
        "lam_all": single(lam_all),
        "spread": single(spread),
        "lines": single(lines),
        "segments": single(segments),
        "plane_weight": single((pick_a @ plane_weight)[:, None]),
    }


def split_two(value):
    high = value.astype(jnp.bfloat16)
    return high, (value - high.astype(jnp.float32)).astype(jnp.bfloat16)


def mul(left, right):
    return jnp.dot(left, right, preferred_element_type=jnp.float32)


def left_mul(matrix, value):
    high, low = split_two(value)
    return mul(matrix[...], jnp.concatenate([high, high, low], axis=0))


def left_place(matrix, value):
    return mul(matrix[...], jnp.concatenate(split_two(value), axis=0))


def right_mul(value, high_ref, low_ref):
    high, low = split_two(value)
    both = mul(jnp.concatenate([high, low], axis=0), high_ref[...])
    rows = value.shape[0]
    return both[:rows] + (mul(high, low_ref[...]) + both[rows:])


def each_other(count, act):
    if count <= 8:
        for step in range(1, count):
            act(step)
    else:

        def body(step, carry):
            act(step)
            return carry

        lax.fori_loop(1, count, body, 0)


def stage_size(stage, n_gx, n_gy):
    return {"x": n_gx, "y": n_gy, "xy": n_gx * n_gy}[stage]


def last_stages(n_gx, n_gy):
    return ("xy",) if n_gx * n_gy <= DIRECT else STAGES


def kernel(n_gx, n_gy, n_in, *refs):
    sources = refs[:n_in]
    out = refs[n_in]
    loaded = refs[n_in + 1 : 2 * n_in + 1]
    load_sem, arrived, sending, own_rows, z_high, z_low, scale, first, field_w, halo_send, halo_recv = refs[
        2 * n_in + 1 : 2 * n_in + 12
    ]
    lanes = refs[2 * n_in + 12 :]
    (
        rhs, pick_a, segments, factor,
        stiff, mass, spread, lines, lam_all, spec_own, spec_in, win_h, win_l, back_h, back_l, spec_out,
        own_cols, before_cols, pick_own, pick_place, plane, plane_weight, inner,
    ) = loaded
    loads = [
        pltpu.make_async_copy(source, target, load_sem.at[index])
        for index, (source, target) in enumerate(zip(sources, loaded))
    ]
    for load in loads[:4]:
        load.start()

    me_x, me_y = lax.axis_index("gx"), lax.axis_index("gy")
    points = rhs.shape[2]
    z_pad, s_pad = win_h.shape

    def beside(off_x, off_y):
        return (lax.rem(me_x + off_x + n_gx, n_gx), lax.rem(me_y + off_y + n_gy, n_gy))

    def each_offset(stage, act):
        if stage == "xy":
            for off_x in range(n_gx):
                for off_y in range(n_gy):
                    if off_x or off_y:
                        act(off_x, off_y)
        elif stage == "x":
            each_other(n_gx, lambda step: act(step, 0))
        else:
            each_other(n_gy, lambda step: act(0, step))

    barrier = pltpu.get_barrier_semaphore()

    def greet(off_x, off_y):
        pl.semaphore_signal(barrier, inc=1, device_id=beside(off_x, off_y), device_id_type=MESH)

    greeted = 0
    for stage in last_stages(n_gx, n_gy):
        each_offset(stage, greet)
        greeted += stage_size(stage, n_gx, n_gy) - 1
    if last_stages(n_gx, n_gy) == STAGES:
        for off_x, off_y, _, _ in SLOTS[4:]:
            greet(off_x, off_y)
            greeted += 1

    def halo_copy(turn, slot, start, rows):
        off_x, off_y, _, _ = SLOTS[slot]
        return pltpu.make_async_remote_copy(
            src_ref=sending.at[turn, pl.ds(start, rows)],
            dst_ref=arrived.at[turn, pl.ds(start, rows)],
            send_sem=halo_send.at[turn, slot],
            recv_sem=halo_recv.at[turn, slot],
            device_id=beside(-off_x, -off_y),
            device_id_type=MESH,
        )

    def halo_copies(turn):
        if turn == ROUNDS - 1:
            return [halo_copy(turn, slot, *LAST_PACKED[slot]) for _, slot in LAST]
        return [halo_copy(turn, slot, *PACKED[slot]) for slot in (4, 5, 6, 7, 0, 1, 2, 3)]

    tile_row = lax.broadcasted_iota(jnp.int32, (8, 128), 0)
    tile_lane = lax.broadcasted_iota(jnp.int32, (8, 128), 1)

    def halo_start(turn, rows):
        for slot, (_, _, start, count) in enumerate(SLOTS):
            at = PACKED[slot][0]
            if turn == ROUNDS - 1 and slot not in LAST_PACKED:
                continue
            if count == 8:
                part = rows[start : start + 8]
                sending[turn, pl.ds(at, 8)] = jnp.where(tile_row < 4, part[:, :128], part[:, 128:])
            else:
                sending[turn, pl.ds(at, 16)] = rows[start : start + 16, :128]
                sending[turn, pl.ds(at + 16, 8)] = rows[start : start + 8, 128:] + pltpu.roll(
                    rows[start + 8 : start + 16, 128:], 64, 1
                )
        for copy in halo_copies(turn):
            copy.start()
        own_rows[turn] = rows[:OWN]

    def left_half(tile):
        return jnp.where(tile_lane < 64, tile, 0.0)

    def corner_rows(turn, slot):
        tile = arrived[turn, pl.ds(PACKED[slot][0], 8)]
        upper = jnp.where(tile_row < 4, tile, 0.0)
        return jnp.concatenate([upper, jnp.where(tile_row < 4, 0.0, tile)], axis=1)

    def first_rows(turn, slot):
        at = PACKED[slot][0]
        tail = arrived[turn, pl.ds(at + 16, 8)]
        return jnp.concatenate([arrived[turn, pl.ds(at, 8)], left_half(tail)], axis=1)

    def second_rows(turn, slot):
        at = PACKED[slot][0]
        tail = pltpu.roll(arrived[turn, pl.ds(at + 16, 8)], 64, 1)
        return jnp.concatenate([arrived[turn, pl.ds(at + 8, 8)], left_half(tail)], axis=1)

    def halo_wait(turn):
        for copy in halo_copies(turn):
            copy.wait_recv()

    def stack(turn):
        parts = []
        for slot in range(4):
            parts += [first_rows(turn, slot), second_rows(turn, slot)]
        parts += [corner_rows(turn, slot) for slot in range(4, 8)]
        return jnp.concatenate(parts, axis=0)

    def halo_drain(turn):
        for copy in halo_copies(turn):
            copy.wait_send()

    def slot_of(stage, off_x, off_y):
        at_x, at_y = beside(off_x, off_y)
        return {"x": at_x, "y": at_y, "xy": at_x * n_gy + at_y}[stage]

    class Lane:
        def __init__(self, stages, buffers):
            self.legs = [(stage,) + tuple(buffers[3 * at : 3 * at + 3]) for at, stage in enumerate(stages)]

        def copy(self, leg, off_x, off_y, slot):
            stage, buf, send, recv = leg
            index = off_x * n_gy + off_y if stage == "xy" else off_x + off_y
            return pltpu.make_async_remote_copy(
                src_ref=buf.at[slot],
                dst_ref=buf.at[slot],
                send_sem=send.at[index],
                recv_sem=recv.at[index],
                device_id=beside(off_x, off_y),
                device_id_type=MESH,
            )

        def put(self, leg, value):
            mine = slot_of(leg[0], 0, 0)
            leg[1][mine] = value
            each_offset(leg[0], lambda x, y: self.copy(leg, x, y, mine).start())

        def take(self, leg):
            each_offset(leg[0], lambda x, y: self.copy(leg, x, y, slot_of(leg[0], -x, -y)).wait_recv())
            return jnp.sum(leg[1][...], axis=0)

        def start(self, value):
            self.put(self.legs[0], value)

        def middle(self):
            for before, after in zip(self.legs, self.legs[1:]):
                self.put(after, self.take(before))

        def finish(self):
            return self.take(self.legs[-1])

        def drain(self):
            for leg in self.legs:
                mine = slot_of(leg[0], 0, 0)
                each_offset(leg[0], lambda x, y: self.copy(leg, x, y, mine).wait_send())

    coarse = [Lane(STAGES, lanes[:6]), Lane(STAGES, lanes[6:12])]
    sums = Lane(last_stages(n_gx, n_gy), lanes[12:])

    point = lax.broadcasted_iota(jnp.int32, (OWN, z_pad), 0)
    at_x, at_y = point // 8, point % 8
    coarse_mask = (at_x >= 1) & (at_x <= 6) & (at_y >= 1) & (at_y <= 6)

    def coarse_start(turn, rows):
        line = jnp.sum(jnp.where(coarse_mask, rows, 0.0), axis=0, keepdims=True)
        held = jnp.sum(segments[...] * line, axis=1, keepdims=True)
        coarse[turn].start(jnp.sum(factor[...] * held, axis=0, keepdims=True))

    def coarse_finish(turn):
        total = coarse[turn].finish()
        values = jnp.sum(factor[...] * total, axis=1, keepdims=True)
        line = jnp.sum(segments[...] * values, axis=0, keepdims=True)
        return jnp.where(coarse_mask, line, 0.0)

    first[...] = jnp.zeros_like(first)
    for load in loads[:4]:
        load.wait()
    for row in range(7):
        first[pl.ds(8 * row, 7), pl.ds(0, points)] = rhs[row]
    right = first[...]
    rows = left_place(pick_a, right)
    pl.semaphore_wait(barrier, greeted)
    halo_start(0, rows)
    coarse_start(0, right)

    for load in loads[4:]:
        load.start()
    for load in loads[4:16]:
        load.wait()

    def spread_out(coef, start, size):
        return jnp.dot(
            jnp.broadcast_to(coef[0], (8, coef.shape[2])), spread[:, start : start + size],
            precision=exact_mode, preferred_element_type=jnp.float32,
        )[0:1]

    stiff_s, mass_s = spread_out(stiff, 0, s_pad), spread_out(mass, 0, s_pad)
    scale[...] = 1.0 / (stiff_s * lam_all[...] + (mass_s + lines[2:3, :s_pad]))

    def prepare_elements():
        for load in loads[16:]:
            load.wait()
        stiff_own, stiff_before = spread_out(stiff, s_pad, z_pad), spread_out(stiff, s_pad + z_pad, z_pad)
        mass_own, mass_before = spread_out(mass, s_pad, z_pad), spread_out(mass, s_pad + z_pad, z_pad)
        weight_own, weight_before = lines[0:1, :z_pad], lines[1:2, :z_pad]
        line_mass = mass_own * weight_own + mass_before * weight_before
        diagonal = lax.broadcasted_iota(jnp.int32, (z_pad, z_pad), 0) == lax.broadcasted_iota(
            jnp.int32, (z_pad, z_pad), 1
        )
        along = own_cols[...] * stiff_own + before_cols[...] * stiff_before
        z_high[...], z_low[...] = split_two(along + jnp.where(diagonal, line_mass, 0.0))
        return stiff_own * weight_own + stiff_before * weight_before

    def element(turn):
        held = left_place(pick_own, own_rows[turn])
        halo_wait(turn)
        wide = held + left_place(pick_place, stack(turn))
        field = wide[:OWN]
        result = left_mul(plane, field * line_stiff) + plane_weight[...] * right_mul(
            wide, z_high, z_low
        )
        return field, result

    def precondition(turn):
        held = left_mul(spec_own, own_rows[2 * turn])
        halo_wait(2 * turn)
        spectral = right_mul(held + left_mul(spec_in, stack(2 * turn)), win_h, win_l) * scale[...]
        coarse[turn].middle()
        result = left_mul(spec_out, right_mul(spectral, back_h, back_l))
        halo_start(2 * turn + 1, result)
        plate = coarse_finish(turn)
        own_rows[2 * turn + 1] = result[:OWN] + plate
        halo_drain(2 * turn)
        coarse[turn].drain()

    def dot_line(left, other):
        return jnp.sum(left * other, axis=0, keepdims=True)

    def gathered(turn, own):
        parts = [second_rows(turn, 0), second_rows(turn, 2), corner_rows(turn, 4)]
        return own + left_place(inner, jnp.concatenate(parts + [jnp.zeros_like(parts[0])], axis=0))

    owned = (at_x < 7) & (at_y < 7)

    precondition(0)
    line_stiff = prepare_elements()
    z_field, w_rows = element(1)
    halo_start(2, w_rows)
    w_local = w_rows[:OWN]
    coarse_start(1, w_local)
    precondition(1)
    field_w[...] = gathered(2, w_local)
    v_field, av_rows = element(3)
    av_local = av_rows[:OWN]
    partial = jnp.concatenate(
        [
            dot_line(right, jnp.where(owned, z_field, 0.0)),
            dot_line(z_field, w_local),
            dot_line(right, jnp.where(owned, v_field, 0.0)),
            dot_line(v_field, w_local),
            dot_line(v_field, av_local),
            dot_line(z_field, av_local),
            jnp.zeros((2, z_pad), jnp.float32),
        ],
        axis=0,
    )
    at_row = lax.broadcasted_iota(jnp.int32, (8, 128), 0)
    at_lane = lax.broadcasted_iota(jnp.int32, (8, 128), 1)
    packed = jnp.where(at_row == at_lane, jnp.sum(partial, axis=1, keepdims=True), 0.0)
    sums.start(jnp.sum(packed, axis=0, keepdims=True))
    halo_start(4, av_rows)
    sums.middle()
    for turn in (1, 3, 4):
        halo_drain(turn)
    sums.drain()
    halo_wait(4)
    av_field = gathered(4, av_local)
    w_field = field_w[...]
    totals = sums.finish()
    rz, zw, rv, vw, vav, zav = [
        jnp.broadcast_to(totals[:, lane : lane + 1], (1, z_pad)) for lane in range(6)
    ]
    step_0 = rz / zw
    rho_1 = rz - step_0 * (rv + zw) + step_0 * step_0 * vw
    momentum = rho_1 / rz
    curve = (
        zw - step_0 * (vw + zav) + step_0 * step_0 * vav
        + momentum * ((zw - step_0 * vw) + (zw - step_0 * zav))
        + momentum * momentum * zw
    )
    step_1 = rho_1 / curve
    next_dir = (z_field - step_0 * v_field) + momentum * z_field
    next_image = (w_field - step_0 * av_field) + momentum * w_field
    final_x = step_0 * z_field + step_1 * next_dir
    final_r = (right - step_0 * w_field) - step_1 * next_image
    out[0] = final_x
    out[1] = final_r


def move(both, to_x, to_r):
    points = to_x.shape[2]
    for row in range(7):
        to_x[row] = both[0, pl.ds(8 * row, 7), pl.ds(0, points)]
        to_r[row] = both[1, pl.ds(8 * row, 7), pl.ds(0, points)]


def local(n_gx, n_gy, right_side, stiff_coef, mass_coef, coarse_factor):
    elements = stiff_coef.shape[2]
    coarse_count, coarse_all = coarse_factor.shape
    tables = {name: jnp.asarray(table) for name, table in constants(elements, coarse_count).items()}
    tables.update(rhs=right_side, stiff=stiff_coef, mass=mass_coef, factor=coarse_factor)
    operands = [tables[name] for name in OPERANDS]
    z_pad = round_up(7 * elements, 128)
    s_pad = round_up(10 * elements, 128)
    dma = pltpu.SemaphoreType.DMA
    single = jnp.float32
    whole = pl.BlockSpec(memory_space=pltpu.VMEM)
    shape = jax.ShapeDtypeStruct(right_side.shape, single)
    lanes = []
    last = last_stages(n_gx, n_gy)
    for width, stages in ((coarse_all, STAGES), (coarse_all, STAGES), (128, last)):
        for stage in stages:
            size = stage_size(stage, n_gx, n_gy)
            lanes += [pltpu.VMEM((size, 1, width), single), dma((size,)), dma((size,))]
    result = pl.pallas_call(
        functools.partial(kernel, n_gx, n_gy, len(operands)),
        out_shape=jax.ShapeDtypeStruct((2, OWN, z_pad), single),
        in_specs=[pl.BlockSpec(memory_space=pltpu.HBM)] * len(operands),
        out_specs=whole,
        scratch_shapes=[pltpu.VMEM(operand.shape, operand.dtype) for operand in operands]
        + [
            dma((len(operands),)),
            pltpu.VMEM((ROUNDS, MESSAGE, 128), single),
            pltpu.VMEM((ROUNDS, MESSAGE, 128), single),
            pltpu.VMEM((ROUNDS, OWN, z_pad), single),
            pltpu.VMEM((z_pad, z_pad), jnp.bfloat16),
            pltpu.VMEM((z_pad, z_pad), jnp.bfloat16),
            pltpu.VMEM((SPEC, s_pad), single),
            pltpu.VMEM((OWN, z_pad), single),
            pltpu.VMEM((OWN, z_pad), single),
            dma((ROUNDS, 8)),
            dma((ROUNDS, 8)),
        ]
        + lanes,
        compiler_params=pltpu.CompilerParams(
            collective_id=0, has_side_effects=True, vmem_limit_bytes=60 * 1024 * 1024
        ),
    )(*operands)
    return pl.pallas_call(
        move,
        out_shape=(shape, shape),
        in_specs=[whole],
        out_specs=(whole, whole),
        compiler_params=pltpu.CompilerParams(vmem_limit_bytes=60 * 1024 * 1024),
    )(result)


def solution(mesh):
    placed = (P("gx", "gy", None), P("gx", "gy", None), P("gx", "gy", None), P(("gx", "gy"), None))
    return jax.shard_map(
        functools.partial(local, mesh.shape["gx"], mesh.shape["gy"]),
        mesh=mesh,
        in_specs=placed,
        out_specs=(P("gx", "gy", None), P("gx", "gy", None)),
        check_vma=False,
    )
```
